32 devices in a mesh: clip: 8 (over z, x), row: 4 (over y, core).
Axes of the slice: x: 2, y: 2, z: 4, core: 2. Of those that a mesh axis runs over, the one named last changes fastest.
Arguments:
- latents: float32 [8, 8, 16, 256], P('clip', None, 'row'), may hold values from -6 to 6
- noise: float32 [8, 8, 16, 256], P('clip', None, 'row'), may hold values from -6 to 6
- levels: int32 [8, 8], P('clip'), may hold values from 0 to 999
- clip_ids: int32 [8, 8], P('clip'), may hold values from 0 to 1, as said below
- clip_lens: int32 [8, 2], P('clip'), may hold values from 0 to 8, as said below
- embed_w: float32 [16, 1024], P(None, ('clip', 'row')), may hold values from -1.5 to 1.5
- table_w: float32 [1000, 1024], P(None, ('clip', 'row')), may hold values from -6 to 6
- adaln_w: float32 [1024, 8192], P(('clip', 'row')), may hold values from -0.1875 to 0.1875
- qkv_w: float32 [1024, 3072], P(('clip', 'row')), may hold values from -0.1875 to 0.1875
- proj_w: float32 [1024, 1024], P(('clip', 'row')), may hold values from -0.75 to 0.75
- up_w: float32 [1024, 4096], P(('clip', 'row')), may hold values from -0.1875 to 0.1875
- down_w: float32 [4096, 1024], P(('clip', 'row')), may hold values from -0.09375 to 0.09375
- head_w: float32 [1024, 16], P(('clip', 'row')), may hold values from -0.1875 to 0.1875
- embed_avg: float32 [16, 1024], P(None, ('clip', 'row')), may hold values from -0.00012207031 to 0.00012207031
- table_avg: float32 [1000, 1024], P(None, ('clip', 'row')), may hold values from -0.00012207031 to 0.00012207031
- adaln_avg: float32 [1024, 8192], P(('clip', 'row')), may hold values from -0.00012207031 to 0.00012207031
- qkv_avg: float32 [1024, 3072], P(('clip', 'row')), may hold values from -0.00012207031 to 0.00012207031
- proj_avg: float32 [1024, 1024], P(('clip', 'row')), may hold values from -0.00012207031 to 0.00012207031
- up_avg: float32 [1024, 4096], P(('clip', 'row')), may hold values from -0.00012207031 to 0.00012207031
- down_avg: float32 [4096, 1024], P(('clip', 'row')), may hold values from -0.00012207031 to 0.00012207031
- head_avg: float32 [1024, 16], P(('clip', 'row')), may hold values from -0.0024414062 to 0.0024414062
- embed_sq: float32 [16, 1024], P(None, ('clip', 'row')), may hold values from 5.5234377e-06 to 2.2109374e-05
- table_sq: float32 [1000, 1024], P(None, ('clip', 'row')), may hold values from 1.75e-06 to 6.984375e-06
- adaln_sq: float32 [1024, 8192], P(('clip', 'row')), may hold values from 1.75e-06 to 6.984375e-06
- qkv_sq: float32 [1024, 3072], P(('clip', 'row')), may hold values from 1.75e-06 to 6.984375e-06
- proj_sq: float32 [1024, 1024], P(('clip', 'row')), may hold values from 1.75e-06 to 6.984375e-06
- up_sq: float32 [1024, 4096], P(('clip', 'row')), may hold values from 1.75e-06 to 6.984375e-06
- down_sq: float32 [4096, 1024], P(('clip', 'row')), may hold values from 1.75e-06 to 6.984375e-06
- head_sq: float32 [1024, 16], P(('clip', 'row')), may hold values from 3.4921875e-05 to 0.00013984375
Outputs:
- embed_new: float32 [16, 1024], P(None, ('clip', 'row'))
- table_new: float32 [1000, 1024], P(None, ('clip', 'row'))
- adaln_new: float32 [1024, 8192], P(('clip', 'row'))
- qkv_new: float32 [1024, 3072], P(('clip', 'row'))
- proj_new: float32 [1024, 1024], P(('clip', 'row'))
- up_new: float32 [1024, 4096], P(('clip', 'row'))
- down_new: float32 [4096, 1024], P(('clip', 'row'))
- head_new: float32 [1024, 16], P(('clip', 'row'))
- embed_mom: float32 [2, 16, 1024], P(None, None, ('clip', 'row'))
- table_mom: float32 [2, 1000, 1024], P(None, None, ('clip', 'row'))
- adaln_mom: float32 [2, 1024, 8192], P(None, ('clip', 'row'))
- qkv_mom: float32 [2, 1024, 3072], P(None, ('clip', 'row'))
- proj_mom: float32 [2, 1024, 1024], P(None, ('clip', 'row'))
- up_mom: float32 [2, 1024, 4096], P(None, ('clip', 'row'))
- down_mom: float32 [2, 4096, 1024], P(None, ('clip', 'row'))
- head_mom: float32 [2, 1024, 16], P(None, ('clip', 'row'))
- norms: float32 [8, 2], replicated
- loss: float32 [1], replicated
The draws below stay inside these ranges and needn't reach their ends.
Inputs may be any that keep to these rules, and one draw needn't show every extreme that they name: In each group the frames of a clip slot are consecutive and clip_ids never falls: either every frame has id 0 (one clip of 8 frames) or frame f has id f // 4. Some group is of each kind in every draw. A group of one clip has clip_lens [8, 0, ...]; in the other groups every slot has 1 to 4 true frames, its first frames.
All inputs are finite; a program needn't handle non-finite values.
Results may differ from the reference program's by a relative error of at most 0.015.
The reference program's roundings to bfloat16 on the way count: a program that leaves them out, or rounds other values in their place, can miss the bound.
Values may be sent and summed in bfloat16 or wider, within the bound.
No kernel may reach another device: no remote copies, remote signals or barrier semaphores. Data moves between devices by JAX's collectives and lax.ppermute only.
A program may use at most 256 MiB of HBM per device.

```python
import math
import jax
import jax.numpy as jnp
from jax import lax

D = 1024
HEADS = 16
HD = 64
FF = 4096
PD = 16
GRID = 16
LEVELS = 1000
SHORT = 4
STEP = 7
FRAMES = 8
CLIPS = 2
GROUPS = 8
TOKENS = 16384


def clip_plan(key):
    long_pick = jax.random.randint(jax.random.fold_in(key, 12), (GROUPS,), 0, 4) == 0
    forced = jax.random.randint(jax.random.fold_in(key, 13), (), 0, GROUPS)
    group_idx = jnp.arange(GROUPS, dtype=jnp.int32)
    is_long = (long_pick | (group_idx == forced)) & (group_idx != (forced + 1) % GROUPS)
    frame_idx = jnp.arange(FRAMES, dtype=jnp.int32)
    clip_num = jnp.where(is_long[:, None], 0, (frame_idx // SHORT)[None, :])
    short_len = jax.random.randint(jax.random.fold_in(key, 14), (GROUPS, CLIPS), 1, SHORT + 1)
    long_len = jnp.where(jnp.arange(CLIPS, dtype=jnp.int32)[None, :] == 0, FRAMES, 0)
    clip_len = jnp.where(is_long[:, None], long_len, short_len)
    return (clip_num.astype(jnp.int32), clip_len.astype(jnp.int32))


def draw_clip_ids(key, part):
    return clip_plan(key)[0]


def draw_clip_lens(key, part):
    return clip_plan(key)[1]


def touch_ends(array, own_key, smallest, largest):
    place = [jax.random.randint(jax.random.fold_in(own_key, axis), (), 0, length) for axis, length in enumerate(array.shape)]
    longest = array.shape.index(max(array.shape))
    beside = place[:longest] + [(place[longest] + 1) % array.shape[longest]] + place[longest + 1:]
    return array.at[tuple(place)].set(smallest).at[tuple(beside)].set(largest)


def shard_levels(rng, extent, cuts, smallest, high):
    factor_of, own = 1.0, jax.random.fold_in(rng, 6)
    for dim, shards_of in cuts:
        heights = jnp.exp(jax.random.uniform(jax.random.fold_in(own, dim), (shards_of,), jnp.float32, smallest / len(cuts), high / len(cuts)))
        factor_of = factor_of * jnp.repeat(heights, extent[dim] // shards_of).reshape([-1 if axis == dim else 1 for axis in range(len(extent))])
    return factor_of


def normal_values(own_key, shape, scale, bound, shards=(), held_as=jnp.bfloat16):
    gain = shard_levels(own_key, shape, shards, -0.22, 0.18) if shards else 1.0
    array = jax.random.normal(own_key, shape, jnp.float32) * scale * gain
    return jnp.minimum(jnp.maximum(array, -bound), bound).astype(held_as)


def setup_inputs(seed: int = 0) -> dict:
    key_of = jax.random.split(jax.random.key(seed), 30)
    latents = normal_values(key_of[0], (GROUPS, FRAMES, GRID, GRID * PD), 1.0, 6.0, ((0, 8), (2, 4)), jnp.float32)
    noise = normal_values(key_of[1], (GROUPS, FRAMES, GRID, GRID * PD), 1.0, 6.0, ((0, 8), (2, 4)), jnp.float32)
    levels = touch_ends(jax.random.randint(key_of[2], (GROUPS, FRAMES), 0, LEVELS), jax.random.fold_in(key_of[2], 1), 0, LEVELS - 1).astype(jnp.int32)
    clip_ids = draw_clip_ids(jax.random.fold_in(key_of[29], 71), 0)
    clip_lens = draw_clip_lens(jax.random.fold_in(key_of[29], 71), 0)
    embed_w = normal_values(key_of[5], (PD, D), PD ** -0.5, 1.5, ((1, 32),), jnp.float32)
    table_w = normal_values(key_of[6], (LEVELS, D), 1.0, 6.0, ((1, 32),), jnp.float32)
    adaln_w = normal_values(key_of[7], (D, 8 * D), D ** -0.5, 0.1875, ((0, 32),), jnp.float32)
    qkv_w = normal_values(key_of[8], (D, 3 * D), D ** -0.5, 0.1875, ((0, 32),), jnp.float32)
    proj_w = normal_values(key_of[9], (D, D), (D // 16) ** -0.5, 0.75, ((0, 32),), jnp.float32)
    up_w = normal_values(key_of[10], (D, FF), D ** -0.5, 0.1875, ((0, 32),), jnp.float32)
    down_w = normal_values(key_of[11], (FF, D), FF ** -0.5, 0.09375, ((0, 32),), jnp.float32)
    head_w = normal_values(key_of[12], (D, PD), D ** -0.5, 0.1875, ((0, 32),), jnp.float32)
    embed_avg = normal_values(key_of[13], (PD, D), (0.0011 * TOKENS ** -0.5), 0.00012207031, ((1, 32),), jnp.float32)
    table_avg = normal_values(key_of[14], (LEVELS, D), (0.0011 * TOKENS ** -0.5), 0.00012207031, ((1, 32),), jnp.float32)
    adaln_avg = normal_values(key_of[15], (D, 8 * D), (0.0011 * TOKENS ** -0.5), 0.00012207031, ((0, 32),), jnp.float32)
    qkv_avg = normal_values(key_of[16], (D, 3 * D), (0.0011 * TOKENS ** -0.5), 0.00012207031, ((0, 32),), jnp.float32)
    proj_avg = normal_values(key_of[17], (D, D), (0.0011 * TOKENS ** -0.5), 0.00012207031, ((0, 32),), jnp.float32)
    up_avg = normal_values(key_of[18], (D, FF), (0.0011 * TOKENS ** -0.5), 0.00012207031, ((0, 32),), jnp.float32)
    down_avg = normal_values(key_of[19], (FF, D), (0.0011 * TOKENS ** -0.5), 0.00012207031, ((0, 32),), jnp.float32)
    head_avg = normal_values(key_of[20], (D, PD), (0.022 * TOKENS ** -0.5), 0.0024414062, ((0, 32),), jnp.float32)
    embed_sq = jnp.clip(jnp.exp(math.log(2.2109374185674824e-05) - 1.38700125 * jax.random.uniform(key_of[21], (PD, D), jnp.float32) ** shard_levels(key_of[21], (PD, D), ((1, 32),), -0.2, 0.2)), 5.523437721421942e-06, 2.2109374185674824e-05)
    table_sq = jnp.clip(jnp.exp(math.log(6.984374977037078e-06) - 1.3840597 * jax.random.uniform(key_of[22], (LEVELS, D), jnp.float32) ** shard_levels(key_of[22], (LEVELS, D), ((1, 32),), -0.2, 0.2)), 1.7500000240033842e-06, 6.984374977037078e-06)
    adaln_sq = jnp.clip(jnp.exp(math.log(6.984374977037078e-06) - 1.3840597 * jax.random.uniform(key_of[23], (D, 8 * D), jnp.float32) ** shard_levels(key_of[23], (D, 8 * D), ((0, 32),), -0.2, 0.2)), 1.7500000240033842e-06, 6.984374977037078e-06)
    qkv_sq = jnp.clip(jnp.exp(math.log(6.984374977037078e-06) - 1.3840597 * jax.random.uniform(key_of[24], (D, 3 * D), jnp.float32) ** shard_levels(key_of[24], (D, 3 * D), ((0, 32),), -0.2, 0.2)), 1.7500000240033842e-06, 6.984374977037078e-06)
    proj_sq = jnp.clip(jnp.exp(math.log(6.984374977037078e-06) - 1.3840597 * jax.random.uniform(key_of[25], (D, D), jnp.float32) ** shard_levels(key_of[25], (D, D), ((0, 32),), -0.2, 0.2)), 1.7500000240033842e-06, 6.984374977037078e-06)
    up_sq = jnp.clip(jnp.exp(math.log(6.984374977037078e-06) - 1.3840597 * jax.random.uniform(key_of[26], (D, FF), jnp.float32) ** shard_levels(key_of[26], (D, FF), ((0, 32),), -0.2, 0.2)), 1.7500000240033842e-06, 6.984374977037078e-06)
    down_sq = jnp.clip(jnp.exp(math.log(6.984374977037078e-06) - 1.3840597 * jax.random.uniform(key_of[27], (FF, D), jnp.float32) ** shard_levels(key_of[27], (FF, D), ((0, 32),), -0.2, 0.2)), 1.7500000240033842e-06, 6.984374977037078e-06)
    head_sq = jnp.clip(jnp.exp(math.log(0.00013984375) - 1.3874123 * jax.random.uniform(key_of[28], (D, PD), jnp.float32) ** shard_levels(key_of[28], (D, PD), ((0, 32),), -0.2, 0.2)), 3.492187533993274e-05, 0.00013984375)
    return {"latents": latents, "noise": noise, "levels": levels, "clip_ids": clip_ids, "clip_lens": clip_lens, "embed_w": embed_w, "table_w": table_w, "adaln_w": adaln_w, "qkv_w": qkv_w, "proj_w": proj_w, "up_w": up_w, "down_w": down_w, "head_w": head_w, "embed_avg": embed_avg, "table_avg": table_avg, "adaln_avg": adaln_avg, "qkv_avg": qkv_avg, "proj_avg": proj_avg, "up_avg": up_avg, "down_avg": down_avg, "head_avg": head_avg, "embed_sq": embed_sq, "table_sq": table_sq, "adaln_sq": adaln_sq, "qkv_sq": qkv_sq, "proj_sq": proj_sq, "up_sq": up_sq, "down_sq": down_sq, "head_sq": head_sq}


@jax.custom_vjp
def low(v):
    return lax.optimization_barrier(v.astype(jnp.bfloat16)).astype(jnp.float32)

@jax.custom_vjp
def low_back(v):
    return v

def low_keep(v):
    return (low(v), None)

def low_pass(kept, grad):
    return (grad,)

def back_keep(v):
    return (v, None)

def back_low(kept, grad):
    return (low(grad),)
low.defvjp(low_keep, low_pass)
low_back.defvjp(back_keep, back_low)
precise = lax.Precision.HIGHEST
beta_one = 0.9
beta_two = 0.999
adam_eps = 1e-08
weight_decay = 0.01
learn_rate = 1.0
norm_eps = 1e-06

def matmul(left, right):
    return jnp.dot(left, right, precision=precise, preferred_element_type=jnp.float32)

def layer_norm(values):
    center = values - lax.optimization_barrier(jnp.mean(values, axis=-1, keepdims=True))
    spread = lax.optimization_barrier(jnp.mean(center * center, axis=-1, keepdims=True))
    return center * lax.rsqrt(spread + norm_eps)

def modulate(normed, shift, scale):
    return normed * (1.0 + scale[:, None, :]) + shift[:, None, :]

def gelu_tanh(values):
    return jax.nn.gelu(values, approximate=True)

def frame_layout(clip_row, length_row):
    frame_idx = jnp.arange(FRAMES, dtype=jnp.int32)
    same_clip = clip_row[:, None] == clip_row[None, :]
    starts = lax.optimization_barrier(jnp.min(jnp.where(same_clip, frame_idx[None, :], FRAMES), axis=1))
    frame_pos = frame_idx - starts
    slot_idx = jnp.arange(CLIPS, dtype=jnp.int32)
    length = lax.optimization_barrier(jnp.sum(jnp.where(clip_row[:, None] == slot_idx[None, :], length_row[None, :], 0), axis=1))
    is_true = frame_pos < length
    allowed = same_clip & (frame_idx[None, :] <= frame_idx[:, None]) & is_true[None, :]
    return (frame_pos, is_true, allowed)

def noise_mix(level_row):
    angle = (level_row.astype(jnp.float32) + 0.5) * (math.pi / (2 * LEVELS))
    return (jnp.cos(angle), jnp.sin(angle))

def rotary_angles(along_t, along_r, along_c):
    pieces = []
    for posit_val, width in ((along_t, HD // 4), (along_r, 3 * HD // 8), (along_c, 3 * HD // 8)):
        half_width = width // 2
        frequency = 10000.0 ** (-jnp.arange(half_width, dtype=jnp.float32) / half_width)
        pieces.append(posit_val.astype(jnp.float32)[:, None] * frequency[None, :])
    return jnp.concatenate(pieces, axis=1)

def token_angles(frame_pos, row_pos):
    grid_shape = (FRAMES, row_pos.shape[0], GRID)
    along_t = jnp.broadcast_to(frame_pos[:, None, None], grid_shape).reshape(-1)
    along_r = jnp.broadcast_to(row_pos[:, None][None, :, :], grid_shape).reshape(-1)
    along_c = jnp.broadcast_to(jnp.arange(GRID, dtype=jnp.int32)[None, None, :], grid_shape).reshape(-1)
    return rotary_angles(along_t, along_r, along_c)

def rotate(values, angle):
    cosine = jnp.cos(angle)[:, None, :]
    sine_val = jnp.sin(angle)[:, None, :]
    pieces = []
    offset = 0
    for width in (HD // 4, 3 * HD // 8, 3 * HD // 8):
        half_width = width // 2
        lower_h = values[..., offset:offset + half_width]
        upper_h = values[..., offset + half_width:offset + width]
        angle_lo = offset // 2
        cos_part = cosine[..., angle_lo:angle_lo + half_width]
        sin_part = sine_val[..., angle_lo:angle_lo + half_width]
        pieces.append(lower_h * cos_part - upper_h * sin_part)
        pieces.append(upper_h * cos_part + lower_h * sin_part)
        offset += width
    return jnp.concatenate(pieces, axis=-1)

def group_loss(rounded, clean, fresh, level_row, clip_row, length_row):
    w_embed, w_table, w_adaln, w_qkv, w_proj, w_up, w_down, w_head = rounded
    per_frame = GRID * GRID
    count_tok = FRAMES * per_frame
    frame_pos, is_true, allowed = frame_layout(clip_row, length_row)
    alpha, sigma = noise_mix(level_row)
    clean = clean.reshape(FRAMES, per_frame, PD)
    fresh = fresh.reshape(FRAMES, per_frame, PD)
    noisy = alpha[:, None, None] * clean + sigma[:, None, None] * fresh
    target = alpha[:, None, None] * fresh - sigma[:, None, None] * clean
    hidden0 = low_back(matmul(low(noisy.reshape(count_tok, PD)), w_embed)).reshape(FRAMES, per_frame, D)
    cond = w_table[level_row]
    modul = low_back(matmul(low(jax.nn.silu(cond)), w_adaln))
    shift_a, scale_a, gate_a, shift_m, scale_m, gate_m, shift_f, scale_f = jnp.split(modul, 8, axis=1)
    angle = token_angles(frame_pos, jnp.arange(GRID, dtype=jnp.int32))
    mask = jnp.broadcast_to(allowed[:, None, :, None], (FRAMES, per_frame, FRAMES, per_frame)).reshape(count_tok, count_tok)
    scale = HD ** (-0.5)
    attn_in = low(modulate(layer_norm(hidden0), shift_a, scale_a).reshape(count_tok, D))
    qkv = low_back(matmul(attn_in, w_qkv))
    queries = low(rotate(qkv[:, :D].reshape(count_tok, HEADS, HD), angle))
    keys_all = low(rotate(qkv[:, D:2 * D].reshape(count_tok, HEADS, HD), angle))
    values_all = low(qkv[:, 2 * D:].reshape(count_tok, HEADS, HD))

    def one_head(items):
        scores = low_back(jnp.einsum('qd,kd->qk', items[0], items[1], precision=precise)) * scale
        scores = jnp.where(mask, scores, -1e+30)
        top = lax.optimization_barrier(jnp.max(scores, axis=1, keepdims=True))
        log_sum = top + jnp.log(lax.optimization_barrier(jnp.sum(jnp.exp(scores - top), axis=1, keepdims=True)))
        weights_p = jnp.exp(scores - log_sum)
        return low_back(jnp.einsum('qk,kd->qd', low(weights_p), items[2], precision=precise))
    heads_out = lax.map(jax.checkpoint(one_head), (queries.transpose(1, 0, 2), keys_all.transpose(1, 0, 2), values_all.transpose(1, 0, 2)))
    attn_b = low(heads_out.transpose(1, 0, 2).reshape(count_tok, D))
    proj_out = low_back(matmul(attn_b, w_proj)).reshape(FRAMES, per_frame, D)
    hidden1 = hidden0 + gate_a[:, None, :] * proj_out
    mlp_in = low(modulate(layer_norm(hidden1), shift_m, scale_m).reshape(count_tok, D))
    act_b = low(gelu_tanh(low_back(matmul(mlp_in, w_up))))
    down_out = low_back(matmul(act_b, w_down)).reshape(FRAMES, per_frame, D)
    hidden2 = hidden1 + gate_m[:, None, :] * down_out
    final_in = low(modulate(layer_norm(hidden2), shift_f, scale_f).reshape(count_tok, D))
    pred = low_back(matmul(final_in, w_head))
    token_true = jnp.broadcast_to(is_true[:, None], (FRAMES, per_frame)).reshape(count_tok, 1).astype(jnp.float32)
    error = (pred - target.reshape(count_tok, PD)) * token_true
    return jnp.sum(error * error)

def lamb_direction(weight, gradient, first_m, second_m, fix_one, fix_two):
    first_n = beta_one * first_m + (1.0 - beta_one) * gradient
    second_n = jnp.sqrt(beta_two * second_m * second_m + (1.0 - beta_two) * gradient * gradient)
    update = first_n / fix_one / (second_n / math.sqrt(fix_two) + adam_eps) + weight_decay * weight
    return (first_n, second_n, update)

def reference(latents, noise, levels, clip_ids, clip_lens, embed_w, table_w, adaln_w, qkv_w, proj_w, up_w, down_w, head_w, embed_avg, table_avg, adaln_avg, qkv_avg, proj_avg, up_avg, down_avg, head_avg, embed_sq, table_sq, adaln_sq, qkv_sq, proj_sq, up_sq, down_sq, head_sq):
    masters = (embed_w, table_w, adaln_w, qkv_w, proj_w, up_w, down_w, head_w)
    firsts = (embed_avg, table_avg, adaln_avg, qkv_avg, proj_avg, up_avg, down_avg, head_avg)
    seconds = (embed_sq, table_sq, adaln_sq, qkv_sq, proj_sq, up_sq, down_sq, head_sq)

    def frames_true(items):
        return jnp.sum(frame_layout(items[0], items[1])[1].astype(jnp.float32))
    count = jnp.sum(lax.map(frames_true, (clip_ids, clip_lens))) * (GRID * GRID)

    def total_loss(weights):
        rounded = tuple((low(weight) for weight in weights))

        def one_group(carry, items):
            return (carry + jax.checkpoint(group_loss)(rounded, *items), None)
        total, unused = lax.scan(one_group, jnp.zeros((), jnp.float32), (latents, noise, levels, clip_ids, clip_lens))
        return total / (PD * count)
    loss_val, pullback = jax.vjp(total_loss, masters)
    grads = pullback(jnp.ones((), jnp.float32))[0]
    fix_one = 1.0 - beta_one ** STEP
    fix_two = 1.0 - beta_two ** STEP
    news, moms, norm_rows = ([], [], [])
    for weight, gradient, first_m, second_m in zip(masters, grads, firsts, seconds):
        first_n, second_n, update = lamb_direction(weight, gradient, first_m, second_m, fix_one, fix_two)
        weight_norm = jnp.sqrt(jnp.sum(weight * weight))
        update_norm = jnp.sqrt(jnp.sum(update * update))
        news.append(weight - learn_rate * (weight_norm / update_norm) * update)
        moms.append(jnp.stack([first_n, second_n]))
        norm_rows.append(jnp.stack([weight_norm, update_norm]))
    return (news[0], news[1], news[2], news[3], news[4], news[5], news[6], news[7], moms[0], moms[1], moms[2], moms[3], moms[4], moms[5], moms[6], moms[7], jnp.stack(norm_rows), loss_val.reshape(1))
```

```python
import functools
import math

import jax
import jax.numpy as jnp
from jax import lax
from jax.experimental import pallas as pl
from jax.experimental.pallas import tpu as pltpu
from jax.sharding import PartitionSpec as P

D = 1024
HEADS = 16
HD = 64
FF = 4096
PD = 16
GRID = 16
LEVELS = 1000
STEP = 7
FRAMES = 8
CLIPS = 2
PER_FRAME = GRID * GRID
TOK = FRAMES * PER_FRAME
BOTH = ("clip", "row")
VMEM_BYTES = 56 * 1024 * 1024

precise = lax.Precision.HIGHEST
beta_one = 0.9
beta_two = 0.999
adam_eps = 1e-08
weight_decay = 0.01
learn_rate = 1.0
norm_eps = 1e-06
f32 = jnp.float32
bf16 = jnp.bfloat16


def to_low(values):
    return values.astype(bf16)


def dot_low(formula, left, right):
    return jnp.einsum(formula, left, right, preferred_element_type=f32)


def mm(left, right, left_dim, right_dim):
    return lax.dot_general(
        left, right, (((left_dim,), (right_dim,)), ((), ())), preferred_element_type=f32
    )


def layer_norm(values):
    center = values - jnp.mean(values, axis=-1, keepdims=True)
    spread = jnp.mean(center * center, axis=-1, keepdims=True)
    return center * lax.rsqrt(spread + norm_eps)


def norm_parts(values):
    center = values - jnp.mean(values, axis=-1, keepdims=True)
    spread = jnp.mean(center * center, axis=-1, keepdims=True)
    inverse = lax.rsqrt(spread + norm_eps)
    return center * inverse, inverse


def norm_back(normed, inverse, grad):
    mean_g = jnp.mean(grad, axis=-1, keepdims=True)
    mean_gn = jnp.mean(grad * normed, axis=-1, keepdims=True)
    return inverse * (grad - mean_g - normed * mean_gn)


def modulate(normed, shift, scale):
    return normed * (1.0 + scale[:, None, :]) + shift[:, None, :]


def gelu_tanh(values):
    return jax.nn.gelu(values, approximate=True)


def frame_layout(clip_row, length_row):
    frame_idx = jnp.arange(FRAMES, dtype=jnp.int32)
    same_clip = clip_row[:, None] == clip_row[None, :]
    starts = jnp.min(jnp.where(same_clip, frame_idx[None, :], FRAMES), axis=1)
    frame_pos = frame_idx - starts
    slot_idx = jnp.arange(CLIPS, dtype=jnp.int32)
    length = jnp.sum(
        jnp.where(clip_row[:, None] == slot_idx[None, :], length_row[None, :], 0), axis=1
    )
    is_true = frame_pos < length
    stops = jnp.minimum(frame_idx + 1, starts + length)
    return (frame_pos, is_true, starts, stops)


def noise_mix(level_row):
    angle = (level_row.astype(f32) + 0.5) * (math.pi / (2 * LEVELS))
    return (jnp.cos(angle), jnp.sin(angle))


def group_angles(frame_pos, lanes):
    place = jnp.arange(GRID, dtype=jnp.int32)
    j = jnp.arange(lanes, dtype=jnp.int32) % (HD // 2)
    edges = (0, HD // 8, HD // 8 + 3 * HD // 16, HD // 2)
    tables, masks = [], []
    for k, along in enumerate((frame_pos, place, place)):
        size = edges[k + 1] - edges[k]
        frequency = 10000.0 ** (-(j - edges[k]).astype(f32) / size)
        masks.append((j >= edges[k]) & (j < edges[k + 1]))
        frequency = jnp.where(masks[k], frequency, 0.0)
        tables.append(along.astype(f32)[:, None] * frequency[None, :])
    shape = (FRAMES, GRID, GRID, lanes)
    result = []
    for fn in (jnp.cos, jnp.sin):
        at_f = fn(tables[0])[:, None, None, :]
        at_r = fn(tables[1])[None, :, None, :]
        at_c = fn(tables[2])[None, None, :, :]
        value = jnp.where(masks[0], at_f, jnp.where(masks[1], at_r, at_c))
        result.append(jnp.broadcast_to(value, shape).reshape(TOK, lanes))
    return result


def rotary_order(width):
    order = []
    heads = width // HD
    for half in range(2):
        for head in range(heads):
            offset = 0
            for part in (HD // 4, 3 * HD // 8, 3 * HD // 8):
                start = head * HD + offset + half * (part // 2)
                order.extend(range(start, start + part // 2))
                offset += part
    return order


def rotary_permutation(width):
    order = jnp.array(rotary_order(width), dtype=jnp.int32)
    return (jnp.arange(width, dtype=jnp.int32)[:, None] == order[None, :]).astype(bf16)


def shape_of_mesh():
    clips, rows = lax.axis_size("clip"), lax.axis_size("row")
    ny, nz = rows // 2, 4
    nx = clips // nz
    bits = [count.bit_length() - 1 for count in (rows, rows * nx)]
    return (ny, nx, nz), (1, bits[0], bits[1])


def exchange(values, mask):
    count = lax.axis_size("clip") * lax.axis_size("row")
    return lax.ppermute(values, BOTH, [(i, i ^ mask) for i in range(count)])


def along(number):
    sizes, bits = shape_of_mesh()
    return {m: m << bits[number] for m in range(1, sizes[number])}


def chip_gather(shard, use_y=True, hold=None, hold_x=None):
    z_masks, x_masks = along(2), along(1)
    y_masks = along(0) if use_y else {}
    got = [exchange(shard, mask) for mask in z_masks.values()]
    own = jnp.stack([shard] + got)
    if hold is not None:
        own = tie(own, hold)
    pieces = [(own, 0, 0, 0)]
    at_y = {m: exchange(own, mask) for m, mask in y_masks.items()}
    sent = own if hold_x is None else tie(own, hold_x)
    at_x = {m: exchange(sent, mask) for m, mask in x_masks.items()}
    pieces += [(array, m, 0, 0) for m, array in at_y.items()]
    pieces += [(array, 0, m, 0) for m, array in at_x.items()]
    half = own.shape[0] // 2
    for my in at_y:
        for mx in at_x:
            pieces.append((exchange(at_y[my][:half], x_masks[mx]), my, mx, 0))
            pieces.append((exchange(at_x[mx][half:], y_masks[my]), my, mx, half))
    return pieces


def chip_scatter(groups, use_y=True, direct=False, hold=None):
    z_masks, x_masks = along(2), along(1)
    y_masks = along(0) if use_y else {}
    half = groups[0, 0].shape[0] // 2
    at_y = {m: [[], []] for m in y_masks}
    at_x = {m: [[], []] for m in x_masks}
    slant = []
    for my in y_masks:
        for mx in x_masks:
            piece = groups[my, mx]
            if direct:
                slant.append((piece, y_masks[my] ^ x_masks[mx]))
                continue
            at_y[my][0].append(exchange(piece[:half], x_masks[mx]))
            at_x[mx][1].append(exchange(piece[half:], y_masks[my]))

    def total(piece, terms):
        if not terms:
            return piece
        result = piece.astype(f32)
        for term in terms:
            result = result + term.astype(f32)
        return to_low(result)

    def joined(piece, terms):
        if not (terms[0] or terms[1]):
            return piece
        return jnp.concatenate([total(piece[:half], terms[0]), total(piece[half:], terms[1])])

    sent = [(joined(groups[m, 0], at_y[m]), mask) for m, mask in y_masks.items()]
    sent += [(joined(groups[0, m], at_x[m]), mask) for m, mask in x_masks.items()]
    own = total(groups[0, 0], [exchange(piece, mask) for piece, mask in sent + slant])
    if hold is not None:
        own = tie(own, hold)
    result = own[0].astype(f32)
    for m, mask in z_masks.items():
        result = result + exchange(own[m], mask).astype(f32)
    return result, tuple(piece for piece, mask in sent), own


def tie(values, *others):
    return lax.optimization_barrier((values,) + others)[0]


def row_masks():
    return [1 << bit for bit in range(lax.axis_size("row").bit_length() - 1)]


def row_sum(values):
    for mask in row_masks():
        values = values + exchange(values, mask)
    return values


def row_gather(values):
    place = lax.axis_index("row")
    values = values[None]
    for mask in row_masks():
        other = exchange(values, mask)
        first = place & mask == 0
        values = jnp.concatenate(
            [jnp.where(first, values, other), jnp.where(first, other, values)], axis=0
        )
    return values


def spread(values, axes):
    names = axes if isinstance(axes, tuple) else (axes,)
    count = 1
    for name in names:
        count *= lax.axis_size(name)
    copies = jnp.broadcast_to(values[None], (count,) + values.shape)
    return lax.all_to_all(copies, axes, 0, 0, tiled=True)


def run_kernel(
    kernel, grid, inputs, outputs, scratch=(), scalars=None, after=(), flops=0, moved=2**22, exps=0
):
    count = 0 if scalars is None else 1

    def spec(block, index):
        if index is None:
            zeros = (0,) * len(block)
            return pl.BlockSpec(block, lambda *ids: zeros)
        return pl.BlockSpec(block, lambda *ids: index(*ids[: len(grid)]))

    arrays, in_specs = [], []
    for entry in inputs:
        arrays.append(entry[0])
        if len(entry) == 1:
            in_specs.append(spec(entry[0].shape, None))
        elif len(entry) == 2:
            in_specs.append(pl.BlockSpec(memory_space=entry[1]))
        else:
            in_specs.append(spec(entry[1], entry[2]))
    many, extra = len(arrays), len(after)
    arrays.extend(after)
    in_specs.extend([pl.BlockSpec(memory_space=pl.ANY)] * extra)
    out_specs, out_shape = [], []
    for shape, dtype, *rest in outputs:
        out_shape.append(jax.ShapeDtypeStruct(shape, dtype))
        if not rest:
            out_specs.append(spec(shape, None))
        elif len(rest) == 1:
            out_specs.append(pl.BlockSpec(memory_space=rest[0]))
        else:
            out_specs.append(spec(*rest))

    def wrapped(*refs):
        kernel(*refs[: count + many], *refs[count + many + extra :])

    call = pl.pallas_call(
        wrapped,
        grid_spec=pltpu.PrefetchScalarGridSpec(
            num_scalar_prefetch=count,
            grid=grid,
            in_specs=in_specs,
            out_specs=out_specs,
            scratch_shapes=list(scratch),
        ),
        out_shape=out_shape,
        compiler_params=pltpu.CompilerParams(vmem_limit_bytes=VMEM_BYTES),
        cost_estimate=pl.CostEstimate(flops=flops, bytes_accessed=moved, transcendentals=exps),
    )
    return call(*([] if scalars is None else [scalars]), *arrays)


def frame_rows(columns):
    return (PER_FRAME, columns), lambda f: (f, 0)


def head_mask(width, head, rotary):
    lane = lax.broadcasted_iota(jnp.int32, (1, width), 1)
    if rotary:
        return (lane % (width // 2)) // (HD // 2) == head
    return lane // HD == head


def chip_number(coords, my, mx, mz):
    return ((coords[2] ^ mz) * coords[5] + (coords[1] ^ mx)) * coords[4] + (coords[0] ^ my)


def run_place(coords, pieces, columns, after=()):
    rows = pieces[0][0].shape[1]
    chips = sum(piece[0].shape[0] for piece in pieces)
    edges = [sum(columns[:k]) for k in range(len(columns) + 1)]

    def kernel(coords_ref, *refs):
        sources = refs[: len(pieces)]
        targets = refs[len(pieces) : len(pieces) + len(columns)]
        sems = refs[-1]
        copies = []
        for source, (array, my, mx, first) in zip(sources, pieces):
            for k in range(array.shape[0]):
                chip = chip_number(coords_ref, my, mx, first + k)
                spot = pl.ds(pl.multiple_of(chip * rows, rows), rows)
                for number, target in enumerate(targets):
                    lanes = pl.ds(edges[number], columns[number])
                    copies.append(
                        pltpu.make_async_copy(
                            source.at[k, :, lanes], target.at[spot, :], sems.at[len(copies)]
                        )
                    )
        for copy in copies:
            copy.start()
        for copy in copies:
            copy.wait()

    return run_kernel(
        kernel,
        (1,),
        [(piece[0], pl.ANY) for piece in pieces],
        [((chips * rows, wide), bf16) for wide in columns],
        [pltpu.SemaphoreType.DMA((chips * len(columns),))],
        coords,
        after,
        moved=4 * chips * rows * sum(columns),
    )


def run_qkv(coords, noisy, embed, shift, scale, cosine, sine, pieces, after=()):
    rows, columns = pieces[0][0].shape[1:]
    width = columns // 3
    half = width // 2

    def kernel(coords_ref, noisy_ref, embed_ref, shift_ref, scale_ref, cos_ref, sin_ref, *refs):
        sources = refs[: len(pieces)]
        q_ref, k_ref, v_ref, in_ref, w_ref, sems = refs[len(pieces) :]
        frame = pl.program_id(0)

        def copies():
            made = []
            for source, (array, my, mx, first) in zip(sources, pieces):
                for k in range(array.shape[0]):
                    place = (coords_ref[2] ^ (first + k)) * coords_ref[5] + (coords_ref[1] ^ mx)
                    spot = pl.ds(pl.multiple_of(place * rows, rows), rows)
                    made.append(
                        pltpu.make_async_copy(source.at[k], w_ref.at[spot, :], sems.at[len(made)])
                    )
            return made

        @pl.when(frame == 0)
        def start():
            for copy in copies():
                copy.start()

        hidden = mm(noisy_ref[...], embed_ref[...], 1, 0)
        normed, unused = norm_parts(hidden)
        spot = pl.ds(frame, 1)
        attn_in = to_low(normed * (1.0 + scale_ref[spot, :]) + shift_ref[spot, :])
        in_ref[...] = attn_in

        @pl.when(frame == 0)
        def finish():
            for copy in copies():
                copy.wait()

        out = mm(attn_in, w_ref[...], 1, 0)
        cos, sin = cos_ref[...], sin_ref[...]
        for ref, base, factor in ((q_ref, 0, HD**-0.5), (k_ref, width, 1.0)):
            lower = out[:, base : base + half]
            upper = out[:, base + half : base + width]
            ref[:, :half] = to_low(lower * cos - upper * sin) * factor
            ref[:, half:] = to_low(upper * cos + lower * sin) * factor
        v_ref[...] = to_low(out[:, 2 * width :])

    chips = sum(piece[0].shape[0] for piece in pieces)
    return run_kernel(
        kernel,
        (FRAMES,),
        [
            (noisy, *frame_rows(PD)),
            (embed,),
            (shift,),
            (scale,),
            (cosine, *frame_rows(half)),
            (sine, *frame_rows(half)),
        ]
        + [(piece[0], pl.ANY) for piece in pieces],
        [((TOK, width), bf16, *frame_rows(width))] * 3
        + [((TOK, D), bf16, *frame_rows(D)), ((D, columns), bf16)],
        [pltpu.SemaphoreType.DMA((chips,))],
        coords,
        after,
        flops=2 * TOK * D * columns,
        moved=12 * 2**20,
    )


def attend_kernel(span_ref, q_ref, k_ref, v_ref, o_ref, lse_ref, q_scr, s_scr, m_scr, l_scr, acc_scr):
    frame = pl.program_id(0)
    width = q_ref.shape[1]
    heads = width // HD
    block = PER_FRAME
    start, stop = span_ref[0, frame], span_ref[1, frame]
    query = q_ref[...]
    for head in range(heads):
        q_scr[head * block : (head + 1) * block, :] = jnp.where(
            head_mask(width, head, True), query, jnp.zeros_like(query)
        )
    m_scr[...] = jnp.full_like(m_scr, -1e30)
    l_scr[...] = jnp.zeros_like(l_scr)
    acc_scr[...] = jnp.zeros_like(acc_scr)

    def scores(e, carry):
        keys = k_ref[pl.ds(e * block, block), :]
        for head in range(heads):
            rows = slice(head * block, (head + 1) * block)
            score = mm(q_scr[rows, :], keys, 1, 1)
            s_scr[e, rows, :] = score
            top = jnp.maximum(score[:, :128], score[:, 128:])
            m_scr[rows, :] = jnp.maximum(m_scr[rows, :], top)
        return carry

    lax.fori_loop(start, stop, scores, 0)
    for head in range(heads):
        rows = slice(head * block, (head + 1) * block)
        m_scr[rows, :] = jnp.broadcast_to(
            jnp.max(m_scr[rows, :], axis=1, keepdims=True), (block, 128)
        )

    def combine(e, carry):
        values = v_ref[pl.ds(e * block, block), :]
        for head in range(heads):
            rows = slice(head * block, (head + 1) * block)
            top = m_scr[rows, :]
            left = jnp.exp(s_scr[e, rows, :128] - top)
            right = jnp.exp(s_scr[e, rows, 128:] - top)
            l_scr[rows, :] = l_scr[rows, :] + (left + right)
            weight = jnp.concatenate([to_low(left), to_low(right)], axis=1)
            acc_scr[rows, :] = acc_scr[rows, :] + mm(weight, values, 1, 0)
        return carry

    lax.fori_loop(start, stop, combine, 0)
    result = jnp.zeros((block, width), f32)
    for head in range(heads):
        rows = slice(head * block, (head + 1) * block)
        total = jnp.sum(l_scr[rows, :], axis=1, keepdims=True)
        lse_ref[rows, :] = m_scr[rows, :] + jnp.log(total)
        result = jnp.where(head_mask(width, head, False), acc_scr[rows, :] / total, result)
    o_ref[...] = to_low(result).reshape(o_ref.shape)


def run_attend(span, query, keys, values, rows, after=()):
    width = query.shape[1]
    heads = width // HD
    block = PER_FRAME
    per_frame = block // rows
    return run_kernel(
        attend_kernel,
        (FRAMES,),
        [(query, *frame_rows(width)), (keys,), (values,)],
        [
            ((rows, FRAMES, per_frame, width), bf16, (rows, 1, per_frame, width), lambda f: (0, f, 0, 0)),
            ((FRAMES * heads * block, 128), f32, (heads * block, 128), lambda f: (f, 0)),
        ],
        [
            pltpu.VMEM((heads * block, width), bf16),
            pltpu.VMEM((FRAMES, heads * block, block), f32),
            pltpu.VMEM((heads * block, 128), f32),
            pltpu.VMEM((heads * block, 128), f32),
            pltpu.VMEM((heads * block, width), f32),
        ],
        span,
        after,
        flops=2 * 2 * 36 * block * block * 256 * heads,
        moved=10 * 2**20,
        exps=36 * block * block * heads,
    )


def attend_back_kernel(
    span_ref, q_ref, k_ref, v_ref, o_ref, g_ref, lse_ref, cos_ref, sin_ref, out_ref,
    q_scr, g_scr, d_scr, dq_scr, dk_scr, dv_scr, p_scr, s_scr,
):
    frame = pl.program_id(0)
    width = q_ref.shape[1]
    half = width // 2
    heads = width // HD
    block = PER_FRAME
    start, stop = span_ref[0, frame], span_ref[1, frame]

    @pl.when(frame == 0)
    def clear():
        dk_scr[...] = jnp.zeros_like(dk_scr)
        dv_scr[...] = jnp.zeros_like(dv_scr)

    query = q_ref[...]
    grad = g_ref[...].reshape(block, width)
    product = grad.astype(f32) * o_ref[...].reshape(block, width).astype(f32)
    for head in range(heads):
        rows = slice(head * block, (head + 1) * block)
        q_scr[rows, :] = jnp.where(head_mask(width, head, True), query, jnp.zeros_like(query))
        own = head_mask(width, head, False)
        g_scr[rows, :] = jnp.where(own, grad, jnp.zeros_like(grad))
        inner = jnp.sum(jnp.where(own, product, 0.0), axis=1, keepdims=True)
        d_scr[rows, :] = jnp.broadcast_to(inner, (block, 128))
    dq_scr[...] = jnp.zeros_like(dq_scr)

    def step(e, carry):
        spot = pl.ds(e * block, block)
        keys, values = k_ref[spot, :], v_ref[spot, :]
        for head in range(heads):
            rows = slice(head * block, (head + 1) * block)
            score = mm(q_scr[rows, :], keys, 1, 1)
            grad_w = mm(g_scr[rows, :], values, 1, 1)
            lse, inner = lse_ref[rows, :], d_scr[rows, :]
            for part in range(2):
                lanes = slice(part * 128, (part + 1) * 128)
                weight = jnp.exp(score[:, lanes] - lse)
                p_scr[rows, lanes] = to_low(weight)
                s_scr[rows, lanes] = to_low(weight * (grad_w[:, lanes] - inner))
            dq_scr[rows, :] = dq_scr[rows, :] + mm(s_scr[rows, :], keys, 1, 0)
        dk_scr[spot, :] = dk_scr[spot, :] + mm(s_scr[...], q_scr[...], 0, 0)
        dv_scr[spot, :] = dv_scr[spot, :] + mm(p_scr[...], g_scr[...], 0, 0)
        return carry

    lax.fori_loop(start, stop, step, 0)

    def unrotate(grads, cosine, sine, where, base):
        lower, upper = grads[:, :half], grads[:, half:]
        out_ref[where, base : base + half] = to_low(lower * cosine + upper * sine)
        out_ref[where, base + half : base + width] = to_low(upper * cosine - lower * sine)

    total = jnp.zeros((block, width), f32)
    for head in range(heads):
        rows = slice(head * block, (head + 1) * block)
        total = jnp.where(head_mask(width, head, True), dq_scr[rows, :], total)
    spot = pl.ds(frame * block, block)
    unrotate(total * HD**-0.5, cos_ref[spot, :], sin_ref[spot, :], spot, 0)

    @pl.when(frame == FRAMES - 1)
    def finish():
        def one(e, carry):
            spot = pl.ds(e * block, block)
            unrotate(dk_scr[spot, :], cos_ref[spot, :], sin_ref[spot, :], spot, width)
            out_ref[spot, 2 * width :] = to_low(dv_scr[spot, :])
            return carry

        lax.fori_loop(0, FRAMES, one, 0)


def run_attend_back(span, query, keys, values, out, grad, lse, cosine, sine, after=()):
    block = PER_FRAME
    rows, unused, per_frame, width = out.shape
    heads = width // HD
    parts = (rows, 1, per_frame, width), lambda f: (0, f, 0, 0)
    return run_kernel(
        attend_back_kernel,
        (FRAMES,),
        [
            (query, *frame_rows(width)),
            (keys,),
            (values,),
            (out, *parts),
            (grad, *parts),
            (lse, (heads * block, 128), lambda f: (f, 0)),
            (cosine,),
            (sine,),
        ],
        [((TOK, 3 * width), bf16)],
        [
            pltpu.VMEM((heads * block, width), bf16),
            pltpu.VMEM((heads * block, width), bf16),
            pltpu.VMEM((heads * block, 128), f32),
            pltpu.VMEM((heads * block, width), f32),
            pltpu.VMEM((TOK, width), f32),
            pltpu.VMEM((TOK, width), f32),
            pltpu.VMEM((heads * block, block), bf16),
            pltpu.VMEM((heads * block, block), bf16),
        ],
        span,
        after,
        flops=5 * 2 * 36 * block * block * 256 * heads,
        moved=12 * 2**20,
        exps=36 * block * block * heads,
    )[0]


def run_qkv_back(coords, noisy, embed, scale, attn_in, grad, weight, nx, nz, after=()):
    columns = weight.shape[1]
    rows = D // (nx * nz)

    def kernel(coords_ref, noisy_ref, embed_ref, scale_ref, in_ref, g_ref, w_ref, sum_ref, ge_ref, *refs):
        outs, acc = refs[:nx], refs[nx]
        frame = pl.program_id(0)
        noisy, grad = noisy_ref[...], g_ref[...]
        accumulate(acc, frame, mm(in_ref[...], grad, 0, 0))
        normed, inverse = norm_parts(mm(noisy, embed_ref[...], 1, 0))
        grad_in = mm(grad, w_ref[...], 1, 1)
        spot = pl.ds(frame, 1)
        sum_ref[spot, :D] = jnp.sum(grad_in, axis=0, keepdims=True)
        sum_ref[spot, D:] = jnp.sum(grad_in * normed, axis=0, keepdims=True)
        grad_h = norm_back(normed, inverse, grad_in * (1.0 + scale_ref[spot, :]))
        accumulate(ge_ref, frame, mm(noisy, to_low(grad_h), 0, 0))

        @pl.when(frame == FRAMES - 1)
        def finish():
            for mx in range(nx):
                for mz in range(nz):
                    place = (coords_ref[2] ^ mz) * coords_ref[5] + (coords_ref[1] ^ mx)
                    where = pl.ds(pl.multiple_of(place * rows, rows), rows)
                    outs[mx][mz] = to_low(acc[where, :])

    outs = run_kernel(
        kernel,
        (FRAMES,),
        [
            (noisy, *frame_rows(PD)),
            (embed,),
            (scale,),
            (attn_in, *frame_rows(D)),
            (grad, *frame_rows(columns)),
            (weight,),
        ],
        [((FRAMES, 2 * D), f32), ((PD, D), f32)] + [((nz, rows, columns), bf16)] * nx,
        [pltpu.VMEM((D, columns), f32)],
        coords,
        after,
        flops=4 * TOK * D * columns,
        moved=12 * 2**20,
    )
    return outs[0], outs[1], {(0, mx): out for mx, out in enumerate(outs[2:])}


REST = {
    name: slice(k * D, (k + 1) * D)
    for k, name in enumerate(("gate_a", "shift_m", "scale_m", "gate_m", "shift_f", "scale_f"))
}


def by_frame(ref, name, first, count, per_frame):
    rows = [
        jnp.broadcast_to(ref[pl.ds(first + k, 1), REST[name]], (per_frame, D))
        for k in range(count)
    ]
    return jnp.concatenate(rows, axis=0)


def store_sums(ref, first, number, values, per_frame):
    for k in range(values.shape[0] // per_frame):
        rows = values[k * per_frame : (k + 1) * per_frame]
        lanes = slice(number * D, (number + 1) * D)
        ref[pl.ds(first + k, 1), lanes] = jnp.sum(rows, axis=0, keepdims=True)


def run_proj(coords, attn, noisy, embed, rest, own, other, after=()):
    rows, tokens, width = attn.shape
    per_frame, steps = tokens // FRAMES, 2
    block, count = tokens // steps, FRAMES // steps

    def kernel(coords_ref, a_ref, n_ref, e_ref, rest_ref, own_ref, other_ref, h_ref, p_ref, in_ref):
        first = pl.program_id(0) * count
        mine = coords_ref[3] == 0
        attn_b = jnp.concatenate([a_ref[r] for r in range(rows)], axis=1)
        one, two = mm(attn_b, own_ref[...], 1, 0), mm(attn_b, other_ref[...], 1, 0)
        out = jnp.concatenate([jnp.where(mine, one, two), jnp.where(mine, two, one)], axis=1)
        p_ref[...] = out
        hidden = mm(n_ref[...], e_ref[...], 1, 0)
        hidden = hidden + by_frame(rest_ref, "gate_a", first, count, per_frame) * out
        h_ref[...] = hidden
        normed, unused = norm_parts(hidden)
        scale = by_frame(rest_ref, "scale_m", first, count, per_frame)
        shift = by_frame(rest_ref, "shift_m", first, count, per_frame)
        in_ref[...] = to_low(normed * (1.0 + scale) + shift)

    part = (block, D), lambda i: (i, 0)
    return run_kernel(
        kernel,
        (steps,),
        [
            (attn, (rows, block, width), lambda i: (0, i, 0)),
            (noisy, (block, PD), lambda i: (i, 0)),
            (embed,),
            (rest,),
            (own,),
            (other,),
        ],
        [((tokens, D), f32, *part), ((tokens, D), f32, *part), ((tokens, D), bf16, *part)],
        scalars=coords,
        after=after,
        flops=2 * tokens * D * D,
        moved=10 * 2**20,
    )


GELU_C = math.sqrt(2.0 / math.pi)
GELU_A = 0.044715


def gelu_value(x):
    return 0.5 * x * (1.0 + jnp.tanh(GELU_C * (x + GELU_A * (x * x * x))))


def gelu_slope(x):
    square = x * x
    t = jnp.tanh(GELU_C * x * (1.0 + GELU_A * square))
    return 0.5 * (1.0 + t) + (0.5 * GELU_C) * x * (1.0 - t * t) * (1.0 + 3.0 * GELU_A * square)


CHUNK = 512


def down_rows(weight):
    return weight, (CHUNK, D), lambda j: (j, 0)


def up_columns(weight):
    return weight, (D, CHUNK), lambda j: (0, j)


def run_up(mlp_in, up, after=()):
    tokens, hidden = mlp_in.shape[0], up.shape[1]

    def kernel(in_ref, up_ref, out_ref, act_ref):
        out = mm(in_ref[...], up_ref[...], 1, 0)
        out_ref[...] = out
        act_ref[...] = to_low(gelu_value(out))

    part = (tokens, CHUNK), lambda j: (0, j)
    return run_kernel(
        kernel,
        (hidden // CHUNK,),
        [(mlp_in,), up_columns(up)],
        [((tokens, hidden), f32, *part), ((tokens, hidden), bf16, *part)],
        after=after,
        flops=2 * tokens * D * hidden,
        moved=10 * 2**20,
    )


def run_up_down(mlp_in, up, down, after=()):
    tokens, hidden = mlp_in.shape[0], up.shape[1]
    steps = hidden // CHUNK

    def kernel(in_ref, up_ref, down_ref, out_ref, act_ref, part_ref, acc):
        j = pl.program_id(0)
        out = mm(in_ref[...], up_ref[...], 1, 0)
        out_ref[...] = out
        act = to_low(gelu_value(out))
        act_ref[...] = act
        accumulate(acc, j, mm(act, down_ref[...], 1, 0))

        @pl.when(j == steps - 1)
        def finish():
            part_ref[...] = to_low(acc[...])

    part = (tokens, CHUNK), lambda j: (0, j)
    return run_kernel(
        kernel,
        (steps,),
        [(mlp_in,), up_columns(up), down_rows(down)],
        [
            ((tokens, hidden), f32, *part),
            ((tokens, hidden), bf16, *part),
            ((tokens, D), bf16),
        ],
        [pltpu.VMEM((tokens, D), f32)],
        after=after,
        flops=4 * tokens * D * hidden,
        moved=16 * 2**20,
    )


def accumulate(acc, step, term):
    @pl.when(step == 0)
    def first():
        acc[...] = term

    @pl.when(step > 0)
    def more():
        acc[...] = acc[...] + term


def run_down(act, down, after=()):
    tokens, hidden = act.shape

    def kernel(act_ref, down_ref, out_ref):
        accumulate(out_ref, pl.program_id(0), mm(act_ref[...], down_ref[...], 1, 0))

    return run_kernel(
        kernel,
        (hidden // CHUNK,),
        [(act, (tokens, CHUNK), lambda j: (0, j)), down_rows(down)],
        [((tokens, D), f32)],
        after=after,
        flops=2 * tokens * D * hidden,
        moved=8 * 2**20,
    )[0]


def run_head(flags, hidden1, part, got, rest, head, target, after=()):
    tokens = hidden1.shape[0]
    per_frame = tokens // FRAMES

    def kernel(
        flag_ref, h_ref, p_ref, got_ref, rest_ref, head_ref, t_ref,
        gd_ref, gh_ref, sum_ref, ghead_ref, loss_ref,
    ):
        frame = pl.program_id(0)

        @pl.when(frame == 0)
        def clear():
            ghead_ref[...] = jnp.zeros_like(ghead_ref)

        mod = lambda name: rest_ref[pl.ds(frame, 1), REST[name]]
        down_out = p_ref[...] + got_ref[...].astype(f32)
        hidden = h_ref[...] + mod("gate_m") * down_out
        normed, inverse = norm_parts(hidden)
        scale = 1.0 + mod("scale_f")
        final_in = to_low(normed * scale + mod("shift_f"))
        pred = mm(final_in, head_ref[...], 1, 0)
        error = (pred - t_ref[...]) * flag_ref[frame]
        loss_ref[pl.ds(frame, 1), :] = jnp.broadcast_to(
            jnp.sum(jnp.sum(error * error, axis=1, keepdims=True), axis=0, keepdims=True), (1, 128)
        )
        grad_pred = to_low(2.0 * error / flag_ref[FRAMES])
        ghead_ref[...] = ghead_ref[...] + mm(final_in, grad_pred, 0, 0)
        grad_fin = mm(grad_pred, head_ref[...], 1, 1)
        store_sums(sum_ref, frame, 1, grad_fin, per_frame)
        store_sums(sum_ref, frame, 2, grad_fin * normed, per_frame)
        grad = norm_back(normed, inverse, grad_fin * scale)
        gh_ref[...] = grad
        store_sums(sum_ref, frame, 0, grad * down_out, per_frame)
        gd_ref[...] = to_low(grad * mod("gate_m"))

    part_spec = (per_frame, D), lambda f: (f, 0)
    return run_kernel(
        kernel,
        (FRAMES,),
        [
            (flags, pltpu.SMEM),
            (hidden1, *part_spec),
            (part, *part_spec),
            (got, *part_spec),
            (rest,),
            (head,),
            (target, (per_frame, PD), lambda f: (f, 0)),
        ],
        [
            ((tokens, D), bf16, *part_spec),
            ((tokens, D), f32, *part_spec),
            ((FRAMES, 3 * D), f32),
            ((D, PD), f32),
            ((FRAMES, 128), f32),
        ],
        after=after,
        flops=8 * tokens * D * PD,
        moved=10 * 2**20,
    )


def run_act_back(grad, down, up_out, after=()):
    tokens, hidden = up_out.shape

    def kernel(g_ref, down_ref, up_ref, out_ref):
        grad_act = mm(g_ref[...], down_ref[...], 1, 1)
        out_ref[...] = to_low(grad_act * gelu_slope(up_ref[...]))

    part = (tokens, CHUNK), lambda j: (0, j)
    return run_kernel(
        kernel,
        (hidden // CHUNK,),
        [(grad,), down_rows(down), (up_out, *part)],
        [((tokens, hidden), bf16, *part)],
        after=after,
        flops=2 * tokens * D * hidden,
        moved=10 * 2**20,
    )[0]


def run_act_up_back(grad, down, up_out, up, after=()):
    tokens, hidden = up_out.shape
    steps = hidden // CHUNK

    def kernel(g_ref, down_ref, o_ref, up_ref, out_ref, part_ref, acc):
        j = pl.program_id(0)
        grad_act = mm(g_ref[...], down_ref[...], 1, 1)
        grad_out = to_low(grad_act * gelu_slope(o_ref[...]))
        out_ref[...] = grad_out
        accumulate(acc, j, mm(grad_out, up_ref[...], 1, 1))

        @pl.when(j == steps - 1)
        def finish():
            part_ref[...] = to_low(acc[...])

    part = (tokens, CHUNK), lambda j: (0, j)
    return run_kernel(
        kernel,
        (steps,),
        [(grad,), down_rows(down), (up_out, *part), up_columns(up)],
        [((tokens, hidden), bf16, *part), ((tokens, D), bf16)],
        [pltpu.VMEM((tokens, D), f32)],
        after=after,
        flops=4 * tokens * D * hidden,
        moved=16 * 2**20,
    )


def run_up_back(grad, up, after=()):
    tokens, hidden = grad.shape

    def kernel(g_ref, up_ref, out_ref):
        accumulate(out_ref, pl.program_id(0), mm(g_ref[...], up_ref[...], 1, 1))

    return run_kernel(
        kernel,
        (hidden // CHUNK,),
        [(grad, (tokens, CHUNK), lambda j: (0, j)), up_columns(up)],
        [((tokens, D), f32)],
        after=after,
        flops=2 * tokens * D * hidden,
        moved=8 * 2**20,
    )[0]


def group_list(sizes):
    ny, nx, nz = sizes
    return [(my, mx) for my in range(ny) for mx in range(nx)]


def run_down_dw(coords, sizes, acts, grads, after=()):
    groups, nz = group_list(sizes), sizes[2]
    hidden = acts[0].shape[1]
    rows = hidden // (len(groups) * nz)
    steps = hidden // CHUNK

    def kernel(coords_ref, a_ref, b_ref, ga_ref, gb_ref, *refs):
        outs, acc = refs[: len(groups)], refs[len(groups)]
        j = pl.program_id(0)
        acc[j] = mm(a_ref[...], ga_ref[...], 0, 0) + mm(b_ref[...], gb_ref[...], 0, 0)

        @pl.when(j == steps - 1)
        def finish():
            for out, (my, mx) in zip(outs, groups):
                for mz in range(nz):
                    first = chip_number(coords_ref, my, mx, mz) * rows
                    spot = pl.ds(pl.multiple_of(first % CHUNK, rows), rows)
                    out[mz] = to_low(acc[first // CHUNK, spot, :])

    part = (acts[0].shape[0], CHUNK), lambda j: (0, j)
    outs = run_kernel(
        kernel,
        (steps,),
        [(acts[0], *part), (acts[1], *part), (grads[0],), (grads[1],)],
        [((nz, rows, D), bf16)] * len(groups),
        [pltpu.VMEM((steps, CHUNK, D), f32)],
        coords,
        after,
        flops=4 * acts[0].shape[0] * D * hidden,
        moved=10 * 2**20,
    )
    return dict(zip(groups, outs))


def run_up_dw(coords, sizes, ins, grads, proj, after=()):
    groups, nz = group_list(sizes), sizes[2]
    hidden = grads[0].shape[1]
    rows = D // (len(groups) * nz)
    steps = hidden // CHUNK

    def kernel(coords_ref, a_ref, b_ref, ga_ref, gb_ref, proj_ref, *refs):
        outs, acc = refs[: len(groups)], refs[len(groups)]
        j = pl.program_id(0)

        @pl.when(j < steps)
        def up_part():
            acc[...] = mm(a_ref[...], ga_ref[...], 0, 0) + mm(b_ref[...], gb_ref[...], 0, 0)

        @pl.when(j == steps)
        def proj_part():
            acc[...] = proj_ref[...].astype(f32)

        for out, (my, mx) in zip(outs, groups):
            for mz in range(nz):
                first = chip_number(coords_ref, my, mx, mz) * rows
                out[mz] = to_low(acc[pl.ds(pl.multiple_of(first, rows), rows), :])

    part = (grads[0].shape[0], CHUNK), lambda j: (0, jnp.minimum(j, steps - 1))
    outs = run_kernel(
        kernel,
        (steps + 1,),
        [(ins[0],), (ins[1],), (grads[0], *part), (grads[1], *part), (proj,)],
        [((nz, rows, hidden + CHUNK), bf16, (nz, rows, CHUNK), lambda j: (0, 0, j))] * len(groups),
        [pltpu.VMEM((D, CHUNK), f32)],
        coords,
        after,
        flops=4 * ins[0].shape[0] * D * hidden,
        moved=14 * 2**20,
    )
    return dict(zip(groups, outs))


def run_proj_back(coords, grad_h2, part, got, hidden1, proj_out, rest, own, other, attn, noisy, after=()):
    rows, tokens, width = attn.shape
    per_frame, steps = tokens // FRAMES, 2
    block, count = tokens // steps, FRAMES // steps

    def kernel(
        coords_ref, g_ref, p_ref, got_ref, h_ref, po_ref, rest_ref, own_ref, other_ref, a_ref, n_ref,
        ga_ref, mine_ref, theirs_ref, sum_ref, ge_ref, acc,
    ):
        step = pl.program_id(0)
        first = step * count
        mine = coords_ref[3] == 0
        grad_mlp = p_ref[...] + got_ref[...].astype(f32)
        normed, inverse = norm_parts(h_ref[...])
        store_sums(sum_ref, first, 1, grad_mlp, per_frame)
        store_sums(sum_ref, first, 2, grad_mlp * normed, per_frame)
        scale = by_frame(rest_ref, "scale_m", first, count, per_frame)
        grad = g_ref[...] + norm_back(normed, inverse, grad_mlp * (1.0 + scale))
        store_sums(sum_ref, first, 0, grad * po_ref[...], per_frame)
        low = to_low(grad * by_frame(rest_ref, "gate_a", first, count, per_frame))
        lower, upper = low[:, : D // 2], low[:, D // 2 :]
        grad_attn = mm(jnp.where(mine, lower, upper), own_ref[...], 1, 1)
        grad_attn = grad_attn + mm(jnp.where(mine, upper, lower), other_ref[...], 1, 1)
        grad_attn = to_low(grad_attn)
        attn_b = jnp.concatenate([a_ref[r] for r in range(rows)], axis=1)
        for r in range(rows):
            ga_ref[r] = grad_attn[:, r * width : (r + 1) * width]
        accumulate(acc, step, mm(attn_b, low, 0, 0))
        accumulate(ge_ref, step, mm(n_ref[...], to_low(grad), 0, 0))

        @pl.when(step == steps - 1)
        def finish():
            lower, upper = to_low(acc[:, : D // 2]), to_low(acc[:, D // 2 :])
            mine_ref[...] = jnp.where(mine, lower, upper)
            theirs_ref[...] = jnp.where(mine, upper, lower)

    piece = (block, D), lambda i: (i, 0)
    wide = (rows, block, width), lambda i: (0, i, 0)
    return run_kernel(
        kernel,
        (steps,),
        [
            (grad_h2, *piece),
            (part, *piece),
            (got, *piece),
            (hidden1, *piece),
            (proj_out, *piece),
            (rest,),
            (own,),
            (other,),
            (attn, *wide),
            (noisy, (block, PD), lambda i: (i, 0)),
        ],
        [
            ((rows, tokens, width), bf16, *wide),
            ((D, D // 2), bf16),
            ((D, D // 2), bf16),
            ((FRAMES, 3 * D), f32),
            ((PD, D), f32),
        ],
        [pltpu.VMEM((D, D), f32)],
        coords,
        after,
        flops=4 * tokens * D * D,
        moved=18 * 2**20,
    )


def run_lamb(entries, slots, fixes, after=()):
    def kernel(*refs):
        many = len(entries)
        ins, outs = refs[: 4 * many], refs[4 * many : 6 * many]
        sums = refs[6 * many]
        lane = lax.broadcasted_iota(jnp.int32, (1, 128), 1)
        row = jnp.zeros((1, 128), f32)
        for k, slot in enumerate(slots):
            weight, grad, first, second = (ref[...] for ref in ins[4 * k : 4 * k + 4])
            mom_ref, update_ref = outs[2 * k : 2 * k + 2]
            first_n, second_n, update = lamb_direction(weight, grad, first, second, *fixes)
            mom_ref[0] = first_n
            mom_ref[1] = second_n
            update_ref[...] = update
            for value, place in ((weight, 2 * slot), (update, 2 * slot + 1)):
                total = jnp.sum(value * value, axis=0, keepdims=True)
                total = jnp.sum(total, axis=1, keepdims=True)
                row = row + jnp.where(lane == place, total, 0.0)
        sums[...] = row

    outputs = []
    for weight, *unused in entries:
        outputs += [((2,) + weight.shape, f32), (weight.shape, f32)]
    moved = 28 * sum(entry[0].size for entry in entries)
    flat = [(array,) for entry in entries for array in entry]
    outs = run_kernel(kernel, (1,), flat, outputs + [((1, 128), f32)], after=after, moved=moved)
    return outs[0:-1:2], outs[1:-1:2], outs[-1]


def run_update(weights, updates, totals):
    def kernel(totals_ref, *refs):
        many = len(weights)
        lane = lax.broadcasted_iota(jnp.int32, (1, 128), 1)
        norms = jnp.sqrt(jnp.sum(totals_ref[...], axis=0, keepdims=True))
        for k in range(many):
            weight_ref, update_ref, out_ref = refs[k], refs[many + k], refs[2 * many + k]
            pick = lambda at: jnp.sum(jnp.where(lane == at, norms, 0.0), axis=1, keepdims=True)
            trust = learn_rate * (pick(2 * k) / pick(2 * k + 1))
            out_ref[...] = weight_ref[...] - trust * update_ref[...]

    return run_kernel(
        kernel,
        (1,),
        [(totals,)] + [(array,) for array in list(weights) + list(updates)],
        [(weight.shape, f32) for weight in weights],
        moved=12 * sum(weight.size for weight in weights),
    )


def lamb_direction(weight, gradient, first_m, second_m, fix_one, fix_two):
    first_n = beta_one * first_m + (1.0 - beta_one) * gradient
    second_n = jnp.sqrt(beta_two * second_m * second_m + (1.0 - beta_two) * gradient * gradient)
    update = first_n / fix_one / (second_n / math.sqrt(fix_two) + adam_eps) + weight_decay * weight
    return (first_n, second_n, update)


def body(
    latents, noise, levels, clip_ids, clip_lens,
    embed_w, table_w, adaln_w, qkv_w, proj_w, up_w, down_w, head_w,
    embed_avg, table_avg, adaln_avg, qkv_avg, proj_avg, up_avg, down_avg, head_avg,
    embed_sq, table_sq, adaln_sq, qkv_sq, proj_sq, up_sq, down_sq, head_sq,
):
    masters = (embed_w, table_w, adaln_w, qkv_w, proj_w, up_w, down_w, head_w)
    firsts = (embed_avg, table_avg, adaln_avg, qkv_avg, proj_avg, up_avg, down_avg, head_avg)
    seconds = (embed_sq, table_sq, adaln_sq, qkv_sq, proj_sq, up_sq, down_sq, head_sq)
    clips, rows = lax.axis_size("clip"), lax.axis_size("row")
    count_dev = clips * rows
    sizes, unused_bits = shape_of_mesh()
    ny, nx, nz = sizes
    clip_index, row_index = lax.axis_index("clip"), lax.axis_index("row")
    core = row_index % 2
    coords = jnp.stack(
        [
            row_index // 2,
            clip_index % nx,
            clip_index // nx,
            core,
            jnp.full_like(core, ny),
            jnp.full_like(core, nx),
        ]
    ).astype(jnp.int32)
    part = D // count_dev
    width = D // rows
    row_local = GRID // rows
    per_frame = row_local * GRID
    count_tok = FRAMES * per_frame
    hidden = FF // 2
    unit = FF // count_dev
    level_row = levels[0]
    frame_pos, is_true, starts, stops = frame_layout(clip_ids[0], clip_lens[0])
    span = jnp.stack([starts, stops]).astype(jnp.int32)

    own_count = jnp.sum(is_true.astype(f32))
    packed = jnp.concatenate(
        [
            level_row.astype(f32),
            jnp.broadcast_to(own_count, (8,)),
            embed_w.reshape(-1),
            head_w.reshape(-1),
        ]
    )
    everyone = spread(packed.reshape(1, -1), BOTH).reshape(count_dev, -1)
    all_levels = everyone[::rows, :FRAMES].astype(jnp.int32).reshape(-1)
    count = jnp.sum(everyone[::rows, FRAMES]) * PER_FRAME
    embed_b = to_low(everyone[:, 16 : 16 + PD * part].reshape(count_dev, PD, part))
    embed_b = embed_b.transpose(1, 0, 2).reshape(PD, D)
    head_b = to_low(everyone[:, 16 + PD * part :]).reshape(D, PD)

    one_hot = (all_levels[:, None] == jnp.arange(LEVELS, dtype=jnp.int32)[None, :]).astype(f32)
    cond = dot_low("fl,ld->fd", to_low(one_hot), to_low(table_w))
    cond_act = to_low(jax.nn.silu(cond))
    adaln_low = to_low(adaln_w)

    def mod_terms(lower, upper):
        wide = (upper - lower) * D // rows
        terms = to_low(dot_low("fd,dm->fm", cond_act, adaln_low[:, lower * D : upper * D]))
        terms = terms.reshape(clips, FRAMES, rows, wide).transpose(0, 2, 1, 3)
        return terms.reshape(count_dev, FRAMES, wide)

    def modulation(terms):
        total = row_gather(jnp.sum(terms.astype(f32), axis=0))
        return total.transpose(1, 0, 2).reshape(FRAMES, -1)

    first_terms = lax.all_to_all(mod_terms(0, 2), BOTH, 0, 0, tiled=True)
    first = modulation(first_terms)
    shift_a, scale_a = first[:, :D], first[:, D:]

    alpha, sigma = noise_mix(level_row)
    clean = latents[0].reshape(FRAMES, per_frame, PD)
    fresh = noise[0].reshape(FRAMES, per_frame, PD)
    noisy = alpha[:, None, None] * clean + sigma[:, None, None] * fresh
    target = (alpha[:, None, None] * fresh - sigma[:, None, None] * clean).reshape(count_tok, PD)
    noisy_own = to_low(noisy).reshape(count_tok, PD)
    perm = rotary_permutation(width)
    qkv_low = to_low(qkv_w).reshape(part, 3, rows, width)
    turned = to_low(dot_low("dgrw,wv->rdgv", qkv_low[:, :2], perm))
    mine = jnp.concatenate([turned, qkv_low[:, 2:].transpose(2, 0, 1, 3)], axis=2)
    mine = mine.reshape(rows, part, 3 * width)
    token_cols = count_tok * PD // part
    tokens = jnp.broadcast_to(noisy_own.reshape(1, part, token_cols), (rows, part, token_cols))
    mine = tie(jnp.concatenate([mine, tokens], axis=2), everyone)
    mine = lax.all_to_all(mine, "row", 0, 0, tiled=True)
    noisy_all = mine[:, :, 3 * width :].reshape(rows, FRAMES, per_frame, PD)
    noisy_all = noisy_all.transpose(1, 0, 2, 3).reshape(TOK, PD)
    qkv_pieces = chip_gather(
        mine[:, :, : 3 * width].reshape(rows * part, 3 * width), False, hold=first_terms
    )

    def halves(weight, blocks):
        parts = weight.reshape(weight.shape[0], -1, 2, weight.shape[1] // (2 * blocks))
        mine = lax.dynamic_index_in_dim(parts, core, 2, keepdims=False)
        theirs = lax.dynamic_index_in_dim(parts, 1 - core, 2, keepdims=False)
        return mine.reshape(weight.shape[0], -1), theirs.reshape(weight.shape[0], -1)

    up_mine, up_theirs = halves(to_low(up_w), count_dev // 2)
    proj_mine, proj_theirs = halves(to_low(proj_w), 1)
    tall_mine = jnp.concatenate([up_mine, proj_mine], axis=1)
    tall_got = exchange(jnp.concatenate([up_theirs, proj_theirs], axis=1), 1)
    is_zero = core == 0
    tall = jnp.concatenate(
        [jnp.where(is_zero, tall_mine, tall_got), jnp.where(is_zero, tall_got, tall_mine)]
    )
    tall_pieces = chip_gather(tall, hold=qkv_pieces[0][0], hold_x=qkv_pieces[1][0])
    down_pieces = chip_gather(tie(to_low(down_w), tall_pieces[0][0]))

    cosine, sine = group_angles(frame_pos, width // 2)
    query, keys, values, attn_in, qkv_b = run_qkv(
        coords, noisy_all, embed_b, shift_a, scale_a, cosine, sine, qkv_pieces,
        after=(tall_pieces[0][0],),
    )
    attn_heads, lse = run_attend(span, query, keys, values, rows)
    rest_terms = lax.all_to_all(tie(mod_terms(2, 8), query), BOTH, 0, 0, tiled=True)
    rest = modulation(rest_terms)

    def swap_row(wide):
        return lax.all_to_all(wide, "row", 0, 0, tiled=True)

    attn = tie(attn_heads, rest_terms, down_pieces[0][0]).reshape(rows, count_tok, width)
    attn = swap_row(attn)
    up_b, proj_own = run_place(coords, tall_pieces, (hidden, D // 2), after=(attn_heads,))
    proj_other = exchange(proj_own, 1)
    hidden1, proj_out, mlp_in = run_proj(
        coords, attn, noisy_own, embed_b, rest, proj_own, proj_other
    )
    mlp_in_other = exchange(mlp_in, 1)
    up_out, act = run_up(mlp_in, up_b)
    down_b = run_place(coords, down_pieces, (D,), after=(act,))[0]
    up_out_other, act_other, part_other = run_up_down(mlp_in_other, up_b, down_b)
    part_got = exchange(part_other, 1)
    part_own = run_down(act, down_b, after=(part_other,))
    flags = jnp.concatenate([is_true.astype(f32), (PD * count).reshape(1)])
    grad_down_out, grad_h2, sums_f, grad_head, losses = run_head(
        flags, hidden1, part_own, part_got, rest, head_b, target
    )
    loss_local = jnp.sum(losses[:, 0])

    grad_down_other = exchange(grad_down_out, 1)
    grad_up = run_act_back(grad_down_out, down_b, up_out)
    down_groups = run_down_dw(
        coords, sizes, (act, act_other), (grad_down_out, grad_down_other), after=(grad_up,)
    )
    scatter_down = lambda hold: chip_scatter(down_groups, hold=hold)
    grad_up_other, mlp_other = run_act_up_back(
        grad_down_other, down_b, up_out_other, up_b, after=(down_groups[0, 0],)
    )
    mlp_got = exchange(mlp_other, 1)
    mlp_own = run_up_back(grad_up, up_b, after=(mlp_other,))
    grad_attn, proj_mine, proj_theirs, sums_m, embed_h1 = run_proj_back(
        coords, grad_h2, mlp_own, mlp_got, hidden1, proj_out, rest,
        proj_own, proj_other, attn, noisy_own,
    )
    grad_attn = swap_row(grad_attn).reshape(rows, FRAMES, per_frame, width)
    proj_term = to_low(proj_mine.astype(f32) + exchange(proj_theirs, 1).astype(f32))
    tall_groups = run_up_dw(
        coords, sizes, (mlp_in, mlp_in_other), (grad_up, grad_up_other), proj_term
    )
    down_sum, down_xy, down_z = scatter_down(tall_groups[0, 0])
    tall_sum, tall_xy, tall_z = chip_scatter(tall_groups, direct=True)
    grad_qkv = run_attend_back(
        span, query, keys, values, attn_heads, grad_attn, lse, cosine, sine,
        after=(tall_groups[0, 0], down_z),
    )
    sums_a, grad_embed, qkv_groups = run_qkv_back(
        coords, noisy_all, embed_b, scale_a, attn_in, grad_qkv, qkv_b, nx, nz,
        after=(tall_z, down_sum),
    )
    qkv_sum, unused_xy, qkv_z = chip_scatter(qkv_groups, False)
    grad_embed = grad_embed + embed_h1

    keep = lax.dynamic_slice_in_dim(tall_sum, core * part, part)
    got = exchange(to_low(lax.dynamic_slice_in_dim(tall_sum, (1 - core) * part, part)), 1)
    got = got.astype(f32)
    pair_sum = jnp.stack([jnp.where(is_zero, keep, got), jnp.where(is_zero, got, keep)], axis=1)
    up_sum = pair_sum[:, :, :hidden].reshape(part, 2, count_dev // 2, unit)
    up_sum = up_sum.transpose(0, 2, 1, 3).reshape(part, FF)
    proj_sum = pair_sum[:, :, hidden:].reshape(part, D)
    qkv_sum = tie(to_low(qkv_sum), tall_sum).reshape(rows, part, 3 * width)
    qkv_sum = swap_row(qkv_sum).reshape(rows, part, 3, width)
    turned = dot_low("rdgv,wv->dgrw", qkv_sum[:, :, :2], perm)
    straight = qkv_sum[:, :, 2:].transpose(1, 2, 0, 3).astype(f32)
    qkv_sum = jnp.concatenate([turned, straight], axis=1).reshape(part, 3 * D)

    def mod_row(values_mod):
        wide = values_mod.shape[1] // rows
        total = to_low(row_sum(values_mod))
        return lax.dynamic_slice_in_dim(total, row_index * wide, wide, axis=1)

    def mod_all(total):
        wide = total.shape[-1]
        total = total.reshape(clips, rows, FRAMES, wide)
        return total.transpose(0, 2, 1, 3).reshape(clips * FRAMES, rows * wide)

    mod_rest = mod_row(jnp.concatenate([sums_m, sums_f], axis=1))
    mod_rest = mod_all(spread(tie(mod_rest, grad_qkv), BOTH))

    small = jnp.concatenate(
        [
            grad_embed.reshape(PD, count_dev, part).transpose(1, 0, 2).reshape(count_dev, -1),
            grad_head.reshape(count_dev, -1),
        ],
        axis=1,
    )
    small = to_low(small).reshape(count_dev, 1, -1)
    mod_first = mod_row(sums_a)
    wide = mod_first.shape[-1]
    lines = small.shape[-1] // wide
    last = jnp.concatenate(
        [
            jnp.broadcast_to(mod_first[None], (count_dev, FRAMES, wide)),
            small.reshape(count_dev, lines, wide),
        ],
        axis=1,
    )
    last = lax.all_to_all(tie(last, qkv_z), BOTH, 0, 0, tiled=True)
    mod_first = mod_all(last[:, :FRAMES])
    small = jnp.sum(last[:, FRAMES:].astype(f32), axis=0).reshape(-1)
    embed_sum = small[: PD * part].reshape(PD, part)
    head_sum = small[PD * part :].reshape(part, PD)
    grad_mod_b = jnp.concatenate([mod_first, mod_rest], axis=1)
    grad_adaln = dot_low("fd,fm->dm", cond_act, grad_mod_b)
    grad_cond_act = dot_low("fm,dm->fd", grad_mod_b, adaln_low)
    unused_silu, silu_pull = jax.vjp(jax.nn.silu, cond)
    grad_cond = silu_pull(grad_cond_act)[0]
    grad_table = jnp.einsum(
        "fl,fd->dl", one_hot, grad_cond, precision=precise, preferred_element_type=f32
    )

    fixes = (1.0 - beta_one**STEP, 1.0 - beta_two**STEP)
    reduced = (
        embed_sum, grad_table, grad_adaln, qkv_sum, proj_sum, up_sum, down_sum, head_sum.T,
    )
    turned = (1, 7)
    flip = lambda k, array: jnp.swapaxes(array, -1, -2) if k in turned else array
    weights = [flip(k, array) for k, array in enumerate(masters)]
    entries = [
        (weights[k], reduced[k], flip(k, firsts[k]), flip(k, seconds[k])) for k in range(8)
    ]
    moms, updates, rows_of_sums = [None] * 8, [None] * 8, []
    for group in ((6,), (4, 5), (3,), (0, 1, 2, 7)):
        got_moms, got_updates, sums = run_lamb([entries[k] for k in group], group, fixes)
        rows_of_sums.append(sums)
        for k, mom, update in zip(group, got_moms, got_updates):
            moms[k], updates[k] = flip(k, mom), update
    lane = jnp.arange(128, dtype=jnp.int32)[None, :]
    sums = sum(rows_of_sums) + jnp.where(lane == 16, loss_local, 0.0)
    totals = spread(sums, BOTH).reshape(count_dev, 128)
    news = run_update(weights, updates, totals)
    news = [flip(k, array) for k, array in enumerate(news)]
    totals = jnp.sum(totals, axis=0)
    norms = jnp.sqrt(totals[:16].reshape(8, 2))
    return (*news, *moms, norms, totals[16:17] / (PD * count))


def solution(mesh):
    wide, tall = P(None, BOTH), P(BOTH, None)
    weights = (wide, wide, tall, tall, tall, tall, tall, tall)
    moments = (P(None, None, BOTH),) * 2 + (P(None, BOTH, None),) * 6
    return jax.shard_map(
        body,
        mesh=mesh,
        in_specs=(
            P("clip", None, "row", None),
            P("clip", None, "row", None),
            P("clip", None),
            P("clip", None),
            P("clip", None),
        )
        + weights * 3,
        out_specs=weights + moments + (P(), P()),
        check_vma=False,
    )
```

```python
import functools
import math

import jax
import jax.numpy as jnp
from jax import lax
from jax.experimental import pallas as pl
from jax.experimental.pallas import tpu as pltpu
from jax.sharding import PartitionSpec as P

D = 1024
HEADS = 16
HD = 64
FF = 4096
PD = 16
GRID = 16
LEVELS = 1000
STEP = 7
FRAMES = 8
CLIPS = 2
PER_FRAME = GRID * GRID
TOK = FRAMES * PER_FRAME
BOTH = ("clip", "row")
VMEM_BYTES = 56 * 1024 * 1024

precise = lax.Precision.HIGHEST
beta_one = 0.9
beta_two = 0.999
adam_eps = 1e-08
weight_decay = 0.01
learn_rate = 1.0
norm_eps = 1e-06
f32 = jnp.float32
bf16 = jnp.bfloat16


def to_low(values):
    return values.astype(bf16)


def dot_low(formula, left, right):
    return jnp.einsum(formula, left, right, preferred_element_type=f32)


def mm(left, right, left_dim, right_dim):
    return lax.dot_general(
        left, right, (((left_dim,), (right_dim,)), ((), ())), preferred_element_type=f32
    )


def layer_norm(values):
    center = values - jnp.mean(values, axis=-1, keepdims=True)
    spread = jnp.mean(center * center, axis=-1, keepdims=True)
    return center * lax.rsqrt(spread + norm_eps)


def norm_parts(values):
    center = values - jnp.mean(values, axis=-1, keepdims=True)
    spread = jnp.mean(center * center, axis=-1, keepdims=True)
    inverse = lax.rsqrt(spread + norm_eps)
    return center * inverse, inverse


def norm_back(normed, inverse, grad):
    mean_g = jnp.mean(grad, axis=-1, keepdims=True)
    mean_gn = jnp.mean(grad * normed, axis=-1, keepdims=True)
    return inverse * (grad - mean_g - normed * mean_gn)


def modulate(normed, shift, scale):
    return normed * (1.0 + scale[:, None, :]) + shift[:, None, :]


def gelu_tanh(values):
    return jax.nn.gelu(values, approximate=True)


def frame_layout(clip_row, length_row):
    frame_idx = jnp.arange(FRAMES, dtype=jnp.int32)
    same_clip = clip_row[:, None] == clip_row[None, :]
    starts = jnp.min(jnp.where(same_clip, frame_idx[None, :], FRAMES), axis=1)
    frame_pos = frame_idx - starts
    slot_idx = jnp.arange(CLIPS, dtype=jnp.int32)
    length = jnp.sum(
        jnp.where(clip_row[:, None] == slot_idx[None, :], length_row[None, :], 0), axis=1
    )
    is_true = frame_pos < length
    stops = jnp.minimum(frame_idx + 1, starts + length)
    return (frame_pos, is_true, starts, stops)


def noise_mix(level_row):
    angle = (level_row.astype(f32) + 0.5) * (math.pi / (2 * LEVELS))
    return (jnp.cos(angle), jnp.sin(angle))


def group_angles(frame_pos, lanes):
    place = jnp.arange(GRID, dtype=jnp.int32)
    j = jnp.arange(lanes, dtype=jnp.int32) % (HD // 2)
    edges = (0, HD // 8, HD // 8 + 3 * HD // 16, HD // 2)
    tables, masks = [], []
    for k, along in enumerate((frame_pos, place, place)):
        size = edges[k + 1] - edges[k]
        frequency = 10000.0 ** (-(j - edges[k]).astype(f32) / size)
        masks.append((j >= edges[k]) & (j < edges[k + 1]))
        frequency = jnp.where(masks[k], frequency, 0.0)
        tables.append(along.astype(f32)[:, None] * frequency[None, :])
    shape = (FRAMES, GRID, GRID, lanes)
    result = []
    for fn in (jnp.cos, jnp.sin):
        at_f = fn(tables[0])[:, None, None, :]
        at_r = fn(tables[1])[None, :, None, :]
        at_c = fn(tables[2])[None, None, :, :]
        value = jnp.where(masks[0], at_f, jnp.where(masks[1], at_r, at_c))
        result.append(jnp.broadcast_to(value, shape).reshape(TOK, lanes))
    return result


def rotary_order(width):
    order = []
    heads = width // HD
    for half in range(2):
        for head in range(heads):
            offset = 0
            for part in (HD // 4, 3 * HD // 8, 3 * HD // 8):
                start = head * HD + offset + half * (part // 2)
                order.extend(range(start, start + part // 2))
                offset += part
    return order


def rotary_permutation(width):
    order = jnp.array(rotary_order(width), dtype=jnp.int32)
    return (jnp.arange(width, dtype=jnp.int32)[:, None] == order[None, :]).astype(bf16)


def shape_of_mesh():
    clips, rows = lax.axis_size("clip"), lax.axis_size("row")
    ny, nz = rows // 2, 4
    nx = clips // nz
    bits = [count.bit_length() - 1 for count in (rows, rows * nx)]
    return (ny, nx, nz), (1, bits[0], bits[1])


def exchange(values, mask):
    count = lax.axis_size("clip") * lax.axis_size("row")
    return lax.ppermute(values, BOTH, [(i, i ^ mask) for i in range(count)])


def along(number):
    sizes, bits = shape_of_mesh()
    return {m: m << bits[number] for m in range(1, sizes[number])}


class Gather:
    def __init__(self, shard, use_y=True):
        self.shard = shard
        self.z_masks, self.x_masks = along(2), along(1)
        self.y_masks = along(0) if use_y else {}

    def go_z(self, *hold):
        came = [exchange(self.shard, mask) for mask in self.z_masks.values()]
        self.own = jnp.stack([self.shard] + came)
        if hold:
            self.own = tie(self.own, *hold)

    def go_direct(self):
        self.go_xy()
        self.slant = [
            (exchange(self.own, y_mask ^ x_mask), my, mx, 0)
            for my, y_mask in self.y_masks.items()
            for mx, x_mask in self.x_masks.items()
        ]

    def go_xy(self, hold_x=()):
        self.at_y = {m: exchange(self.own, mask) for m, mask in self.y_masks.items()}
        sent = tie(self.own, *hold_x) if hold_x else self.own
        self.at_x = {m: exchange(sent, mask) for m, mask in self.x_masks.items()}

    def came_xy(self):
        return tuple(self.at_y.values()) + tuple(self.at_x.values())

    def go_slant(self, *hold):
        at_y, at_x = self.at_y, self.at_x
        if hold:
            at_y = {m: tie(array, *hold) for m, array in at_y.items()}
            at_x = {m: tie(array, *hold) for m, array in at_x.items()}
        half = self.own.shape[0] // 2
        self.slant = []
        for my in at_y:
            for mx in at_x:
                self.slant.append((exchange(at_y[my][:half], self.x_masks[mx]), my, mx, 0))
                self.slant.append((exchange(at_x[mx][half:], self.y_masks[my]), my, mx, half))

    def pieces(self):
        pieces = [(self.own, 0, 0, 0)]
        pieces += [(array, m, 0, 0) for m, array in self.at_y.items()]
        pieces += [(array, 0, m, 0) for m, array in self.at_x.items()]
        return pieces + self.slant


class Scatter:
    def __init__(self, groups, *hold):
        self.groups = groups
        self.z_masks, self.x_masks, self.y_masks = along(2), along(1), along(0)
        half = groups[0, 0].shape[0] // 2
        at_y = {m: [[], []] for m in self.y_masks}
        at_x = {m: [[], []] for m in self.x_masks}
        for my in self.y_masks:
            for mx in self.x_masks:
                piece = groups[my, mx]
                one = exchange(piece[:half], self.x_masks[mx])
                two = exchange(piece[half:], self.y_masks[my])
                if hold:
                    one, two = tie(one, *hold), tie(two, *hold)
                at_y[my][0].append(one)
                at_x[mx][1].append(two)

        def joined(piece, terms):
            if not (terms[0] or terms[1]):
                return piece
            parts = total(piece[:half], terms[0]), total(piece[half:], terms[1])
            return jnp.concatenate(parts)

        self.sent = {(m, 0): joined(groups[m, 0], at_y[m]) for m in self.y_masks}
        self.sent.update({(0, m): joined(groups[0, m], at_x[m]) for m in self.x_masks})

    def go_xy(self, extra=None, *hold):
        masks = {(m, 0): mask for m, mask in self.y_masks.items()}
        masks.update({(0, m): mask for m, mask in self.x_masks.items()})
        sent, self.extra, slant = dict(self.sent), extra, []
        if extra is not None:
            sent = {g: jnp.concatenate([piece, extra[g]], axis=2) for g, piece in sent.items()}
            slant = [(extra[my, mx], self.y_masks[my] ^ self.x_masks[mx])
                     for my in self.y_masks for mx in self.x_masks]
        if hold:
            sent = {g: tie(piece, *hold) for g, piece in sent.items()}
        self.came = [exchange(piece, masks[g]) for g, piece in sent.items()]
        self.came_slant = [exchange(piece, mask) for piece, mask in slant]

    def go_z(self, *hold):
        came = list(self.came)
        if hold:
            came = [tie(array, *hold) for array in came]
        width = self.groups[0, 0].shape[2]
        self.own = total(self.groups[0, 0], [array[:, :, :width] for array in came])
        if self.extra is not None:
            terms = [array[:, :, width:] for array in came] + self.came_slant
            self.own = jnp.concatenate([self.own, total(self.extra[0, 0], terms)], axis=2)
        self.came_z = [exchange(self.own[m], mask) for m, mask in self.z_masks.items()]

    def result(self, *hold):
        came = list(self.came_z)
        if hold:
            came = [tie(array, *hold) for array in came]
        value = self.own[0].astype(f32)
        for array in came:
            value = value + array.astype(f32)
        return value


def total(piece, terms):
    if not terms:
        return piece
    value = piece.astype(f32)
    for term in terms:
        value = value + term.astype(f32)
    return to_low(value)


def tie(values, *others):
    return lax.optimization_barrier((values,) + others)[0]


def row_masks():
    return [1 << bit for bit in range(lax.axis_size("row").bit_length() - 1)]


def row_sum(values, *hold):
    for mask in row_masks():
        values = values + exchange(to_low(values), mask).astype(f32)
    return tie(values, *hold) if hold else values


def row_gather(values):
    place = lax.axis_index("row")
    values = values[None]
    for mask in row_masks():
        other = exchange(values, mask)
        first = place & mask == 0
        values = jnp.concatenate(
            [jnp.where(first, values, other), jnp.where(first, other, values)], axis=0
        )
    return values


def row_swap(values):
    place = lax.axis_index("row")
    steps = len(row_masks())
    values = values.reshape((2,) * steps + values.shape[1:])
    for step, mask in enumerate(row_masks()):
        axis = steps - 1 - step
        mine = (place >> step) & 1
        keep = lax.dynamic_index_in_dim(values, mine, axis, keepdims=False)
        got = exchange(lax.dynamic_index_in_dim(values, 1 - mine, axis, keepdims=False), mask)
        low, high = jnp.where(mine == 0, keep, got), jnp.where(mine == 0, got, keep)
        values = jnp.stack([low, high], axis=axis)
    return values.reshape((-1,) + values.shape[steps:])


def spread(values, axes):
    names = axes if isinstance(axes, tuple) else (axes,)
    count = 1
    for name in names:
        count *= lax.axis_size(name)
    copies = jnp.broadcast_to(values[None], (count,) + values.shape)
    return lax.all_to_all(copies, axes, 0, 0, tiled=True)


def run_kernel(
    kernel, grid, inputs, outputs, scratch=(), scalars=None, after=(), flops=0, moved=2**22, exps=0
):
    count = 0 if scalars is None else 1

    def spec(block, index):
        if index is None:
            zeros = (0,) * len(block)
            return pl.BlockSpec(block, lambda *ids: zeros)
        return pl.BlockSpec(block, lambda *ids: index(*ids[: len(grid)]))

    arrays, in_specs = [], []
    for entry in inputs:
        arrays.append(entry[0])
        if len(entry) == 1:
            in_specs.append(spec(entry[0].shape, None))
        elif len(entry) == 2:
            in_specs.append(pl.BlockSpec(memory_space=entry[1]))
        else:
            in_specs.append(spec(entry[1], entry[2]))
    many, extra = len(arrays), len(after)
    arrays.extend(after)
    in_specs.extend([pl.BlockSpec(memory_space=pl.ANY)] * extra)
    out_specs, out_shape = [], []
    for shape, dtype, *rest in outputs:
        out_shape.append(jax.ShapeDtypeStruct(shape, dtype))
        if not rest:
            out_specs.append(spec(shape, None))
        elif len(rest) == 1:
            out_specs.append(pl.BlockSpec(memory_space=rest[0]))
        else:
            out_specs.append(spec(*rest))

    def wrapped(*refs):
        kernel(*refs[: count + many], *refs[count + many + extra :])

    call = pl.pallas_call(
        wrapped,
        grid_spec=pltpu.PrefetchScalarGridSpec(
            num_scalar_prefetch=count,
            grid=grid,
            in_specs=in_specs,
            out_specs=out_specs,
            scratch_shapes=list(scratch),
        ),
        out_shape=out_shape,
        compiler_params=pltpu.CompilerParams(vmem_limit_bytes=VMEM_BYTES),
        cost_estimate=pl.CostEstimate(flops=flops, bytes_accessed=moved, transcendentals=exps),
    )
    return call(*([] if scalars is None else [scalars]), *arrays)


def frame_rows(columns):
    return (PER_FRAME, columns), lambda f: (f, 0)


def frame_lines(ref, first, count, per_frame):
    lines = [
        jnp.broadcast_to(ref[pl.ds(first + k, 1), :], (per_frame, ref.shape[1]))
        for k in range(count)
    ]
    return jnp.concatenate(lines, axis=0)


def head_mask(width, head, rotary):
    lane = lax.broadcasted_iota(jnp.int32, (1, width), 1)
    if rotary:
        return (lane % (width // 2)) // (HD // 2) == head
    return lane // HD == head


def chip_number(coords, my, mx, mz):
    return ((coords[2] ^ mz) * coords[5] + (coords[1] ^ mx)) * coords[4] + (coords[0] ^ my)


def run_place(coords, pieces, columns, after=()):
    rows = pieces[0][0].shape[1]
    chips = sum(piece[0].shape[0] for piece in pieces)
    edges = [sum(columns[:k]) for k in range(len(columns) + 1)]

    def kernel(coords_ref, *refs):
        sources = refs[: len(pieces)]
        targets = refs[len(pieces) : len(pieces) + len(columns)]
        sems = refs[-1]
        copies = []
        for source, (array, my, mx, first) in zip(sources, pieces):
            for k in range(array.shape[0]):
                chip = chip_number(coords_ref, my, mx, first + k)
                spot = pl.ds(pl.multiple_of(chip * rows, rows), rows)
                for number, target in enumerate(targets):
                    lanes = pl.ds(edges[number], columns[number])
                    copies.append(
                        pltpu.make_async_copy(
                            source.at[k, :, lanes], target.at[spot, :], sems.at[len(copies)]
                        )
                    )
        for copy in copies:
            copy.start()
        for copy in copies:
            copy.wait()

    return run_kernel(
        kernel,
        (1,),
        [(piece[0], pl.ANY) for piece in pieces],
        [((chips * rows, wide), bf16) for wide in columns],
        [pltpu.SemaphoreType.DMA((chips * len(columns),))],
        coords,
        after,
        moved=4 * chips * rows * sum(columns),
    )


def run_qkv_attend(coords, span, noisy, embed, shift, scale, cosine, sine, pieces, ranks, after=()):
    rows, columns = pieces[0][0].shape[1:]
    width = columns // 3
    half, heads, per_frame = width // 2, width // HD, PER_FRAME // ranks
    count = 2
    block, steps = count * PER_FRAME, FRAMES // count
    stack = heads * PER_FRAME
    base = coords.shape[0]

    def kernel(number_ref, noisy_ref, embed_ref, shift_ref, scale_ref, cos_ref, sin_ref, *refs):
        sources = refs[: len(pieces)]
        q_ref, k_ref, v_ref, in_ref, w_ref, o_ref, lse_ref, sems, *scratch = refs[len(pieces) :]
        step = pl.program_id(0)

        def copies():
            made = []
            for source, (array, my, mx, first) in zip(sources, pieces):
                for k in range(array.shape[0]):
                    place = (number_ref[2] ^ (first + k)) * number_ref[5] + (number_ref[1] ^ mx)
                    spot = pl.ds(pl.multiple_of(place * rows, rows), rows)
                    made.append(
                        pltpu.make_async_copy(source.at[k], w_ref.at[spot, :], sems.at[len(made)])
                    )
            return made

        @pl.when(step == 0)
        def start():
            for copy in copies():
                copy.start()

        @pl.when(step < steps)
        def project():
            normed, unused = norm_parts(mm(noisy_ref[...], embed_ref[...], 1, 0))
            scale = frame_lines(scale_ref, step * count, count, PER_FRAME)
            shift = frame_lines(shift_ref, step * count, count, PER_FRAME)
            attn_in = to_low(normed * (1.0 + scale) + shift)
            in_ref[...] = attn_in

            @pl.when(step == 0)
            def finish():
                for copy in copies():
                    copy.wait()

            out = mm(attn_in, w_ref[...], 1, 0)
            cos, sin = cos_ref[...], sin_ref[...]
            spot = pl.ds(step * block, block)
            for ref, first, factor in ((q_ref, 0, HD**-0.5), (k_ref, width, 1.0)):
                lower = out[:, first : first + half]
                upper = out[:, first + half : first + width]
                ref[spot, :half] = to_low(lower * cos - upper * sin) * factor
                ref[spot, half:] = to_low(upper * cos + lower * sin) * factor
            v_ref[spot, :] = to_low(out[:, 2 * width :])

        @pl.when(step >= steps)
        def attend():
            frame = step - steps
            first, last = number_ref[base + frame], number_ref[base + FRAMES + frame]
            attend_frame(frame, first, last, q_ref, k_ref, v_ref, o_ref, lse_ref, *scratch)

    lines = lambda wide: ((block, wide), lambda i: (jnp.minimum(i, steps - 1), 0))
    at_frame = lambda i: jnp.maximum(i - steps, 0)
    chips = sum(piece[0].shape[0] for piece in pieces)
    return run_kernel(
        kernel,
        (steps + FRAMES,),
        [
            (noisy, *lines(PD)),
            (embed,),
            (shift,),
            (scale,),
            (cosine, *lines(half)),
            (sine, *lines(half)),
        ]
        + [(piece[0], pl.ANY) for piece in pieces],
        [((TOK, width), bf16)] * 3
        + [
            ((TOK, D), bf16, *lines(D)),
            ((D, columns), bf16),
            (
                (ranks, FRAMES, per_frame, width),
                bf16,
                (ranks, 1, per_frame, width),
                lambda i: (0, at_frame(i), 0, 0),
            ),
            ((FRAMES * stack, 128), f32, (stack, 128), lambda i: (at_frame(i), 0)),
        ],
        [
            pltpu.SemaphoreType.DMA((chips,)),
            pltpu.VMEM((stack, width), bf16),
            pltpu.VMEM((FRAMES, stack, PER_FRAME), f32),
            pltpu.VMEM((stack, 128), f32),
            pltpu.VMEM((stack, 128), f32),
            pltpu.VMEM((stack, width), f32),
        ],
        jnp.concatenate([coords, span.reshape(-1)]),
        after,
        flops=2 * TOK * D * columns + 4 * 36 * PER_FRAME * PER_FRAME * 256 * heads,
        moved=20 * 2**20,
        exps=36 * PER_FRAME * PER_FRAME * heads,
    )


def attend_frame(frame, start, stop, q_ref, k_ref, v_ref, o_ref, lse_ref, q_scr, s_scr, m_scr, l_scr, acc_scr):
    width = q_ref.shape[1]
    heads = width // HD
    block = PER_FRAME
    query = q_ref[pl.ds(frame * block, block), :]
    for head in range(heads):
        q_scr[head * block : (head + 1) * block, :] = jnp.where(
            head_mask(width, head, True), query, jnp.zeros_like(query)
        )
    m_scr[...] = jnp.full_like(m_scr, -1e30)
    l_scr[...] = jnp.zeros_like(l_scr)
    acc_scr[...] = jnp.zeros_like(acc_scr)

    def scores(e, carry):
        keys = k_ref[pl.ds(e * block, block), :]
        for head in range(heads):
            rows = slice(head * block, (head + 1) * block)
            score = mm(q_scr[rows, :], keys, 1, 1)
            s_scr[e, rows, :] = score
            top = jnp.maximum(score[:, :128], score[:, 128:])
            m_scr[rows, :] = jnp.maximum(m_scr[rows, :], top)
        return carry

    lax.fori_loop(start, stop, scores, 0)
    for head in range(heads):
        rows = slice(head * block, (head + 1) * block)
        m_scr[rows, :] = jnp.broadcast_to(
            jnp.max(m_scr[rows, :], axis=1, keepdims=True), (block, 128)
        )

    def combine(e, carry):
        values = v_ref[pl.ds(e * block, block), :]
        for head in range(heads):
            rows = slice(head * block, (head + 1) * block)
            top = m_scr[rows, :]
            left = jnp.exp(s_scr[e, rows, :128] - top)
            right = jnp.exp(s_scr[e, rows, 128:] - top)
            l_scr[rows, :] = l_scr[rows, :] + (left + right)
            weight = jnp.concatenate([to_low(left), to_low(right)], axis=1)
            acc_scr[rows, :] = acc_scr[rows, :] + mm(weight, values, 1, 0)
        return carry

    lax.fori_loop(start, stop, combine, 0)
    result = jnp.zeros((block, width), f32)
    for head in range(heads):
        rows = slice(head * block, (head + 1) * block)
        total = jnp.sum(l_scr[rows, :], axis=1, keepdims=True)
        lse_ref[rows, :] = m_scr[rows, :] + jnp.log(total)
        result = jnp.where(head_mask(width, head, False), acc_scr[rows, :] / total, result)
    o_ref[...] = to_low(result).reshape(o_ref.shape)


def attend_back_kernel(
    span_ref, q_ref, k_ref, v_ref, o_ref, g_ref, lse_ref, cos_ref, sin_ref, out_ref,
    q_scr, g_scr, d_scr, dq_scr, dk_scr, dv_scr, p_scr, s_scr,
):
    frame = pl.program_id(0)
    width = q_ref.shape[1]
    half = width // 2
    heads = width // HD
    block = PER_FRAME
    start, stop = span_ref[0, frame], span_ref[1, frame]

    @pl.when(frame == 0)
    def clear():
        dk_scr[...] = jnp.zeros_like(dk_scr)
        dv_scr[...] = jnp.zeros_like(dv_scr)

    query = q_ref[...]
    grad = g_ref[...].reshape(block, width)
    product = grad.astype(f32) * o_ref[...].reshape(block, width).astype(f32)
    for head in range(heads):
        rows = slice(head * block, (head + 1) * block)
        q_scr[rows, :] = jnp.where(head_mask(width, head, True), query, jnp.zeros_like(query))
        own = head_mask(width, head, False)
        g_scr[rows, :] = jnp.where(own, grad, jnp.zeros_like(grad))
        inner = jnp.sum(jnp.where(own, product, 0.0), axis=1, keepdims=True)
        d_scr[rows, :] = jnp.broadcast_to(inner, (block, 128))
    dq_scr[...] = jnp.zeros_like(dq_scr)

    def step(e, carry):
        spot = pl.ds(e * block, block)
        keys, values = k_ref[spot, :], v_ref[spot, :]
        for head in range(heads):
            rows = slice(head * block, (head + 1) * block)
            score = mm(q_scr[rows, :], keys, 1, 1)
            grad_w = mm(g_scr[rows, :], values, 1, 1)
            lse, inner = lse_ref[rows, :], d_scr[rows, :]
            for part in range(2):
                lanes = slice(part * 128, (part + 1) * 128)
                weight = jnp.exp(score[:, lanes] - lse)
                p_scr[rows, lanes] = to_low(weight)
                s_scr[rows, lanes] = to_low(weight * (grad_w[:, lanes] - inner))
        dq_scr[...] = dq_scr[...] + mm(s_scr[...], keys, 1, 0)
        dk_scr[spot, :] = dk_scr[spot, :] + mm(s_scr[...], q_scr[...], 0, 0)
        dv_scr[spot, :] = dv_scr[spot, :] + mm(p_scr[...], g_scr[...], 0, 0)
        return carry

    lax.fori_loop(start, stop, step, 0)

    def unrotate(grads, cosine, sine, where, base):
        lower, upper = grads[:, :half], grads[:, half:]
        out_ref[where, base : base + half] = to_low(lower * cosine + upper * sine)
        out_ref[where, base + half : base + width] = to_low(upper * cosine - lower * sine)

    total = jnp.zeros((block, width), f32)
    for head in range(heads):
        rows = slice(head * block, (head + 1) * block)
        total = jnp.where(head_mask(width, head, True), dq_scr[rows, :], total)
    spot = pl.ds(frame * block, block)
    unrotate(total * HD**-0.5, cos_ref[spot, :], sin_ref[spot, :], spot, 0)

    @pl.when(frame == FRAMES - 1)
    def finish():
        def one(e, carry):
            spot = pl.ds(e * block, block)
            unrotate(dk_scr[spot, :], cos_ref[spot, :], sin_ref[spot, :], spot, width)
            out_ref[spot, 2 * width :] = to_low(dv_scr[spot, :])
            return carry

        lax.fori_loop(0, FRAMES, one, 0)


def run_attend_back(span, query, keys, values, out, grad, lse, cosine, sine, after=()):
    block = PER_FRAME
    rows, unused, per_frame, width = out.shape
    heads = width // HD
    parts = (rows, 1, per_frame, width), lambda f: (0, f, 0, 0)
    return run_kernel(
        attend_back_kernel,
        (FRAMES,),
        [
            (query, *frame_rows(width)),
            (keys,),
            (values,),
            (out, *parts),
            (grad, *parts),
            (lse, (heads * block, 128), lambda f: (f, 0)),
            (cosine,),
            (sine,),
        ],
        [((TOK, 3 * width), bf16)],
        [
            pltpu.VMEM((heads * block, width), bf16),
            pltpu.VMEM((heads * block, width), bf16),
            pltpu.VMEM((heads * block, 128), f32),
            pltpu.VMEM((heads * block, width), f32),
            pltpu.VMEM((TOK, width), f32),
            pltpu.VMEM((TOK, width), f32),
            pltpu.VMEM((heads * block, block), bf16),
            pltpu.VMEM((heads * block, block), bf16),
        ],
        span,
        after,
        flops=5 * 2 * 36 * block * block * 256 * heads,
        moved=12 * 2**20,
        exps=36 * block * block * heads,
    )[0]


def run_qkv_dw(attn_in, grad, after=()):
    columns = grad.shape[1]
    count = 2
    block, steps = count * PER_FRAME, FRAMES // count

    def kernel(in_ref, g_ref, out_ref, acc):
        step = pl.program_id(0)
        accumulate(acc, step, lambda: mm(in_ref[...], g_ref[...], 0, 0))

        @pl.when(step == steps - 1)
        def finish():
            out_ref[...] = to_low(acc[...])

    return run_kernel(
        kernel,
        (steps,),
        [
            (attn_in, (block, D), lambda i: (i, 0)),
            (grad, (block, columns), lambda i: (i, 0)),
        ],
        [((D, columns), bf16)],
        [pltpu.VMEM((D, columns), f32)],
        after=after,
        flops=2 * TOK * D * columns,
        moved=10 * 2**20,
    )[0]


def run_qkv_back(noisy, embed, scale, grad, weight, after=()):
    columns = weight.shape[1]

    def kernel(noisy_ref, embed_ref, scale_ref, g_ref, w_ref, sum_ref, ge_ref):
        frame = pl.program_id(0)
        noisy = noisy_ref[...]
        normed, inverse = norm_parts(mm(noisy, embed_ref[...], 1, 0))
        grad_in = mm(g_ref[...], w_ref[...], 1, 1)
        spot = pl.ds(frame, 1)
        sum_ref[spot, :D] = jnp.sum(grad_in, axis=0, keepdims=True)
        sum_ref[spot, D:] = jnp.sum(grad_in * normed, axis=0, keepdims=True)
        grad_h = norm_back(normed, inverse, grad_in * (1.0 + scale_ref[spot, :]))
        accumulate(ge_ref, frame, lambda: mm(noisy, to_low(grad_h), 0, 0))

    return run_kernel(
        kernel,
        (FRAMES,),
        [
            (noisy, *frame_rows(PD)),
            (embed,),
            (scale,),
            (grad, *frame_rows(columns)),
            (weight,),
        ],
        [((FRAMES, 2 * D), f32), ((PD, D), f32)],
        after=after,
        flops=2 * TOK * D * columns,
        moved=8 * 2**20,
    )


REST = {
    name: slice(k * D, (k + 1) * D)
    for k, name in enumerate(("gate_a", "shift_m", "scale_m", "gate_m", "shift_f", "scale_f"))
}


def by_frame(ref, name, first, count, per_frame):
    rows = [
        jnp.broadcast_to(ref[pl.ds(first + k, 1), REST[name]], (per_frame, D))
        for k in range(count)
    ]
    return jnp.concatenate(rows, axis=0)


def store_sums(ref, first, number, values, per_frame):
    for k in range(values.shape[0] // per_frame):
        rows = values[k * per_frame : (k + 1) * per_frame]
        lanes = slice(number * D, (number + 1) * D)
        ref[pl.ds(first + k, 1), lanes] = jnp.sum(rows, axis=0, keepdims=True)


def run_proj(coords, attn, noisy, embed, rest, own, other, after=()):
    rows, tokens, width = attn.shape
    per_frame, steps = tokens // FRAMES, 2
    block, count = tokens // steps, FRAMES // steps

    def kernel(coords_ref, a_ref, n_ref, e_ref, rest_ref, own_ref, other_ref, h_ref, p_ref, in_ref):
        first = pl.program_id(0) * count
        mine = coords_ref[3] == 0
        attn_b = jnp.concatenate([a_ref[r] for r in range(rows)], axis=1)
        one, two = mm(attn_b, own_ref[...], 1, 0), mm(attn_b, other_ref[...], 1, 0)
        out = jnp.concatenate([jnp.where(mine, one, two), jnp.where(mine, two, one)], axis=1)
        p_ref[...] = out
        hidden = mm(n_ref[...], e_ref[...], 1, 0)
        hidden = hidden + by_frame(rest_ref, "gate_a", first, count, per_frame) * out
        h_ref[...] = hidden
        normed, unused = norm_parts(hidden)
        scale = by_frame(rest_ref, "scale_m", first, count, per_frame)
        shift = by_frame(rest_ref, "shift_m", first, count, per_frame)
        in_ref[...] = to_low(normed * (1.0 + scale) + shift)

    part = (block, D), lambda i: (i, 0)
    return run_kernel(
        kernel,
        (steps,),
        [
            (attn, (rows, block, width), lambda i: (0, i, 0)),
            (noisy, (block, PD), lambda i: (i, 0)),
            (embed,),
            (rest,),
            (own,),
            (other,),
        ],
        [((tokens, D), f32, *part), ((tokens, D), f32, *part), ((tokens, D), bf16, *part)],
        scalars=coords,
        after=after,
        flops=2 * tokens * D * D,
        moved=10 * 2**20,
    )


GELU_C = math.sqrt(2.0 / math.pi)
GELU_A = 0.044715


def gelu_value(x):
    return 0.5 * x * (1.0 + jnp.tanh(GELU_C * (x + GELU_A * (x * x * x))))


def gelu_slope(x):
    square = x * x
    t = jnp.tanh(GELU_C * x * (1.0 + GELU_A * square))
    return 0.5 * (1.0 + t) + (0.5 * GELU_C) * x * (1.0 - t * t) * (1.0 + 3.0 * GELU_A * square)


CHUNK = 512


def down_rows(weight):
    return weight, (CHUNK, D), lambda j: (j, 0)


def up_columns(weight):
    return weight, (D, CHUNK), lambda j: (0, j)


def run_up(mlp_in, up, after=()):
    tokens, hidden = mlp_in.shape[0], up.shape[1]

    def kernel(in_ref, up_ref, out_ref, act_ref):
        out = mm(in_ref[...], up_ref[...], 1, 0)
        out_ref[...] = out
        act_ref[...] = to_low(gelu_value(out))

    part = (tokens, CHUNK), lambda j: (0, j)
    return run_kernel(
        kernel,
        (hidden // CHUNK,),
        [(mlp_in,), up_columns(up)],
        [((tokens, hidden), f32, *part), ((tokens, hidden), bf16, *part)],
        after=after,
        flops=2 * tokens * D * hidden,
        moved=10 * 2**20,
    )


def parts_of(tokens):
    size = tokens // 2
    return [slice(k * size, (k + 1) * size) for k in range(2)]


def run_up_down(mlp_in, up, down, dtype, after=()):
    tokens, hidden = mlp_in.shape[0], up.shape[1]
    steps = hidden // CHUNK

    def kernel(in_ref, up_ref, down_ref, out_ref, act_ref, part_ref, acc):
        j = pl.program_id(0)

        @pl.when(j == 0)
        def clear():
            acc[...] = jnp.zeros_like(acc)

        spans = parts_of(tokens)
        ready = mm(in_ref[spans[0], :], up_ref[...], 1, 0)
        for k, span in enumerate(spans):
            out = ready
            if k + 1 < len(spans):
                ready = mm(in_ref[spans[k + 1], :], up_ref[...], 1, 0)
            out_ref[span, :] = out
            act_ref[span, :] = to_low(gelu_value(out))
        acc[...] = acc[...] + mm(act_ref[...], down_ref[...], 1, 0)

        @pl.when(j == steps - 1)
        def finish():
            part_ref[...] = acc[...].astype(part_ref.dtype)

    part = (tokens, CHUNK), lambda j: (0, j)
    return run_kernel(
        kernel,
        (steps,),
        [(mlp_in,), up_columns(up), down_rows(down)],
        [
            ((tokens, hidden), f32, *part),
            ((tokens, hidden), bf16, *part),
            ((tokens, D), dtype),
        ],
        [pltpu.VMEM((tokens, D), f32)],
        after=after,
        flops=4 * tokens * D * hidden,
        moved=16 * 2**20,
    )


def accumulate(acc, step, term):
    @pl.when(step == 0)
    def first():
        acc[...] = jnp.zeros_like(acc)

    acc[...] = acc[...] + term()


def run_down(act, down, after=()):
    tokens, hidden = act.shape

    def kernel(act_ref, down_ref, out_ref):
        accumulate(out_ref, pl.program_id(0), lambda: mm(act_ref[...], down_ref[...], 1, 0))

    return run_kernel(
        kernel,
        (hidden // CHUNK,),
        [(act, (tokens, CHUNK), lambda j: (0, j)), down_rows(down)],
        [((tokens, D), f32)],
        after=after,
        flops=2 * tokens * D * hidden,
        moved=8 * 2**20,
    )[0]


def run_head(flags, hidden1, part, got, rest, head, target, after=()):
    tokens = hidden1.shape[0]
    per_frame, count = tokens // FRAMES, 2
    block = count * per_frame

    def kernel(
        flag_ref, h_ref, p_ref, got_ref, rest_ref, head_ref, t_ref,
        gd_ref, gh_ref, sum_ref, ghead_ref, loss_ref,
    ):
        first = pl.program_id(0) * count

        @pl.when(first == 0)
        def clear():
            ghead_ref[...] = jnp.zeros_like(ghead_ref)

        mod = lambda name: by_frame(rest_ref, name, first, count, per_frame)
        frame_of = lax.broadcasted_iota(jnp.int32, (block, 1), 0) // per_frame
        true = jnp.where(frame_of == 0, flag_ref[first], flag_ref[first + 1])
        down_out = p_ref[...] + got_ref[...].astype(f32)
        hidden = h_ref[...] + mod("gate_m") * down_out
        normed, inverse = norm_parts(hidden)
        scale = 1.0 + mod("scale_f")
        final_in = to_low(normed * scale + mod("shift_f"))
        pred = mm(final_in, head_ref[...], 1, 0)
        error = (pred - t_ref[...]) * true
        loss_ref[pl.ds(pl.program_id(0), 1), :] = jnp.broadcast_to(
            jnp.sum(jnp.sum(error * error, axis=1, keepdims=True), axis=0, keepdims=True), (1, 128)
        )
        grad_pred = to_low(2.0 * error / flag_ref[FRAMES])
        ghead_ref[...] = ghead_ref[...] + mm(final_in, grad_pred, 0, 0)
        grad_fin = mm(grad_pred, head_ref[...], 1, 1)
        store_sums(sum_ref, first, 1, grad_fin, per_frame)
        store_sums(sum_ref, first, 2, grad_fin * normed, per_frame)
        grad = norm_back(normed, inverse, grad_fin * scale)
        gh_ref[...] = grad
        store_sums(sum_ref, first, 0, grad * down_out, per_frame)
        gd_ref[...] = to_low(grad * mod("gate_m"))

    part_spec = (block, D), lambda f: (f, 0)
    return run_kernel(
        kernel,
        (FRAMES // count,),
        [
            (flags, pltpu.SMEM),
            (hidden1, *part_spec),
            (part, *part_spec),
            (got, *part_spec),
            (rest,),
            (head,),
            (target, (block, PD), lambda f: (f, 0)),
        ],
        [
            ((tokens, D), bf16, *part_spec),
            ((tokens, D), f32, *part_spec),
            ((FRAMES, 3 * D), f32),
            ((D, PD), f32),
            ((FRAMES // count, 128), f32),
        ],
        after=after,
        flops=8 * tokens * D * PD,
        moved=10 * 2**20,
    )


def run_act_back(grad, down, up_out, after=()):
    tokens, hidden = up_out.shape

    def kernel(g_ref, down_ref, up_ref, out_ref):
        grad_act = mm(g_ref[...], down_ref[...], 1, 1)
        out_ref[...] = to_low(grad_act * gelu_slope(up_ref[...]))

    part = (tokens, CHUNK), lambda j: (0, j)
    return run_kernel(
        kernel,
        (hidden // CHUNK,),
        [(grad,), down_rows(down), (up_out, *part)],
        [((tokens, hidden), bf16, *part)],
        after=after,
        flops=2 * tokens * D * hidden,
        moved=10 * 2**20,
    )[0]


def run_act_up_back(grad, down, up_out, up, dtype, after=()):
    tokens, hidden = up_out.shape
    steps = hidden // CHUNK

    def kernel(g_ref, down_ref, o_ref, up_ref, out_ref, part_ref, acc):
        j = pl.program_id(0)

        @pl.when(j == 0)
        def clear():
            acc[...] = jnp.zeros_like(acc)

        spans = parts_of(tokens)
        ready = mm(g_ref[spans[0], :], down_ref[...], 1, 1)
        for k, span in enumerate(spans):
            grad_act = ready
            if k + 1 < len(spans):
                ready = mm(g_ref[spans[k + 1], :], down_ref[...], 1, 1)
            out_ref[span, :] = to_low(grad_act * gelu_slope(o_ref[span, :]))
        acc[...] = acc[...] + mm(out_ref[...], up_ref[...], 1, 1)

        @pl.when(j == steps - 1)
        def finish():
            part_ref[...] = acc[...].astype(part_ref.dtype)

    part = (tokens, CHUNK), lambda j: (0, j)
    return run_kernel(
        kernel,
        (steps,),
        [(grad,), down_rows(down), (up_out, *part), up_columns(up)],
        [((tokens, hidden), bf16, *part), ((tokens, D), dtype)],
        [pltpu.VMEM((tokens, D), f32)],
        after=after,
        flops=4 * tokens * D * hidden,
        moved=16 * 2**20,
    )


def run_up_back(grad, up, after=()):
    tokens, hidden = grad.shape

    def kernel(g_ref, up_ref, out_ref):
        accumulate(out_ref, pl.program_id(0), lambda: mm(g_ref[...], up_ref[...], 1, 1))

    return run_kernel(
        kernel,
        (hidden // CHUNK,),
        [(grad, (tokens, CHUNK), lambda j: (0, j)), up_columns(up)],
        [((tokens, D), f32)],
        after=after,
        flops=2 * tokens * D * hidden,
        moved=8 * 2**20,
    )[0]


def group_list(sizes):
    ny, nx, nz = sizes
    return [(my, mx) for my in range(ny) for mx in range(nx)]


def run_down_dw(coords, sizes, acts, grads, after=()):
    groups, nz = group_list(sizes), sizes[2]
    hidden = acts[0].shape[1]
    rows = hidden // (len(groups) * nz)
    steps = hidden // CHUNK

    def kernel(coords_ref, a_ref, b_ref, ga_ref, gb_ref, *refs):
        outs, acc = refs[: len(groups)], refs[len(groups)]
        j = pl.program_id(0)
        acc[j] = mm(a_ref[...], ga_ref[...], 0, 0) + mm(b_ref[...], gb_ref[...], 0, 0)

        @pl.when(j == steps - 1)
        def finish():
            for out, (my, mx) in zip(outs, groups):
                for mz in range(nz):
                    first = chip_number(coords_ref, my, mx, mz) * rows
                    spot = pl.ds(pl.multiple_of(first % CHUNK, rows), rows)
                    out[mz] = to_low(acc[first // CHUNK, spot, :])

    part = (acts[0].shape[0], CHUNK), lambda j: (0, j)
    outs = run_kernel(
        kernel,
        (steps,),
        [(acts[0], *part), (acts[1], *part), (grads[0],), (grads[1],)],
        [((nz, rows, D), bf16)] * len(groups),
        [pltpu.VMEM((steps, CHUNK, D), f32)],
        coords,
        after,
        flops=4 * acts[0].shape[0] * D * hidden,
        moved=10 * 2**20,
    )
    return dict(zip(groups, outs))


def run_act_up_dw(coords, sizes, ins, grad_up, grad, down, up_out, up, after=()):
    groups, nz = group_list(sizes), sizes[2]
    rows = D // (len(groups) * nz)
    tokens, hidden = up_out.shape
    steps = hidden // CHUNK

    def kernel(coords_ref, a_ref, b_ref, ga_ref, g_ref, down_ref, o_ref, up_ref, part_ref, *refs):
        outs, (acc, part_acc, gb_scr) = refs[: len(groups)], refs[len(groups) :]
        j = pl.program_id(0)

        @pl.when(j == 0)
        def clear():
            part_acc[...] = jnp.zeros_like(part_acc)

        spans = parts_of(tokens)
        ready = mm(g_ref[spans[0], :], down_ref[...], 1, 1)
        for k, span in enumerate(spans):
            grad_act = ready
            if k + 1 < len(spans):
                ready = mm(g_ref[spans[k + 1], :], down_ref[...], 1, 1)
            gb_scr[span, :] = to_low(grad_act * gelu_slope(o_ref[span, :]))
        acc[...] = mm(a_ref[...], ga_ref[...], 0, 0) + mm(b_ref[...], gb_scr[...], 0, 0)
        part_acc[...] = part_acc[...] + mm(gb_scr[...], up_ref[...], 1, 1)
        for out, (my, mx) in zip(outs, groups):
            for mz in range(nz):
                first = chip_number(coords_ref, my, mx, mz) * rows
                out[mz] = to_low(acc[pl.ds(pl.multiple_of(first, rows), rows), :])

        @pl.when(j == steps - 1)
        def finish():
            part_ref[...] = to_low(part_acc[...])

    part = (tokens, CHUNK), lambda j: (0, j)
    outs = run_kernel(
        kernel,
        (steps,),
        [
            (ins[0],),
            (ins[1],),
            (grad_up, *part),
            (grad,),
            down_rows(down),
            (up_out, *part),
            up_columns(up),
        ],
        [((tokens, D), bf16)]
        + [((nz, rows, hidden), bf16, (nz, rows, CHUNK), lambda j: (0, 0, j))] * len(groups),
        [
            pltpu.VMEM((D, CHUNK), f32),
            pltpu.VMEM((tokens, D), f32),
            pltpu.VMEM((tokens, CHUNK), bf16),
        ],
        coords,
        after,
        flops=8 * tokens * D * hidden,
        moved=26 * 2**20,
    )
    return outs[0], dict(zip(groups, outs[1:]))


def run_add_pieces(coords, sizes, terms, after=()):
    groups, nz = group_list(sizes), sizes[2]
    rows, columns = terms[0].shape[0] // (len(groups) * nz), terms[0].shape[1]

    def kernel(coords_ref, a_ref, b_ref, *refs):
        outs, acc = refs[: len(groups)], refs[len(groups)]
        acc[...] = a_ref[...].astype(f32) + b_ref[...].astype(f32)
        for out, (my, mx) in zip(outs, groups):
            for mz in range(nz):
                first = chip_number(coords_ref, my, mx, mz) * rows
                out[mz] = to_low(acc[pl.ds(pl.multiple_of(first, rows), rows), :])

    outs = run_kernel(
        kernel,
        (1,),
        [(terms[0],), (terms[1],)],
        [((nz, rows, columns), bf16)] * len(groups),
        [pltpu.VMEM(terms[0].shape, f32)],
        coords,
        after,
        moved=6 * terms[0].size,
    )
    return dict(zip(groups, outs))


def run_proj_back(coords, grad_h2, part, got, hidden1, proj_out, rest, own, other, attn, noisy, after=()):
    rows, tokens, width = attn.shape
    per_frame, steps = tokens // FRAMES, 2
    block, count = tokens // steps, FRAMES // steps

    def kernel(
        coords_ref, g_ref, p_ref, got_ref, h_ref, po_ref, rest_ref, own_ref, other_ref, a_ref, n_ref,
        ga_ref, mine_ref, theirs_ref, sum_ref, ge_ref, acc,
    ):
        step = pl.program_id(0)
        first = step * count
        mine = coords_ref[3] == 0
        grad_mlp = p_ref[...] + got_ref[...].astype(f32)
        normed, inverse = norm_parts(h_ref[...])
        store_sums(sum_ref, first, 1, grad_mlp, per_frame)
        store_sums(sum_ref, first, 2, grad_mlp * normed, per_frame)
        scale = by_frame(rest_ref, "scale_m", first, count, per_frame)
        grad = g_ref[...] + norm_back(normed, inverse, grad_mlp * (1.0 + scale))
        store_sums(sum_ref, first, 0, grad * po_ref[...], per_frame)
        low = to_low(grad * by_frame(rest_ref, "gate_a", first, count, per_frame))
        lower, upper = low[:, : D // 2], low[:, D // 2 :]
        grad_attn = mm(jnp.where(mine, lower, upper), own_ref[...], 1, 1)
        grad_attn = grad_attn + mm(jnp.where(mine, upper, lower), other_ref[...], 1, 1)
        grad_attn = to_low(grad_attn)
        attn_b = jnp.concatenate([a_ref[r] for r in range(rows)], axis=1)
        for r in range(rows):
            ga_ref[r] = grad_attn[:, r * width : (r + 1) * width]
        accumulate(acc, step, lambda: mm(attn_b, low, 0, 0))
        accumulate(ge_ref, step, lambda: mm(n_ref[...], to_low(grad), 0, 0))

        @pl.when(step == steps - 1)
        def finish():
            lower, upper = to_low(acc[:, : D // 2]), to_low(acc[:, D // 2 :])
            mine_ref[...] = jnp.where(mine, lower, upper)
            theirs_ref[...] = jnp.where(mine, upper, lower)

    piece = (block, D), lambda i: (i, 0)
    wide = (rows, block, width), lambda i: (0, i, 0)
    return run_kernel(
        kernel,
        (steps,),
        [
            (grad_h2, *piece),
            (part, *piece),
            (got, *piece),
            (hidden1, *piece),
            (proj_out, *piece),
            (rest,),
            (own,),
            (other,),
            (attn, *wide),
            (noisy, (block, PD), lambda i: (i, 0)),
        ],
        [
            ((rows, tokens, width), bf16, *wide),
            ((D, D // 2), bf16),
            ((D, D // 2), bf16),
            ((FRAMES, 3 * D), f32),
            ((PD, D), f32),
        ],
        [pltpu.VMEM((D, D), f32)],
        coords,
        after,
        flops=4 * tokens * D * D,
        moved=18 * 2**20,
    )


def run_lamb(entries, slots, fixes, after=()):
    def kernel(*refs):
        many = len(entries)
        ins, outs = refs[: 4 * many], refs[4 * many : 6 * many]
        sums = refs[6 * many]
        lane = lax.broadcasted_iota(jnp.int32, (1, 128), 1)
        row = jnp.zeros((1, 128), f32)
        for k, slot in enumerate(slots):
            weight, grad, first, second = (ref[...] for ref in ins[4 * k : 4 * k + 4])
            mom_ref, update_ref = outs[2 * k : 2 * k + 2]
            first_n, second_n, update = lamb_direction(weight, grad, first, second, *fixes)
            mom_ref[0] = first_n
            mom_ref[1] = second_n
            update_ref[...] = update
            for value, place in ((weight, 2 * slot), (update, 2 * slot + 1)):
                total = jnp.sum(value * value, axis=0, keepdims=True)
                total = jnp.sum(total, axis=1, keepdims=True)
                row = row + jnp.where(lane == place, total, 0.0)
        sums[...] = row

    outputs = []
    for weight, *unused in entries:
        outputs += [((2,) + weight.shape, f32), (weight.shape, f32)]
    moved = 28 * sum(entry[0].size for entry in entries)
    flat = [(array,) for entry in entries for array in entry]
    outs = run_kernel(kernel, (1,), flat, outputs + [((1, 128), f32)], after=after, moved=moved)
    return outs[0:-1:2], outs[1:-1:2], outs[-1]


def run_update(weights, updates, totals):
    def kernel(totals_ref, *refs):
        many = len(weights)
        lane = lax.broadcasted_iota(jnp.int32, (1, 128), 1)
        norms = jnp.sqrt(jnp.sum(totals_ref[...], axis=0, keepdims=True))
        for k in range(many):
            weight_ref, update_ref, out_ref = refs[k], refs[many + k], refs[2 * many + k]
            pick = lambda at: jnp.sum(jnp.where(lane == at, norms, 0.0), axis=1, keepdims=True)
            trust = learn_rate * (pick(2 * k) / pick(2 * k + 1))
            out_ref[...] = weight_ref[...] - trust * update_ref[...]

    return run_kernel(
        kernel,
        (1,),
        [(totals,)] + [(array,) for array in list(weights) + list(updates)],
        [(weight.shape, f32) for weight in weights],
        moved=12 * sum(weight.size for weight in weights),
    )


def lamb_direction(weight, gradient, first_m, second_m, fix_one, fix_two):
    first_n = beta_one * first_m + (1.0 - beta_one) * gradient
    second_n = jnp.sqrt(beta_two * second_m * second_m + (1.0 - beta_two) * gradient * gradient)
    update = first_n / fix_one / (second_n / math.sqrt(fix_two) + adam_eps) + weight_decay * weight
    return (first_n, second_n, update)


def body(
    latents, noise, levels, clip_ids, clip_lens,
    embed_w, table_w, adaln_w, qkv_w, proj_w, up_w, down_w, head_w,
    embed_avg, table_avg, adaln_avg, qkv_avg, proj_avg, up_avg, down_avg, head_avg,
    embed_sq, table_sq, adaln_sq, qkv_sq, proj_sq, up_sq, down_sq, head_sq,
):
    masters = (embed_w, table_w, adaln_w, qkv_w, proj_w, up_w, down_w, head_w)
    firsts = (embed_avg, table_avg, adaln_avg, qkv_avg, proj_avg, up_avg, down_avg, head_avg)
    seconds = (embed_sq, table_sq, adaln_sq, qkv_sq, proj_sq, up_sq, down_sq, head_sq)
    clips, rows = lax.axis_size("clip"), lax.axis_size("row")
    count_dev = clips * rows
    sizes, unused_bits = shape_of_mesh()
    ny, nx, nz = sizes
    clip_index, row_index = lax.axis_index("clip"), lax.axis_index("row")
    core = row_index % 2
    coords = jnp.stack(
        [
            row_index // 2,
            clip_index % nx,
            clip_index // nx,
            core,
            jnp.full_like(core, ny),
            jnp.full_like(core, nx),
        ]
    ).astype(jnp.int32)
    part = D // count_dev
    width = D // rows
    row_local = GRID // rows
    per_frame = row_local * GRID
    count_tok = FRAMES * per_frame
    hidden = FF // 2
    unit = FF // count_dev
    level_row = levels[0]
    frame_pos, is_true, starts, stops = frame_layout(clip_ids[0], clip_lens[0])
    span = jnp.stack([starts, stops]).astype(jnp.int32)

    own_count = jnp.sum(is_true.astype(f32))
    packed = jnp.concatenate(
        [
            level_row.astype(f32),
            jnp.broadcast_to(own_count, (8,)),
            embed_w.reshape(-1),
            head_w.reshape(-1),
        ]
    )
    everyone = spread(packed.reshape(1, -1), BOTH).reshape(count_dev, -1)
    all_levels = everyone[::rows, :FRAMES].astype(jnp.int32).reshape(-1)
    count = jnp.sum(everyone[::rows, FRAMES]) * PER_FRAME
    embed_b = to_low(everyone[:, 16 : 16 + PD * part].reshape(count_dev, PD, part))
    embed_b = embed_b.transpose(1, 0, 2).reshape(PD, D)
    head_b = to_low(everyone[:, 16 + PD * part :]).reshape(D, PD)

    one_hot = (all_levels[:, None] == jnp.arange(LEVELS, dtype=jnp.int32)[None, :]).astype(f32)
    cond = dot_low("fl,ld->fd", to_low(one_hot), to_low(table_w))
    cond_act = to_low(jax.nn.silu(cond))
    adaln_low = to_low(adaln_w)

    def mod_terms(lower, upper):
        wide = (upper - lower) * D // rows
        terms = to_low(dot_low("fd,dm->fm", cond_act, adaln_low[:, lower * D : upper * D]))
        terms = terms.reshape(clips, FRAMES, rows, wide).transpose(0, 2, 1, 3)
        return terms.reshape(count_dev, FRAMES, wide)

    def modulation(terms):
        total = row_gather(jnp.sum(terms.astype(f32), axis=0))
        return total.transpose(1, 0, 2).reshape(FRAMES, -1)

    first_terms = lax.all_to_all(mod_terms(0, 2), BOTH, 0, 0, tiled=True)
    first = modulation(first_terms)
    shift_a, scale_a = first[:, :D], first[:, D:]

    alpha, sigma = noise_mix(level_row)
    clean = latents[0].reshape(FRAMES, per_frame, PD)
    fresh = noise[0].reshape(FRAMES, per_frame, PD)
    noisy = alpha[:, None, None] * clean + sigma[:, None, None] * fresh
    target = (alpha[:, None, None] * fresh - sigma[:, None, None] * clean).reshape(count_tok, PD)
    noisy_own = to_low(noisy).reshape(count_tok, PD)
    perm = rotary_permutation(width)
    qkv_low = to_low(qkv_w).reshape(part, 3, rows, width)
    turned = to_low(dot_low("dgrw,wv->rdgv", qkv_low[:, :2], perm))
    mine = jnp.concatenate([turned, qkv_low[:, 2:].transpose(2, 0, 1, 3)], axis=2)
    mine = mine.reshape(rows, part, 3 * width)
    token_cols = count_tok * PD // part
    tokens = jnp.broadcast_to(noisy_own.reshape(1, part, token_cols), (rows, part, token_cols))
    mine = row_swap(jnp.concatenate([mine, tokens], axis=2))
    noisy_all = mine[:, :, 3 * width :].reshape(rows, FRAMES, per_frame, PD)
    noisy_all = noisy_all.transpose(1, 0, 2, 3).reshape(TOK, PD)
    def halves(weight, blocks):
        parts = weight.reshape(weight.shape[0], -1, 2, weight.shape[1] // (2 * blocks))
        mine = lax.dynamic_index_in_dim(parts, core, 2, keepdims=False)
        theirs = lax.dynamic_index_in_dim(parts, 1 - core, 2, keepdims=False)
        return mine.reshape(weight.shape[0], -1), theirs.reshape(weight.shape[0], -1)

    up_mine, up_theirs = halves(to_low(up_w), count_dev // 2)
    proj_mine, proj_theirs = halves(to_low(proj_w), 1)
    tall_mine = jnp.concatenate([up_mine, proj_mine], axis=1)
    tall_got = exchange(jnp.concatenate([up_theirs, proj_theirs], axis=1), 1)
    is_zero = core == 0
    tall = jnp.concatenate(
        [jnp.where(is_zero, tall_mine, tall_got), jnp.where(is_zero, tall_got, tall_mine)]
    )
    gather_down = Gather(to_low(down_w))
    gather_down.go_z()
    gather_down.go_xy()
    gather_down.go_slant()
    mine = tie(mine[:, :, : 3 * width], gather_down.own)
    gather_qkv = Gather(mine.reshape(rows * part, 3 * width), False)
    gather_qkv.go_z(first_terms)
    gather_qkv.go_xy()
    gather_qkv.go_slant()
    gather_tall = Gather(tie(tall, gather_qkv.own, *gather_down.came_xy()))
    gather_tall.go_z()
    gather_tall.go_direct()
    rest_sent = mod_terms(2, 8)

    cosine, sine = group_angles(frame_pos, width // 2)
    rest_terms = lax.all_to_all(rest_sent, BOTH, 0, 0, tiled=True)
    query, keys, values, attn_in, qkv_b, attn_heads, lse = run_qkv_attend(
        coords, span, noisy_all, embed_b, shift_a, scale_a, cosine, sine, gather_qkv.pieces(),
        rows, after=(gather_tall.own, rest_sent) + tuple(piece[0] for piece in gather_down.slant),
    )
    rest_terms = tie(rest_terms, query)
    rest = modulation(rest_terms)

    def swap_row(wide):
        return lax.all_to_all(wide, "row", 0, 0, tiled=True)

    attn = tie(attn_heads, rest_terms).reshape(rows, count_tok, width)
    attn = swap_row(attn)
    down_b = run_place(coords, gather_down.pieces(), (D,), after=(attn_heads,))[0]
    up_b, proj_own = run_place(
        coords, gather_tall.pieces(), (hidden, D // 2), after=(down_b,)
    )
    proj_other = exchange(proj_own, 1)
    hidden1, proj_out, mlp_in = run_proj(
        coords, attn, noisy_own, embed_b, rest, proj_own, proj_other
    )
    mlp_in_other = exchange(mlp_in, 1)
    up_out_other, act_other, part_other = run_up_down(mlp_in_other, up_b, down_b, bf16)
    part_got = exchange(part_other, 1)
    up_out, act, part_own = run_up_down(mlp_in, up_b, down_b, f32, after=(part_other,))
    flags = jnp.concatenate([is_true.astype(f32), (PD * count).reshape(1)])
    grad_down_out, grad_h2, sums_f, grad_head, losses = run_head(
        flags, hidden1, part_own, part_got, rest, head_b, target
    )
    loss_local = jnp.sum(losses[:, 0])

    grad_down_other = exchange(grad_down_out, 1)
    down_groups = run_down_dw(
        coords, sizes, (act, act_other), (grad_down_out, grad_down_other)
    )
    scatter_down = Scatter(down_groups)
    grad_up, mlp_own = run_act_up_back(
        grad_down_out, down_b, up_out, up_b, f32, after=(down_groups[0, 0],)
    )
    mlp_other, up_groups = run_act_up_dw(
        coords, sizes, (mlp_in, mlp_in_other), grad_up, grad_down_other, down_b,
        up_out_other, up_b, after=tuple(scatter_down.sent.values()),
    )
    mlp_got = exchange(mlp_other, 1)
    scatter_down.go_xy()
    scatter_down.go_z(up_groups[0, 0])
    grad_attn, proj_mine, proj_theirs, sums_m, embed_h1 = run_proj_back(
        coords, grad_h2, mlp_own, mlp_got, hidden1, proj_out, rest,
        proj_own, proj_other, attn, noisy_own, after=(scatter_down.own,),
    )
    grad_attn = swap_row(grad_attn).reshape(rows, FRAMES, per_frame, width)
    scatter_up = Scatter(up_groups, grad_attn)
    proj_groups = run_add_pieces(coords, sizes, (proj_mine, exchange(proj_theirs, 1)))
    scatter_up.go_xy(proj_groups, grad_attn)

    def mod_row(values_mod, *hold):
        wide = values_mod.shape[1] // rows
        total = to_low(row_sum(values_mod, *hold))
        return lax.dynamic_slice_in_dim(total, row_index * wide, wide, axis=1)

    def mod_all(total):
        wide = total.shape[-1]
        total = total.reshape(clips, rows, FRAMES, wide)
        return total.transpose(0, 2, 1, 3).reshape(clips * FRAMES, rows * wide)

    mod_rest = spread(mod_row(jnp.concatenate([sums_m, sums_f], axis=1)), BOTH)
    grad_qkv = run_attend_back(
        span, query, keys, values, attn_heads, grad_attn, lse, cosine, sine,
        after=(proj_groups[0, 0],) + tuple(scatter_up.sent.values()),
    )
    scatter_up.go_z(grad_qkv)
    grad_qkv_w = run_qkv_dw(
        attn_in, grad_qkv, after=(scatter_up.own, mod_rest, *scatter_down.came_z)
    )
    qkv_terms = grad_qkv_w.reshape(count_dev, part, 3 * width)
    qkv_terms = lax.all_to_all(qkv_terms, BOTH, 0, 0, tiled=True)
    sums_a, grad_embed = run_qkv_back(
        noisy_all, embed_b, scale_a, grad_qkv, qkv_b,
        after=(grad_qkv_w, *scatter_up.came_z),
    )
    tall_sum = scatter_up.result()
    down_sum = scatter_down.result(sums_a)
    grad_embed = grad_embed + embed_h1

    keep = lax.dynamic_slice_in_dim(tall_sum, core * part, part)
    got = exchange(to_low(lax.dynamic_slice_in_dim(tall_sum, (1 - core) * part, part)), 1)
    got = got.astype(f32)
    pair_sum = jnp.stack([jnp.where(is_zero, keep, got), jnp.where(is_zero, got, keep)], axis=1)
    up_sum = pair_sum[:, :, :hidden].reshape(part, 2, count_dev // 2, unit)
    up_sum = up_sum.transpose(0, 2, 1, 3).reshape(part, FF)
    proj_sum = pair_sum[:, :, hidden:].reshape(part, D)
    small = jnp.concatenate(
        [
            grad_embed.reshape(PD, count_dev, part).transpose(1, 0, 2).reshape(count_dev, -1),
            grad_head.reshape(count_dev, -1),
        ],
        axis=1,
    )
    small = to_low(small).reshape(count_dev, 1, -1)
    mod_first = mod_row(sums_a)
    wide = mod_first.shape[-1]
    lines = max(small.shape[-1] // wide, 1)
    small = jnp.pad(small, ((0, 0), (0, 0), (0, lines * wide - small.shape[-1])))
    last = jnp.concatenate(
        [
            jnp.broadcast_to(mod_first[None], (count_dev, FRAMES, wide)),
            small.reshape(count_dev, lines, wide),
        ],
        axis=1,
    )
    last = lax.all_to_all(tie(last, qkv_terms), BOTH, 0, 0, tiled=True)
    small = jnp.sum(last[:, FRAMES:].astype(f32), axis=0).reshape(-1)
    embed_sum = small[: PD * part].reshape(PD, part)
    head_sum = small[PD * part : 2 * PD * part].reshape(part, PD)
    qkv_sum = qkv_terms.reshape(clips, rows, part, 3, width).astype(f32)
    qkv_sum = to_low(jnp.sum(qkv_sum, axis=0))
    turned = dot_low("rdgv,wv->dgrw", qkv_sum[:, :, :2], perm)
    straight = qkv_sum[:, :, 2:].transpose(1, 2, 0, 3).astype(f32)
    qkv_sum = jnp.concatenate([turned, straight], axis=1).reshape(part, 3 * D)

    grad_mod_b = jnp.concatenate([mod_all(last[:, :FRAMES]), mod_all(mod_rest)], axis=1)
    grad_adaln = dot_low("fd,fm->dm", cond_act, grad_mod_b)
    grad_cond_act = dot_low("fm,dm->fd", grad_mod_b, adaln_low)
    unused_silu, silu_pull = jax.vjp(jax.nn.silu, cond)
    grad_cond = silu_pull(grad_cond_act)[0]
    grad_table = jnp.einsum(
        "fl,fd->dl", one_hot, grad_cond, precision=precise, preferred_element_type=f32
    )

    fixes = (1.0 - beta_one**STEP, 1.0 - beta_two**STEP)
    reduced = (
        embed_sum, grad_table, grad_adaln, qkv_sum, proj_sum, up_sum, down_sum, head_sum.T,
    )
    turned = (1, 7)
    flip = lambda k, array: jnp.swapaxes(array, -1, -2) if k in turned else array
    weights = [flip(k, array) for k, array in enumerate(masters)]
    entries = [
        (weights[k], reduced[k], flip(k, firsts[k]), flip(k, seconds[k])) for k in range(8)
    ]
    moms, updates, rows_of_sums = [None] * 8, [None] * 8, []
    for group in ((6,), (4, 5), (3,), (0, 1, 2, 7)):
        got_moms, got_updates, sums = run_lamb([entries[k] for k in group], group, fixes)
        rows_of_sums.append(sums)
        for k, mom, update in zip(group, got_moms, got_updates):
            moms[k], updates[k] = flip(k, mom), update
    lane = jnp.arange(128, dtype=jnp.int32)[None, :]
    sums = sum(rows_of_sums) + jnp.where(lane == 16, loss_local, 0.0)
    totals = spread(sums, BOTH).reshape(count_dev, 128)
    news = run_update(weights, updates, totals)
    news = [flip(k, array) for k, array in enumerate(news)]
    totals = jnp.sum(totals, axis=0)
    norms = jnp.sqrt(totals[:16].reshape(8, 2))
    return (*news, *moms, norms, totals[16:17] / (PD * count))


def solution(mesh):
    wide, tall = P(None, BOTH), P(BOTH, None)
    weights = (wide, wide, tall, tall, tall, tall, tall, tall)
    moments = (P(None, None, BOTH),) * 2 + (P(None, BOTH, None),) * 6
    return jax.shard_map(
        body,
        mesh=mesh,
        in_specs=(
            P("clip", None, "row", None),
            P("clip", None, "row", None),
            P("clip", None),
            P("clip", None),
            P("clip", None),
        )
        + weights * 3,
        out_specs=weights + moments + (P(), P()),
        check_vma=False,
    )
```

```python
import functools
import math

import jax
import jax.numpy as jnp
from jax import lax
from jax.experimental import pallas as pl
from jax.experimental.pallas import tpu as pltpu
from jax.sharding import PartitionSpec as P

D = 1024
HEADS = 16
HD = 64
FF = 4096
PD = 16
GRID = 16
LEVELS = 1000
STEP = 7
FRAMES = 8
CLIPS = 2
PER_FRAME = GRID * GRID
TOK = FRAMES * PER_FRAME
BOTH = ("clip", "row")
VMEM_BYTES = 56 * 1024 * 1024

precise = lax.Precision.HIGHEST
beta_one = 0.9
beta_two = 0.999
adam_eps = 1e-08
weight_decay = 0.01
learn_rate = 1.0
norm_eps = 1e-06
f32 = jnp.float32
bf16 = jnp.bfloat16


def to_low(values):
    return values.astype(bf16)


def dot_low(formula, left, right):
    return jnp.einsum(formula, left, right, preferred_element_type=f32)


def mm(left, right, left_dim, right_dim):
    return lax.dot_general(
        left, right, (((left_dim,), (right_dim,)), ((), ())), preferred_element_type=f32
    )


def layer_norm(values):
    center = values - jnp.mean(values, axis=-1, keepdims=True)
    spread = jnp.mean(center * center, axis=-1, keepdims=True)
    return center * lax.rsqrt(spread + norm_eps)


def norm_parts(values):
    center = values - jnp.mean(values, axis=-1, keepdims=True)
    spread = jnp.mean(center * center, axis=-1, keepdims=True)
    inverse = lax.rsqrt(spread + norm_eps)
    return center * inverse, inverse


def norm_back(normed, inverse, grad):
    mean_g = jnp.mean(grad, axis=-1, keepdims=True)
    mean_gn = jnp.mean(grad * normed, axis=-1, keepdims=True)
    return inverse * (grad - mean_g - normed * mean_gn)


def modulate(normed, shift, scale):
    return normed * (1.0 + scale[:, None, :]) + shift[:, None, :]


def gelu_tanh(values):
    return jax.nn.gelu(values, approximate=True)


def frame_layout(clip_row, length_row):
    frame_idx = jnp.arange(FRAMES, dtype=jnp.int32)
    same_clip = clip_row[:, None] == clip_row[None, :]
    starts = jnp.min(jnp.where(same_clip, frame_idx[None, :], FRAMES), axis=1)
    frame_pos = frame_idx - starts
    slot_idx = jnp.arange(CLIPS, dtype=jnp.int32)
    length = jnp.sum(
        jnp.where(clip_row[:, None] == slot_idx[None, :], length_row[None, :], 0), axis=1
    )
    is_true = frame_pos < length
    stops = jnp.minimum(frame_idx + 1, starts + length)
    return (frame_pos, is_true, starts, stops)


def noise_mix(level_row):
    angle = (level_row.astype(f32) + 0.5) * (math.pi / (2 * LEVELS))
    return (jnp.cos(angle), jnp.sin(angle))


def group_angles(frame_pos, lanes):
    place = jnp.arange(GRID, dtype=jnp.int32)
    j = jnp.arange(lanes, dtype=jnp.int32) % (HD // 2)
    edges = (0, HD // 8, HD // 8 + 3 * HD // 16, HD // 2)
    tables, masks = [], []
    for k, along in enumerate((frame_pos, place, place)):
        size = edges[k + 1] - edges[k]
        frequency = 10000.0 ** (-(j - edges[k]).astype(f32) / size)
        masks.append((j >= edges[k]) & (j < edges[k + 1]))
        frequency = jnp.where(masks[k], frequency, 0.0)
        tables.append(along.astype(f32)[:, None] * frequency[None, :])
    shape = (FRAMES, GRID, GRID, lanes)
    result = []
    for fn in (jnp.cos, jnp.sin):
        at_f = fn(tables[0])[:, None, None, :]
        at_r = fn(tables[1])[None, :, None, :]
        at_c = fn(tables[2])[None, None, :, :]
        value = jnp.where(masks[0], at_f, jnp.where(masks[1], at_r, at_c))
        result.append(jnp.broadcast_to(value, shape).reshape(TOK, lanes))
    return result


def rotary_order(width):
    order = []
    heads = width // HD
    for half in range(2):
        for head in range(heads):
            offset = 0
            for part in (HD // 4, 3 * HD // 8, 3 * HD // 8):
                start = head * HD + offset + half * (part // 2)
                order.extend(range(start, start + part // 2))
                offset += part
    return order


def rotary_permutation(width):
    order = jnp.array(rotary_order(width), dtype=jnp.int32)
    return (jnp.arange(width, dtype=jnp.int32)[:, None] == order[None, :]).astype(bf16)


def shape_of_mesh():
    clips, rows = lax.axis_size("clip"), lax.axis_size("row")
    ny, nz = rows // 2, 4
    nx = clips // nz
    bits = [count.bit_length() - 1 for count in (rows, rows * nx)]
    return (ny, nx, nz), (1, bits[0], bits[1])


def exchange(values, mask):
    count = lax.axis_size("clip") * lax.axis_size("row")
    return lax.ppermute(values, BOTH, [(i, i ^ mask) for i in range(count)])


def along(number):
    sizes, bits = shape_of_mesh()
    return {m: m << bits[number] for m in range(1, sizes[number])}


class Gather:
    def __init__(self, shard, use_y=True):
        self.shard = shard
        self.z_masks, self.x_masks = along(2), along(1)
        self.y_masks = along(0) if use_y else {}

    def go_z(self, *hold):
        came = [exchange(self.shard, mask) for mask in self.z_masks.values()]
        self.own = jnp.stack([self.shard] + came)
        if hold:
            self.own = tie(self.own, *hold)

    def go_direct(self):
        self.go_xy()
        self.slant = [
            (exchange(self.own, y_mask ^ x_mask), my, mx, 0)
            for my, y_mask in self.y_masks.items()
            for mx, x_mask in self.x_masks.items()
        ]

    def go_xy(self, hold_x=()):
        self.at_y = {m: exchange(self.own, mask) for m, mask in self.y_masks.items()}
        sent = tie(self.own, *hold_x) if hold_x else self.own
        self.at_x = {m: exchange(sent, mask) for m, mask in self.x_masks.items()}

    def came_xy(self):
        return tuple(self.at_y.values()) + tuple(self.at_x.values())

    def go_slant(self, *hold):
        at_y, at_x = self.at_y, self.at_x
        if hold:
            at_y = {m: tie(array, *hold) for m, array in at_y.items()}
            at_x = {m: tie(array, *hold) for m, array in at_x.items()}
        half = self.own.shape[0] // 2
        self.slant = []
        for my in at_y:
            for mx in at_x:
                self.slant.append((exchange(at_y[my][:half], self.x_masks[mx]), my, mx, 0))
                self.slant.append((exchange(at_x[mx][half:], self.y_masks[my]), my, mx, half))

    def pieces(self):
        pieces = [(self.own, 0, 0, 0)]
        pieces += [(array, m, 0, 0) for m, array in self.at_y.items()]
        pieces += [(array, 0, m, 0) for m, array in self.at_x.items()]
        return pieces + self.slant


class Scatter:
    def __init__(self, groups, *hold):
        self.groups = groups
        self.z_masks, self.x_masks, self.y_masks = along(2), along(1), along(0)
        half = groups[0, 0].shape[0] // 2
        at_y = {m: [[], []] for m in self.y_masks}
        at_x = {m: [[], []] for m in self.x_masks}
        for my in self.y_masks:
            for mx in self.x_masks:
                piece = groups[my, mx]
                one = exchange(piece[:half], self.x_masks[mx])
                two = exchange(piece[half:], self.y_masks[my])
                if hold:
                    one, two = tie(one, *hold), tie(two, *hold)
                at_y[my][0].append(one)
                at_x[mx][1].append(two)

        def joined(piece, terms):
            if not (terms[0] or terms[1]):
                return piece
            parts = total(piece[:half], terms[0]), total(piece[half:], terms[1])
            return jnp.concatenate(parts)

        self.sent = {(m, 0): joined(groups[m, 0], at_y[m]) for m in self.y_masks}
        self.sent.update({(0, m): joined(groups[0, m], at_x[m]) for m in self.x_masks})

    def go_xy(self, extra=None, *hold):
        masks = {(m, 0): mask for m, mask in self.y_masks.items()}
        masks.update({(0, m): mask for m, mask in self.x_masks.items()})
        sent, self.extra, slant = dict(self.sent), extra, []
        if extra is not None:
            sent = {g: jnp.concatenate([piece, extra[g]], axis=2) for g, piece in sent.items()}
            slant = [(extra[my, mx], self.y_masks[my] ^ self.x_masks[mx])
                     for my in self.y_masks for mx in self.x_masks]
        if hold:
            sent = {g: tie(piece, *hold) for g, piece in sent.items()}
        self.came = [exchange(piece, masks[g]) for g, piece in sent.items()]
        self.came_slant = [exchange(piece, mask) for piece, mask in slant]

    def take_xy(self, *hold):
        came = list(self.came)
        if hold:
            came = [tie(array, *hold) for array in came]
        width = self.groups[0, 0].shape[2]
        self.own = total(self.groups[0, 0], [array[:, :, :width] for array in came])
        if self.extra is not None:
            terms = [array[:, :, width:] for array in came] + self.came_slant
            self.own = jnp.concatenate([self.own, total(self.extra[0, 0], terms)], axis=2)

    def go_z(self, *hold):
        own = tie(self.own, *hold) if hold else self.own
        self.came_z = [exchange(own[m], mask) for m, mask in self.z_masks.items()]

    def result(self, *hold):
        came = list(self.came_z)
        if hold:
            came = [tie(array, *hold) for array in came]
        value = self.own[0].astype(f32)
        for array in came:
            value = value + array.astype(f32)
        return value


def total(piece, terms):
    if not terms:
        return piece
    value = piece.astype(f32)
    for term in terms:
        value = value + term.astype(f32)
    return to_low(value)


def tie(values, *others):
    return lax.optimization_barrier((values,) + others)[0]


def row_masks():
    return [1 << bit for bit in range(lax.axis_size("row").bit_length() - 1)]


def row_sum(values, *hold):
    for mask in row_masks():
        values = values + exchange(to_low(values), mask).astype(f32)
    return tie(values, *hold) if hold else values


def row_gather(values):
    place = lax.axis_index("row")
    values = values[None]
    for mask in row_masks():
        other = exchange(values, mask)
        first = place & mask == 0
        values = jnp.concatenate(
            [jnp.where(first, values, other), jnp.where(first, other, values)], axis=0
        )
    return values


def row_swap(values):
    place = lax.axis_index("row")
    steps = len(row_masks())
    values = values.reshape((2,) * steps + values.shape[1:])
    for step, mask in enumerate(row_masks()):
        axis = steps - 1 - step
        mine = (place >> step) & 1
        keep = lax.dynamic_index_in_dim(values, mine, axis, keepdims=False)
        got = exchange(lax.dynamic_index_in_dim(values, 1 - mine, axis, keepdims=False), mask)
        low, high = jnp.where(mine == 0, keep, got), jnp.where(mine == 0, got, keep)
        values = jnp.stack([low, high], axis=axis)
    return values.reshape((-1,) + values.shape[steps:])


def spread(values, axes):
    names = axes if isinstance(axes, tuple) else (axes,)
    count = 1
    for name in names:
        count *= lax.axis_size(name)
    copies = jnp.broadcast_to(values[None], (count,) + values.shape)
    return lax.all_to_all(copies, axes, 0, 0, tiled=True)


def run_kernel(
    kernel, grid, inputs, outputs, scratch=(), scalars=None, after=(), flops=0, moved=2**22, exps=0
):
    count = 0 if scalars is None else 1

    def spec(block, index):
        if index is None:
            zeros = (0,) * len(block)
            return pl.BlockSpec(block, lambda *ids: zeros)
        return pl.BlockSpec(block, lambda *ids: index(*ids[: len(grid)]))

    arrays, in_specs = [], []
    for entry in inputs:
        arrays.append(entry[0])
        if len(entry) == 1:
            in_specs.append(spec(entry[0].shape, None))
        elif len(entry) == 2:
            in_specs.append(pl.BlockSpec(memory_space=entry[1]))
        else:
            in_specs.append(spec(entry[1], entry[2]))
    many, extra = len(arrays), len(after)
    arrays.extend(after)
    in_specs.extend([pl.BlockSpec(memory_space=pl.ANY)] * extra)
    out_specs, out_shape = [], []
    for shape, dtype, *rest in outputs:
        out_shape.append(jax.ShapeDtypeStruct(shape, dtype))
        if not rest:
            out_specs.append(spec(shape, None))
        elif len(rest) == 1:
            out_specs.append(pl.BlockSpec(memory_space=rest[0]))
        else:
            out_specs.append(spec(*rest))

    def wrapped(*refs):
        kernel(*refs[: count + many], *refs[count + many + extra :])

    call = pl.pallas_call(
        wrapped,
        grid_spec=pltpu.PrefetchScalarGridSpec(
            num_scalar_prefetch=count,
            grid=grid,
            in_specs=in_specs,
            out_specs=out_specs,
            scratch_shapes=list(scratch),
        ),
        out_shape=out_shape,
        compiler_params=pltpu.CompilerParams(vmem_limit_bytes=VMEM_BYTES),
        cost_estimate=pl.CostEstimate(flops=flops, bytes_accessed=moved, transcendentals=exps),
    )
    return call(*([] if scalars is None else [scalars]), *arrays)


def frame_rows(columns):
    return (PER_FRAME, columns), lambda f: (f, 0)


def frame_lines(ref, first, count, per_frame):
    lines = [
        jnp.broadcast_to(ref[pl.ds(first + k, 1), :], (per_frame, ref.shape[1]))
        for k in range(count)
    ]
    return jnp.concatenate(lines, axis=0)


def head_mask(width, head, rotary):
    lane = lax.broadcasted_iota(jnp.int32, (1, width), 1)
    if rotary:
        return (lane % (width // 2)) // (HD // 2) == head
    return lane // HD == head


def chip_number(coords, my, mx, mz):
    return ((coords[2] ^ mz) * coords[5] + (coords[1] ^ mx)) * coords[4] + (coords[0] ^ my)


def run_place(coords, pieces, columns, after=()):
    rows = pieces[0][0].shape[1]
    chips = sum(piece[0].shape[0] for piece in pieces)
    edges = [sum(columns[:k]) for k in range(len(columns) + 1)]

    def kernel(coords_ref, *refs):
        sources = refs[: len(pieces)]
        targets = refs[len(pieces) : len(pieces) + len(columns)]
        sems = refs[-1]
        copies = []
        for source, (array, my, mx, first) in zip(sources, pieces):
            for k in range(array.shape[0]):
                chip = chip_number(coords_ref, my, mx, first + k)
                spot = pl.ds(pl.multiple_of(chip * rows, rows), rows)
                for number, target in enumerate(targets):
                    lanes = pl.ds(edges[number], columns[number])
                    copies.append(
                        pltpu.make_async_copy(
                            source.at[k, :, lanes], target.at[spot, :], sems.at[len(copies)]
                        )
                    )
        for copy in copies:
            copy.start()
        for copy in copies:
            copy.wait()

    return run_kernel(
        kernel,
        (1,),
        [(piece[0], pl.ANY) for piece in pieces],
        [((chips * rows, wide), bf16) for wide in columns],
        [pltpu.SemaphoreType.DMA((chips * len(columns),))],
        coords,
        after,
        moved=4 * chips * rows * sum(columns),
    )


def run_qkv_attend(coords, span, noisy, embed, shift, scale, cosine, sine, pieces, ranks, after=()):
    rows, columns = pieces[0][0].shape[1:]
    width = columns // 3
    half, heads, per_frame = width // 2, width // HD, PER_FRAME // ranks
    count = 2
    block, steps = count * PER_FRAME, FRAMES // count
    stack = heads * PER_FRAME
    base = coords.shape[0]

    def kernel(number_ref, noisy_ref, embed_ref, shift_ref, scale_ref, cos_ref, sin_ref, *refs):
        sources = refs[: len(pieces)]
        q_ref, k_ref, v_ref, in_ref, w_ref, o_ref, lse_ref, sems, *scratch = refs[len(pieces) :]
        step = pl.program_id(0)

        def copies():
            made = []
            for source, (array, my, mx, first) in zip(sources, pieces):
                for k in range(array.shape[0]):
                    place = (number_ref[2] ^ (first + k)) * number_ref[5] + (number_ref[1] ^ mx)
                    spot = pl.ds(pl.multiple_of(place * rows, rows), rows)
                    made.append(
                        pltpu.make_async_copy(source.at[k], w_ref.at[spot, :], sems.at[len(made)])
                    )
            return made

        @pl.when(step == 0)
        def start():
            for copy in copies():
                copy.start()

        @pl.when(step < steps)
        def project():
            normed, unused = norm_parts(mm(noisy_ref[...], embed_ref[...], 1, 0))
            scale = frame_lines(scale_ref, step * count, count, PER_FRAME)
            shift = frame_lines(shift_ref, step * count, count, PER_FRAME)
            attn_in = to_low(normed * (1.0 + scale) + shift)
            in_ref[...] = attn_in

            @pl.when(step == 0)
            def finish():
                for copy in copies():
                    copy.wait()

            out = mm(attn_in, w_ref[...], 1, 0)
            cos, sin = cos_ref[...], sin_ref[...]
            spot = pl.ds(step * block, block)
            for ref, first, factor in ((q_ref, 0, HD**-0.5), (k_ref, width, 1.0)):
                lower = out[:, first : first + half]
                upper = out[:, first + half : first + width]
                ref[spot, :half] = to_low(lower * cos - upper * sin) * factor
                ref[spot, half:] = to_low(upper * cos + lower * sin) * factor
            v_ref[spot, :] = to_low(out[:, 2 * width :])

        @pl.when(step >= steps)
        def attend():
            frame = step - steps
            first, last = number_ref[base + frame], number_ref[base + FRAMES + frame]
            attend_frame(frame, first, last, q_ref, k_ref, v_ref, o_ref, lse_ref, *scratch)

    lines = lambda wide: ((block, wide), lambda i: (jnp.minimum(i, steps - 1), 0))
    at_frame = lambda i: jnp.maximum(i - steps, 0)
    chips = sum(piece[0].shape[0] for piece in pieces)
    return run_kernel(
        kernel,
        (steps + FRAMES,),
        [
            (noisy, *lines(PD)),
            (embed,),
            (shift,),
            (scale,),
            (cosine, *lines(half)),
            (sine, *lines(half)),
        ]
        + [(piece[0], pl.ANY) for piece in pieces],
        [((TOK, width), bf16)] * 3
        + [
            ((TOK, D), bf16, *lines(D)),
            ((D, columns), bf16),
            (
                (ranks, FRAMES, per_frame, width),
                bf16,
                (ranks, 1, per_frame, width),
                lambda i: (0, at_frame(i), 0, 0),
            ),
            ((FRAMES * stack, 128), f32, (stack, 128), lambda i: (at_frame(i), 0)),
        ],
        [
            pltpu.SemaphoreType.DMA((chips,)),
            pltpu.VMEM((stack, width), bf16),
            pltpu.VMEM((FRAMES, stack, PER_FRAME), f32),
            pltpu.VMEM((stack, 128), f32),
            pltpu.VMEM((stack, 128), f32),
            pltpu.VMEM((stack, width), f32),
        ],
        jnp.concatenate([coords, span.reshape(-1)]),
        after,
        flops=2 * TOK * D * columns + 4 * 36 * PER_FRAME * PER_FRAME * 256 * heads,
        moved=20 * 2**20,
        exps=36 * PER_FRAME * PER_FRAME * heads,
    )


def attend_frame(frame, start, stop, q_ref, k_ref, v_ref, o_ref, lse_ref, q_scr, s_scr, m_scr, l_scr, acc_scr):
    width = q_ref.shape[1]
    heads = width // HD
    block = PER_FRAME
    query = q_ref[pl.ds(frame * block, block), :]
    for head in range(heads):
        q_scr[head * block : (head + 1) * block, :] = jnp.where(
            head_mask(width, head, True), query, jnp.zeros_like(query)
        )
    m_scr[...] = jnp.full_like(m_scr, -1e30)
    l_scr[...] = jnp.zeros_like(l_scr)
    acc_scr[...] = jnp.zeros_like(acc_scr)

    def scores(e, carry):
        keys = k_ref[pl.ds(e * block, block), :]
        for head in range(heads):
            rows = slice(head * block, (head + 1) * block)
            score = mm(q_scr[rows, :], keys, 1, 1)
            s_scr[e, rows, :] = score
            top = jnp.maximum(score[:, :128], score[:, 128:])
            m_scr[rows, :] = jnp.maximum(m_scr[rows, :], top)
        return carry

    lax.fori_loop(start, stop, scores, 0)
    for head in range(heads):
        rows = slice(head * block, (head + 1) * block)
        m_scr[rows, :] = jnp.broadcast_to(
            jnp.max(m_scr[rows, :], axis=1, keepdims=True), (block, 128)
        )

    def combine(e, carry):
        values = v_ref[pl.ds(e * block, block), :]
        for head in range(heads):
            rows = slice(head * block, (head + 1) * block)
            top = m_scr[rows, :]
            left = jnp.exp(s_scr[e, rows, :128] - top)
            right = jnp.exp(s_scr[e, rows, 128:] - top)
            l_scr[rows, :] = l_scr[rows, :] + (left + right)
            weight = jnp.concatenate([to_low(left), to_low(right)], axis=1)
            acc_scr[rows, :] = acc_scr[rows, :] + mm(weight, values, 1, 0)
        return carry

    lax.fori_loop(start, stop, combine, 0)
    result = jnp.zeros((block, width), f32)
    for head in range(heads):
        rows = slice(head * block, (head + 1) * block)
        total = jnp.sum(l_scr[rows, :], axis=1, keepdims=True)
        lse_ref[rows, :] = m_scr[rows, :] + jnp.log(total)
        result = jnp.where(head_mask(width, head, False), acc_scr[rows, :] / total, result)
    o_ref[...] = to_low(result).reshape(o_ref.shape)


def attend_back_kernel(
    span_ref, q_ref, k_ref, v_ref, o_ref, g_ref, lse_ref, cos_ref, sin_ref, out_ref,
    q_scr, g_scr, d_scr, dq_scr, dk_scr, dv_scr, p_scr, s_scr,
):
    frame = pl.program_id(0)
    width = q_ref.shape[1]
    half = width // 2
    heads = width // HD
    block = PER_FRAME
    start, stop = span_ref[0, frame], span_ref[1, frame]

    @pl.when(frame == 0)
    def clear():
        dk_scr[...] = jnp.zeros_like(dk_scr)
        dv_scr[...] = jnp.zeros_like(dv_scr)

    query = q_ref[...]
    grad = g_ref[...].reshape(block, width)
    product = grad.astype(f32) * o_ref[...].reshape(block, width).astype(f32)
    for head in range(heads):
        rows = slice(head * block, (head + 1) * block)
        q_scr[rows, :] = jnp.where(head_mask(width, head, True), query, jnp.zeros_like(query))
        own = head_mask(width, head, False)
        g_scr[rows, :] = jnp.where(own, grad, jnp.zeros_like(grad))
        inner = jnp.sum(jnp.where(own, product, 0.0), axis=1, keepdims=True)
        d_scr[rows, :] = jnp.broadcast_to(inner, (block, 128))
    dq_scr[...] = jnp.zeros_like(dq_scr)

    def step(e, carry):
        spot = pl.ds(e * block, block)
        keys, values = k_ref[spot, :], v_ref[spot, :]
        for head in range(heads):
            rows = slice(head * block, (head + 1) * block)
            score = mm(q_scr[rows, :], keys, 1, 1)
            grad_w = mm(g_scr[rows, :], values, 1, 1)
            lse, inner = lse_ref[rows, :], d_scr[rows, :]
            for part in range(2):
                lanes = slice(part * 128, (part + 1) * 128)
                weight = jnp.exp(score[:, lanes] - lse)
                p_scr[rows, lanes] = to_low(weight)
                s_scr[rows, lanes] = to_low(weight * (grad_w[:, lanes] - inner))
        dq_scr[...] = dq_scr[...] + mm(s_scr[...], keys, 1, 0)
        dk_scr[spot, :] = dk_scr[spot, :] + mm(s_scr[...], q_scr[...], 0, 0)
        dv_scr[spot, :] = dv_scr[spot, :] + mm(p_scr[...], g_scr[...], 0, 0)
        return carry

    lax.fori_loop(start, stop, step, 0)

    def unrotate(grads, cosine, sine, where, base):
        lower, upper = grads[:, :half], grads[:, half:]
        out_ref[where, base : base + half] = to_low(lower * cosine + upper * sine)
        out_ref[where, base + half : base + width] = to_low(upper * cosine - lower * sine)

    total = jnp.zeros((block, width), f32)
    for head in range(heads):
        rows = slice(head * block, (head + 1) * block)
        total = jnp.where(head_mask(width, head, True), dq_scr[rows, :], total)
    spot = pl.ds(frame * block, block)
    unrotate(total * HD**-0.5, cos_ref[spot, :], sin_ref[spot, :], spot, 0)

    @pl.when(frame == FRAMES - 1)
    def finish():
        def one(e, carry):
            spot = pl.ds(e * block, block)
            unrotate(dk_scr[spot, :], cos_ref[spot, :], sin_ref[spot, :], spot, width)
            out_ref[spot, 2 * width :] = to_low(dv_scr[spot, :])
            return carry

        lax.fori_loop(0, FRAMES, one, 0)


def run_attend_back(span, query, keys, values, out, grad, lse, cosine, sine, after=()):
    block = PER_FRAME
    rows, unused, per_frame, width = out.shape
    heads = width // HD
    parts = (rows, 1, per_frame, width), lambda f: (0, f, 0, 0)
    return run_kernel(
        attend_back_kernel,
        (FRAMES,),
        [
            (query, *frame_rows(width)),
            (keys,),
            (values,),
            (out, *parts),
            (grad, *parts),
            (lse, (heads * block, 128), lambda f: (f, 0)),
            (cosine,),
            (sine,),
        ],
        [((TOK, 3 * width), bf16)],
        [
            pltpu.VMEM((heads * block, width), bf16),
            pltpu.VMEM((heads * block, width), bf16),
            pltpu.VMEM((heads * block, 128), f32),
            pltpu.VMEM((heads * block, width), f32),
            pltpu.VMEM((TOK, width), f32),
            pltpu.VMEM((TOK, width), f32),
            pltpu.VMEM((heads * block, block), bf16),
            pltpu.VMEM((heads * block, block), bf16),
        ],
        span,
        after,
        flops=5 * 2 * 36 * block * block * 256 * heads,
        moved=12 * 2**20,
        exps=36 * block * block * heads,
    )[0]


def run_qkv_dw(attn_in, grad, after=()):
    columns = grad.shape[1]
    count = 2
    block, steps = count * PER_FRAME, FRAMES // count

    def kernel(in_ref, g_ref, out_ref, acc):
        step = pl.program_id(0)
        accumulate(acc, step, lambda: mm(in_ref[...], g_ref[...], 0, 0))

        @pl.when(step == steps - 1)
        def finish():
            out_ref[...] = to_low(acc[...])

    return run_kernel(
        kernel,
        (steps,),
        [
            (attn_in, (block, D), lambda i: (i, 0)),
            (grad, (block, columns), lambda i: (i, 0)),
        ],
        [((D, columns), bf16)],
        [pltpu.VMEM((D, columns), f32)],
        after=after,
        flops=2 * TOK * D * columns,
        moved=10 * 2**20,
    )[0]


def run_qkv_back(noisy, embed, scale, grad, weight, after=()):
    columns = weight.shape[1]

    def kernel(noisy_ref, embed_ref, scale_ref, g_ref, w_ref, sum_ref, ge_ref):
        frame = pl.program_id(0)
        noisy = noisy_ref[...]
        normed, inverse = norm_parts(mm(noisy, embed_ref[...], 1, 0))
        grad_in = mm(g_ref[...], w_ref[...], 1, 1)
        spot = pl.ds(frame, 1)
        sum_ref[spot, :D] = jnp.sum(grad_in, axis=0, keepdims=True)
        sum_ref[spot, D:] = jnp.sum(grad_in * normed, axis=0, keepdims=True)
        grad_h = norm_back(normed, inverse, grad_in * (1.0 + scale_ref[spot, :]))
        accumulate(ge_ref, frame, lambda: mm(noisy, to_low(grad_h), 0, 0))

    return run_kernel(
        kernel,
        (FRAMES,),
        [
            (noisy, *frame_rows(PD)),
            (embed,),
            (scale,),
            (grad, *frame_rows(columns)),
            (weight,),
        ],
        [((FRAMES, 2 * D), f32), ((PD, D), f32)],
        after=after,
        flops=2 * TOK * D * columns,
        moved=8 * 2**20,
    )


REST = {
    name: slice(k * D, (k + 1) * D)
    for k, name in enumerate(("gate_a", "shift_m", "scale_m", "gate_m", "shift_f", "scale_f"))
}


def by_frame(ref, name, first, count, per_frame):
    rows = [
        jnp.broadcast_to(ref[pl.ds(first + k, 1), REST[name]], (per_frame, D))
        for k in range(count)
    ]
    return jnp.concatenate(rows, axis=0)


def store_sums(ref, first, number, values, per_frame):
    for k in range(values.shape[0] // per_frame):
        rows = values[k * per_frame : (k + 1) * per_frame]
        lanes = slice(number * D, (number + 1) * D)
        ref[pl.ds(first + k, 1), lanes] = jnp.sum(rows, axis=0, keepdims=True)


def run_proj(coords, attn, noisy, embed, rest, own, other, after=()):
    rows, tokens, width = attn.shape
    per_frame, steps = tokens // FRAMES, 2
    block, count = tokens // steps, FRAMES // steps

    def kernel(coords_ref, a_ref, n_ref, e_ref, rest_ref, own_ref, other_ref, h_ref, p_ref, in_ref):
        first = pl.program_id(0) * count
        mine = coords_ref[3] == 0
        attn_b = jnp.concatenate([a_ref[r] for r in range(rows)], axis=1)
        one, two = mm(attn_b, own_ref[...], 1, 0), mm(attn_b, other_ref[...], 1, 0)
        out = jnp.concatenate([jnp.where(mine, one, two), jnp.where(mine, two, one)], axis=1)
        p_ref[...] = out
        hidden = mm(n_ref[...], e_ref[...], 1, 0)
        hidden = hidden + by_frame(rest_ref, "gate_a", first, count, per_frame) * out
        h_ref[...] = hidden
        normed, unused = norm_parts(hidden)
        scale = by_frame(rest_ref, "scale_m", first, count, per_frame)
        shift = by_frame(rest_ref, "shift_m", first, count, per_frame)
        in_ref[...] = to_low(normed * (1.0 + scale) + shift)

    part = (block, D), lambda i: (i, 0)
    return run_kernel(
        kernel,
        (steps,),
        [
            (attn, (rows, block, width), lambda i: (0, i, 0)),
            (noisy, (block, PD), lambda i: (i, 0)),
            (embed,),
            (rest,),
            (own,),
            (other,),
        ],
        [((tokens, D), f32, *part), ((tokens, D), f32, *part), ((tokens, D), bf16, *part)],
        scalars=coords,
        after=after,
        flops=2 * tokens * D * D,
        moved=10 * 2**20,
    )


GELU_C = math.sqrt(2.0 / math.pi)
GELU_A = 0.044715


def gelu_value(x):
    return 0.5 * x * (1.0 + jnp.tanh(GELU_C * (x + GELU_A * (x * x * x))))


def gelu_slope(x):
    square = x * x
    t = jnp.tanh(GELU_C * x * (1.0 + GELU_A * square))
    return 0.5 * (1.0 + t) + (0.5 * GELU_C) * x * (1.0 - t * t) * (1.0 + 3.0 * GELU_A * square)


CHUNK = 512


def down_rows(weight):
    return weight, (CHUNK, D), lambda j: (j, 0)


def up_columns(weight):
    return weight, (D, CHUNK), lambda j: (0, j)


def run_up(mlp_in, up, after=()):
    tokens, hidden = mlp_in.shape[0], up.shape[1]

    def kernel(in_ref, up_ref, out_ref, act_ref):
        out = mm(in_ref[...], up_ref[...], 1, 0)
        out_ref[...] = out
        act_ref[...] = to_low(gelu_value(out))

    part = (tokens, CHUNK), lambda j: (0, j)
    return run_kernel(
        kernel,
        (hidden // CHUNK,),
        [(mlp_in,), up_columns(up)],
        [((tokens, hidden), f32, *part), ((tokens, hidden), bf16, *part)],
        after=after,
        flops=2 * tokens * D * hidden,
        moved=10 * 2**20,
    )


def parts_of(tokens):
    size = tokens // 2
    return [slice(k * size, (k + 1) * size) for k in range(2)]


def run_up_down(mlp_in, up, down, dtype, after=()):
    tokens, hidden = mlp_in.shape[0], up.shape[1]
    steps = hidden // CHUNK

    def kernel(in_ref, up_ref, down_ref, out_ref, act_ref, part_ref, acc):
        j = pl.program_id(0)

        @pl.when(j == 0)
        def clear():
            acc[...] = jnp.zeros_like(acc)

        spans = parts_of(tokens)
        ready = mm(in_ref[spans[0], :], up_ref[...], 1, 0)
        for k, span in enumerate(spans):
            out = ready
            if k + 1 < len(spans):
                ready = mm(in_ref[spans[k + 1], :], up_ref[...], 1, 0)
            out_ref[span, :] = out
            act_ref[span, :] = to_low(gelu_value(out))
        acc[...] = acc[...] + mm(act_ref[...], down_ref[...], 1, 0)

        @pl.when(j == steps - 1)
        def finish():
            part_ref[...] = acc[...].astype(part_ref.dtype)

    part = (tokens, CHUNK), lambda j: (0, j)
    return run_kernel(
        kernel,
        (steps,),
        [(mlp_in,), up_columns(up), down_rows(down)],
        [
            ((tokens, hidden), f32, *part),
            ((tokens, hidden), bf16, *part),
            ((tokens, D), dtype),
        ],
        [pltpu.VMEM((tokens, D), f32)],
        after=after,
        flops=4 * tokens * D * hidden,
        moved=16 * 2**20,
    )


def accumulate(acc, step, term):
    @pl.when(step == 0)
    def first():
        acc[...] = jnp.zeros_like(acc)

    acc[...] = acc[...] + term()


def run_down(act, down, after=()):
    tokens, hidden = act.shape

    def kernel(act_ref, down_ref, out_ref):
        accumulate(out_ref, pl.program_id(0), lambda: mm(act_ref[...], down_ref[...], 1, 0))

    return run_kernel(
        kernel,
        (hidden // CHUNK,),
        [(act, (tokens, CHUNK), lambda j: (0, j)), down_rows(down)],
        [((tokens, D), f32)],
        after=after,
        flops=2 * tokens * D * hidden,
        moved=8 * 2**20,
    )[0]


def run_head(flags, hidden1, part, got, rest, head, target, after=()):
    tokens = hidden1.shape[0]
    per_frame, count = tokens // FRAMES, 2
    block = count * per_frame

    def kernel(
        flag_ref, h_ref, p_ref, got_ref, rest_ref, head_ref, t_ref,
        gd_ref, gh_ref, sum_ref, ghead_ref, loss_ref,
    ):
        first = pl.program_id(0) * count

        @pl.when(first == 0)
        def clear():
            ghead_ref[...] = jnp.zeros_like(ghead_ref)

        mod = lambda name: by_frame(rest_ref, name, first, count, per_frame)
        frame_of = lax.broadcasted_iota(jnp.int32, (block, 1), 0) // per_frame
        true = jnp.where(frame_of == 0, flag_ref[first], flag_ref[first + 1])
        down_out = p_ref[...] + got_ref[...].astype(f32)
        hidden = h_ref[...] + mod("gate_m") * down_out
        normed, inverse = norm_parts(hidden)
        scale = 1.0 + mod("scale_f")
        final_in = to_low(normed * scale + mod("shift_f"))
        pred = mm(final_in, head_ref[...], 1, 0)
        error = (pred - t_ref[...]) * true
        loss_ref[pl.ds(pl.program_id(0), 1), :] = jnp.broadcast_to(
            jnp.sum(jnp.sum(error * error, axis=1, keepdims=True), axis=0, keepdims=True), (1, 128)
        )
        grad_pred = to_low(2.0 * error / flag_ref[FRAMES])
        ghead_ref[...] = ghead_ref[...] + mm(final_in, grad_pred, 0, 0)
        grad_fin = mm(grad_pred, head_ref[...], 1, 1)
        store_sums(sum_ref, first, 1, grad_fin, per_frame)
        store_sums(sum_ref, first, 2, grad_fin * normed, per_frame)
        grad = norm_back(normed, inverse, grad_fin * scale)
        gh_ref[...] = grad
        store_sums(sum_ref, first, 0, grad * down_out, per_frame)
        gd_ref[...] = to_low(grad * mod("gate_m"))

    part_spec = (block, D), lambda f: (f, 0)
    return run_kernel(
        kernel,
        (FRAMES // count,),
        [
            (flags, pltpu.SMEM),
            (hidden1, *part_spec),
            (part, *part_spec),
            (got, *part_spec),
            (rest,),
            (head,),
            (target, (block, PD), lambda f: (f, 0)),
        ],
        [
            ((tokens, D), bf16, *part_spec),
            ((tokens, D), f32, *part_spec),
            ((FRAMES, 3 * D), f32),
            ((D, PD), f32),
            ((FRAMES // count, 128), f32),
        ],
        after=after,
        flops=8 * tokens * D * PD,
        moved=10 * 2**20,
    )


def run_act_back(grad, down, up_out, after=()):
    tokens, hidden = up_out.shape

    def kernel(g_ref, down_ref, up_ref, out_ref):
        grad_act = mm(g_ref[...], down_ref[...], 1, 1)
        out_ref[...] = to_low(grad_act * gelu_slope(up_ref[...]))

    part = (tokens, CHUNK), lambda j: (0, j)
    return run_kernel(
        kernel,
        (hidden // CHUNK,),
        [(grad,), down_rows(down), (up_out, *part)],
        [((tokens, hidden), bf16, *part)],
        after=after,
        flops=2 * tokens * D * hidden,
        moved=10 * 2**20,
    )[0]


def run_act_up_back(grad, down, up_out, up, dtype, after=()):
    tokens, hidden = up_out.shape
    steps = hidden // CHUNK

    def kernel(g_ref, down_ref, o_ref, up_ref, out_ref, part_ref, acc):
        j = pl.program_id(0)

        @pl.when(j == 0)
        def clear():
            acc[...] = jnp.zeros_like(acc)

        spans = parts_of(tokens)
        ready = mm(g_ref[spans[0], :], down_ref[...], 1, 1)
        for k, span in enumerate(spans):
            grad_act = ready
            if k + 1 < len(spans):
                ready = mm(g_ref[spans[k + 1], :], down_ref[...], 1, 1)
            out_ref[span, :] = to_low(grad_act * gelu_slope(o_ref[span, :]))
        acc[...] = acc[...] + mm(out_ref[...], up_ref[...], 1, 1)

        @pl.when(j == steps - 1)
        def finish():
            part_ref[...] = acc[...].astype(part_ref.dtype)

    part = (tokens, CHUNK), lambda j: (0, j)
    return run_kernel(
        kernel,
        (steps,),
        [(grad,), down_rows(down), (up_out, *part), up_columns(up)],
        [((tokens, hidden), bf16, *part), ((tokens, D), dtype)],
        [pltpu.VMEM((tokens, D), f32)],
        after=after,
        flops=4 * tokens * D * hidden,
        moved=16 * 2**20,
    )


def run_up_back(grad, up, after=()):
    tokens, hidden = grad.shape

    def kernel(g_ref, up_ref, out_ref):
        accumulate(out_ref, pl.program_id(0), lambda: mm(g_ref[...], up_ref[...], 1, 1))

    return run_kernel(
        kernel,
        (hidden // CHUNK,),
        [(grad, (tokens, CHUNK), lambda j: (0, j)), up_columns(up)],
        [((tokens, D), f32)],
        after=after,
        flops=2 * tokens * D * hidden,
        moved=8 * 2**20,
    )[0]


def group_list(sizes):
    ny, nx, nz = sizes
    return [(my, mx) for my in range(ny) for mx in range(nx)]


def run_down_dw(coords, sizes, acts, grads, after=()):
    groups, nz = group_list(sizes), sizes[2]
    hidden = acts[0].shape[1]
    rows = hidden // (len(groups) * nz)
    steps = hidden // CHUNK

    def kernel(coords_ref, a_ref, b_ref, ga_ref, gb_ref, *refs):
        outs, acc = refs[: len(groups)], refs[len(groups)]
        j = pl.program_id(0)
        acc[j] = mm(a_ref[...], ga_ref[...], 0, 0) + mm(b_ref[...], gb_ref[...], 0, 0)

        @pl.when(j == steps - 1)
        def finish():
            for out, (my, mx) in zip(outs, groups):
                for mz in range(nz):
                    first = chip_number(coords_ref, my, mx, mz) * rows
                    spot = pl.ds(pl.multiple_of(first % CHUNK, rows), rows)
                    out[mz] = to_low(acc[first // CHUNK, spot, :])

    part = (acts[0].shape[0], CHUNK), lambda j: (0, j)
    outs = run_kernel(
        kernel,
        (steps,),
        [(acts[0], *part), (acts[1], *part), (grads[0],), (grads[1],)],
        [((nz, rows, D), bf16)] * len(groups),
        [pltpu.VMEM((steps, CHUNK, D), f32)],
        coords,
        after,
        flops=4 * acts[0].shape[0] * D * hidden,
        moved=10 * 2**20,
    )
    return dict(zip(groups, outs))


def run_act_up_dw(coords, sizes, ins, grad_up, grad, down, up_out, up, after=()):
    groups, nz = group_list(sizes), sizes[2]
    rows = D // (len(groups) * nz)
    tokens, hidden = up_out.shape
    steps = hidden // CHUNK

    def kernel(coords_ref, a_ref, b_ref, ga_ref, g_ref, down_ref, o_ref, up_ref, part_ref, *refs):
        outs, (acc, part_acc, gb_scr) = refs[: len(groups)], refs[len(groups) :]
        j = pl.program_id(0)

        @pl.when(j == 0)
        def clear():
            part_acc[...] = jnp.zeros_like(part_acc)

        spans = parts_of(tokens)
        ready = mm(g_ref[spans[0], :], down_ref[...], 1, 1)
        for k, span in enumerate(spans):
            grad_act = ready
            if k + 1 < len(spans):
                ready = mm(g_ref[spans[k + 1], :], down_ref[...], 1, 1)
            gb_scr[span, :] = to_low(grad_act * gelu_slope(o_ref[span, :]))
        acc[...] = mm(a_ref[...], ga_ref[...], 0, 0) + mm(b_ref[...], gb_scr[...], 0, 0)
        part_acc[...] = part_acc[...] + mm(gb_scr[...], up_ref[...], 1, 1)
        for out, (my, mx) in zip(outs, groups):
            for mz in range(nz):
                first = chip_number(coords_ref, my, mx, mz) * rows
                out[mz] = to_low(acc[pl.ds(pl.multiple_of(first, rows), rows), :])

        @pl.when(j == steps - 1)
        def finish():
            part_ref[...] = to_low(part_acc[...])

    part = (tokens, CHUNK), lambda j: (0, j)
    outs = run_kernel(
        kernel,
        (steps,),
        [
            (ins[0],),
            (ins[1],),
            (grad_up, *part),
            (grad,),
            down_rows(down),
            (up_out, *part),
            up_columns(up),
        ],
        [((tokens, D), bf16)]
        + [((nz, rows, hidden), bf16, (nz, rows, CHUNK), lambda j: (0, 0, j))] * len(groups),
        [
            pltpu.VMEM((D, CHUNK), f32),
            pltpu.VMEM((tokens, D), f32),
            pltpu.VMEM((tokens, CHUNK), bf16),
        ],
        coords,
        after,
        flops=8 * tokens * D * hidden,
        moved=26 * 2**20,
    )
    return outs[0], dict(zip(groups, outs[1:]))


def run_add_pieces(coords, sizes, terms, after=()):
    groups, nz = group_list(sizes), sizes[2]
    rows, columns = terms[0].shape[0] // (len(groups) * nz), terms[0].shape[1]

    def kernel(coords_ref, a_ref, b_ref, *refs):
        outs, acc = refs[: len(groups)], refs[len(groups)]
        acc[...] = a_ref[...].astype(f32) + b_ref[...].astype(f32)
        for out, (my, mx) in zip(outs, groups):
            for mz in range(nz):
                first = chip_number(coords_ref, my, mx, mz) * rows
                out[mz] = to_low(acc[pl.ds(pl.multiple_of(first, rows), rows), :])

    outs = run_kernel(
        kernel,
        (1,),
        [(terms[0],), (terms[1],)],
        [((nz, rows, columns), bf16)] * len(groups),
        [pltpu.VMEM(terms[0].shape, f32)],
        coords,
        after,
        moved=6 * terms[0].size,
    )
    return dict(zip(groups, outs))


def run_proj_back(coords, grad_h2, part, got, hidden1, proj_out, rest, own, other, attn, noisy, after=()):
    rows, tokens, width = attn.shape
    per_frame, steps = tokens // FRAMES, 2
    block, count = tokens // steps, FRAMES // steps

    def kernel(
        coords_ref, g_ref, p_ref, got_ref, h_ref, po_ref, rest_ref, own_ref, other_ref, a_ref, n_ref,
        ga_ref, mine_ref, theirs_ref, sum_ref, ge_ref, acc,
    ):
        step = pl.program_id(0)
        first = step * count
        mine = coords_ref[3] == 0
        grad_mlp = p_ref[...] + got_ref[...].astype(f32)
        normed, inverse = norm_parts(h_ref[...])
        store_sums(sum_ref, first, 1, grad_mlp, per_frame)
        store_sums(sum_ref, first, 2, grad_mlp * normed, per_frame)
        scale = by_frame(rest_ref, "scale_m", first, count, per_frame)
        grad = g_ref[...] + norm_back(normed, inverse, grad_mlp * (1.0 + scale))
        store_sums(sum_ref, first, 0, grad * po_ref[...], per_frame)
        low = to_low(grad * by_frame(rest_ref, "gate_a", first, count, per_frame))
        lower, upper = low[:, : D // 2], low[:, D // 2 :]
        grad_attn = mm(jnp.where(mine, lower, upper), own_ref[...], 1, 1)
        grad_attn = grad_attn + mm(jnp.where(mine, upper, lower), other_ref[...], 1, 1)
        grad_attn = to_low(grad_attn)
        attn_b = jnp.concatenate([a_ref[r] for r in range(rows)], axis=1)
        for r in range(rows):
            ga_ref[r] = grad_attn[:, r * width : (r + 1) * width]
        accumulate(acc, step, lambda: mm(attn_b, low, 0, 0))
        accumulate(ge_ref, step, lambda: mm(n_ref[...], to_low(grad), 0, 0))

        @pl.when(step == steps - 1)
        def finish():
            lower, upper = to_low(acc[:, : D // 2]), to_low(acc[:, D // 2 :])
            mine_ref[...] = jnp.where(mine, lower, upper)
            theirs_ref[...] = jnp.where(mine, upper, lower)

    piece = (block, D), lambda i: (i, 0)
    wide = (rows, block, width), lambda i: (0, i, 0)
    return run_kernel(
        kernel,
        (steps,),
        [
            (grad_h2, *piece),
            (part, *piece),
            (got, *piece),
            (hidden1, *piece),
            (proj_out, *piece),
            (rest,),
            (own,),
            (other,),
            (attn, *wide),
            (noisy, (block, PD), lambda i: (i, 0)),
        ],
        [
            ((rows, tokens, width), bf16, *wide),
            ((D, D // 2), bf16),
            ((D, D // 2), bf16),
            ((FRAMES, 3 * D), f32),
            ((PD, D), f32),
        ],
        [pltpu.VMEM((D, D), f32)],
        coords,
        after,
        flops=4 * tokens * D * D,
        moved=18 * 2**20,
    )


def run_lamb(entries, slots, fixes, after=()):
    def kernel(*refs):
        many = len(entries)
        ins, outs = refs[: 4 * many], refs[4 * many : 6 * many]
        sums = refs[6 * many]
        lane = lax.broadcasted_iota(jnp.int32, (1, 128), 1)
        row = jnp.zeros((1, 128), f32)
        for k, slot in enumerate(slots):
            weight, grad, first, second = (ref[...] for ref in ins[4 * k : 4 * k + 4])
            mom_ref, update_ref = outs[2 * k : 2 * k + 2]
            first_n, second_n, update = lamb_direction(weight, grad, first, second, *fixes)
            mom_ref[0] = first_n
            mom_ref[1] = second_n
            update_ref[...] = update
            for value, place in ((weight, 2 * slot), (update, 2 * slot + 1)):
                total = jnp.sum(value * value, axis=0, keepdims=True)
                total = jnp.sum(total, axis=1, keepdims=True)
                row = row + jnp.where(lane == place, total, 0.0)
        sums[...] = row

    outputs = []
    for weight, *unused in entries:
        outputs += [((2,) + weight.shape, f32), (weight.shape, f32)]
    moved = 28 * sum(entry[0].size for entry in entries)
    flat = [(array,) for entry in entries for array in entry]
    outs = run_kernel(kernel, (1,), flat, outputs + [((1, 128), f32)], after=after, moved=moved)
    return outs[0:-1:2], outs[1:-1:2], outs[-1]


def run_update(weights, updates, totals):
    def kernel(totals_ref, *refs):
        many = len(weights)
        lane = lax.broadcasted_iota(jnp.int32, (1, 128), 1)
        norms = jnp.sqrt(jnp.sum(totals_ref[...], axis=0, keepdims=True))
        for k in range(many):
            weight_ref, update_ref, out_ref = refs[k], refs[many + k], refs[2 * many + k]
            pick = lambda at: jnp.sum(jnp.where(lane == at, norms, 0.0), axis=1, keepdims=True)
            trust = learn_rate * (pick(2 * k) / pick(2 * k + 1))
            out_ref[...] = weight_ref[...] - trust * update_ref[...]

    return run_kernel(
        kernel,
        (1,),
        [(totals,)] + [(array,) for array in list(weights) + list(updates)],
        [(weight.shape, f32) for weight in weights],
        moved=12 * sum(weight.size for weight in weights),
    )


def lamb_direction(weight, gradient, first_m, second_m, fix_one, fix_two):
    first_n = beta_one * first_m + (1.0 - beta_one) * gradient
    second_n = jnp.sqrt(beta_two * second_m * second_m + (1.0 - beta_two) * gradient * gradient)
    update = first_n / fix_one / (second_n / math.sqrt(fix_two) + adam_eps) + weight_decay * weight
    return (first_n, second_n, update)


def body(
    latents, noise, levels, clip_ids, clip_lens,
    embed_w, table_w, adaln_w, qkv_w, proj_w, up_w, down_w, head_w,
    embed_avg, table_avg, adaln_avg, qkv_avg, proj_avg, up_avg, down_avg, head_avg,
    embed_sq, table_sq, adaln_sq, qkv_sq, proj_sq, up_sq, down_sq, head_sq,
):
    masters = (embed_w, table_w, adaln_w, qkv_w, proj_w, up_w, down_w, head_w)
    firsts = (embed_avg, table_avg, adaln_avg, qkv_avg, proj_avg, up_avg, down_avg, head_avg)
    seconds = (embed_sq, table_sq, adaln_sq, qkv_sq, proj_sq, up_sq, down_sq, head_sq)
    clips, rows = lax.axis_size("clip"), lax.axis_size("row")
    count_dev = clips * rows
    sizes, unused_bits = shape_of_mesh()
    ny, nx, nz = sizes
    clip_index, row_index = lax.axis_index("clip"), lax.axis_index("row")
    core = row_index % 2
    coords = jnp.stack(
        [
            row_index // 2,
            clip_index % nx,
            clip_index // nx,
            core,
            jnp.full_like(core, ny),
            jnp.full_like(core, nx),
        ]
    ).astype(jnp.int32)
    part = D // count_dev
    width = D // rows
    row_local = GRID // rows
    per_frame = row_local * GRID
    count_tok = FRAMES * per_frame
    hidden = FF // 2
    unit = FF // count_dev
    level_row = levels[0]
    frame_pos, is_true, starts, stops = frame_layout(clip_ids[0], clip_lens[0])
    span = jnp.stack([starts, stops]).astype(jnp.int32)

    own_count = jnp.sum(is_true.astype(f32))
    packed = jnp.concatenate(
        [
            level_row.astype(f32),
            jnp.broadcast_to(own_count, (8,)),
            embed_w.reshape(-1),
            head_w.reshape(-1),
        ]
    )
    everyone = spread(packed.reshape(1, -1), BOTH).reshape(count_dev, -1)
    all_levels = everyone[::rows, :FRAMES].astype(jnp.int32).reshape(-1)
    count = jnp.sum(everyone[::rows, FRAMES]) * PER_FRAME
    embed_b = to_low(everyone[:, 16 : 16 + PD * part].reshape(count_dev, PD, part))
    embed_b = embed_b.transpose(1, 0, 2).reshape(PD, D)
    head_b = to_low(everyone[:, 16 + PD * part :]).reshape(D, PD)

    one_hot = (all_levels[:, None] == jnp.arange(LEVELS, dtype=jnp.int32)[None, :]).astype(f32)
    cond = dot_low("fl,ld->fd", to_low(one_hot), to_low(table_w))
    cond_act = to_low(jax.nn.silu(cond))
    adaln_low = to_low(adaln_w)

    def mod_terms(lower, upper):
        wide = (upper - lower) * D // rows
        terms = to_low(dot_low("fd,dm->fm", cond_act, adaln_low[:, lower * D : upper * D]))
        terms = terms.reshape(clips, FRAMES, rows, wide).transpose(0, 2, 1, 3)
        return terms.reshape(count_dev, FRAMES, wide)

    def modulation(terms):
        total = row_gather(jnp.sum(terms.astype(f32), axis=0))
        return total.transpose(1, 0, 2).reshape(FRAMES, -1)

    first_terms = lax.all_to_all(mod_terms(0, 2), BOTH, 0, 0, tiled=True)
    first = modulation(first_terms)
    shift_a, scale_a = first[:, :D], first[:, D:]

    alpha, sigma = noise_mix(level_row)
    clean = latents[0].reshape(FRAMES, per_frame, PD)
    fresh = noise[0].reshape(FRAMES, per_frame, PD)
    noisy = alpha[:, None, None] * clean + sigma[:, None, None] * fresh
    target = (alpha[:, None, None] * fresh - sigma[:, None, None] * clean).reshape(count_tok, PD)
    noisy_own = to_low(noisy).reshape(count_tok, PD)
    perm = rotary_permutation(width)
    qkv_low = to_low(qkv_w).reshape(part, 3, rows, width)
    turned = to_low(dot_low("dgrw,wv->rdgv", qkv_low[:, :2], perm))
    mine = jnp.concatenate([turned, qkv_low[:, 2:].transpose(2, 0, 1, 3)], axis=2)
    mine = mine.reshape(rows, part, 3 * width)
    token_cols = count_tok * PD // part
    tokens = jnp.broadcast_to(noisy_own.reshape(1, part, token_cols), (rows, part, token_cols))
    mine = row_swap(jnp.concatenate([mine, tokens], axis=2))
    noisy_all = mine[:, :, 3 * width :].reshape(rows, FRAMES, per_frame, PD)
    noisy_all = noisy_all.transpose(1, 0, 2, 3).reshape(TOK, PD)
    def halves(weight, blocks):
        parts = weight.reshape(weight.shape[0], -1, 2, weight.shape[1] // (2 * blocks))
        mine = lax.dynamic_index_in_dim(parts, core, 2, keepdims=False)
        theirs = lax.dynamic_index_in_dim(parts, 1 - core, 2, keepdims=False)
        return mine.reshape(weight.shape[0], -1), theirs.reshape(weight.shape[0], -1)

    up_mine, up_theirs = halves(to_low(up_w), count_dev // 2)
    proj_mine, proj_theirs = halves(to_low(proj_w), 1)
    tall_mine = jnp.concatenate([up_mine, proj_mine], axis=1)
    tall_got = exchange(jnp.concatenate([up_theirs, proj_theirs], axis=1), 1)
    is_zero = core == 0
    tall = jnp.concatenate(
        [jnp.where(is_zero, tall_mine, tall_got), jnp.where(is_zero, tall_got, tall_mine)]
    )
    gather_down = Gather(to_low(down_w))
    gather_down.go_z()
    gather_down.go_xy()
    gather_down.go_slant()
    mine = tie(mine[:, :, : 3 * width], gather_down.own)
    gather_qkv = Gather(mine.reshape(rows * part, 3 * width), False)
    gather_qkv.go_z(first_terms)
    gather_qkv.go_xy()
    gather_qkv.go_slant()
    gather_tall = Gather(tie(tall, gather_qkv.own, *gather_down.came_xy()))
    gather_tall.go_z()
    gather_tall.go_direct()
    rest_sent = mod_terms(2, 8)

    cosine, sine = group_angles(frame_pos, width // 2)
    flags = jnp.concatenate([is_true.astype(f32), (PD * count).reshape(1)])
    rest_terms = lax.all_to_all(rest_sent, BOTH, 0, 0, tiled=True)
    query, keys, values, attn_in, qkv_b, attn_heads, lse = run_qkv_attend(
        coords, span, noisy_all, embed_b, shift_a, scale_a, cosine, sine, gather_qkv.pieces(),
        rows, after=(gather_tall.own, rest_sent, flags, head_b) + tuple(piece[0] for piece in gather_down.slant),
    )
    rest_terms = tie(rest_terms, query)
    rest = modulation(rest_terms)

    def swap_row(wide):
        return lax.all_to_all(wide, "row", 0, 0, tiled=True)

    attn = tie(attn_heads, rest_terms).reshape(rows, count_tok, width)
    attn = swap_row(attn)
    down_b = run_place(coords, gather_down.pieces(), (D,), after=(attn_heads,))[0]
    up_b, proj_own = run_place(
        coords, gather_tall.pieces(), (hidden, D // 2), after=(down_b,)
    )
    proj_other = exchange(proj_own, 1)
    hidden1, proj_out, mlp_in = run_proj(
        coords, attn, noisy_own, embed_b, rest, proj_own, proj_other
    )
    mlp_in_other = exchange(mlp_in, 1)
    up_out_other, act_other, part_other = run_up_down(mlp_in_other, up_b, down_b, bf16)
    part_got = exchange(part_other, 1)
    up_out, act, part_own = run_up_down(mlp_in, up_b, down_b, f32, after=(part_other,))
    grad_down_out, grad_h2, sums_f, grad_head, losses = run_head(
        flags, hidden1, part_own, part_got, rest, head_b, target
    )
    loss_local = jnp.sum(losses[:, 0])

    grad_down_other = exchange(grad_down_out, 1)
    down_groups = run_down_dw(
        coords, sizes, (act, act_other), (grad_down_out, grad_down_other)
    )
    scatter_down = Scatter(down_groups)
    grad_up, mlp_own = run_act_up_back(
        grad_down_out, down_b, up_out, up_b, f32, after=(down_groups[0, 0],)
    )
    mlp_other, up_groups = run_act_up_dw(
        coords, sizes, (mlp_in, mlp_in_other), grad_up, grad_down_other, down_b,
        up_out_other, up_b, after=tuple(scatter_down.sent.values()),
    )
    mlp_got = exchange(mlp_other, 1)
    scatter_down.go_xy()
    scatter_down.take_xy(up_groups[0, 0])
    scatter_down.go_z()
    grad_attn, proj_mine, proj_theirs, sums_m, embed_h1 = run_proj_back(
        coords, grad_h2, mlp_own, mlp_got, hidden1, proj_out, rest,
        proj_own, proj_other, attn, noisy_own, after=(scatter_down.own,),
    )
    grad_attn = swap_row(grad_attn).reshape(rows, FRAMES, per_frame, width)
    scatter_up = Scatter(up_groups, proj_mine)
    proj_groups = run_add_pieces(coords, sizes, (proj_mine, exchange(proj_theirs, 1)))
    scatter_up.go_xy(proj_groups, grad_attn)

    def mod_row(values_mod, *hold):
        wide = values_mod.shape[1] // rows
        total = to_low(row_sum(values_mod, *hold))
        return lax.dynamic_slice_in_dim(total, row_index * wide, wide, axis=1)

    def mod_all(total):
        wide = total.shape[-1]
        total = total.reshape(clips, rows, FRAMES, wide)
        return total.transpose(0, 2, 1, 3).reshape(clips * FRAMES, rows * wide)

    mod_rest = spread(mod_row(jnp.concatenate([sums_m, sums_f], axis=1)), BOTH)
    grad_qkv = run_attend_back(
        span, query, keys, values, attn_heads, grad_attn, lse, cosine, sine,
        after=(proj_groups[0, 0],) + tuple(scatter_up.sent.values()),
    )
    scatter_up.take_xy(grad_qkv)
    grad_qkv_w = run_qkv_dw(
        attn_in, grad_qkv, after=(scatter_up.own, mod_rest, *scatter_down.came_z)
    )
    qkv_terms = grad_qkv_w.reshape(count_dev, part, 3 * width)
    qkv_terms = lax.all_to_all(qkv_terms, BOTH, 0, 0, tiled=True)
    scatter_up.go_z(qkv_terms)
    sums_a, grad_embed = run_qkv_back(
        noisy_all, embed_b, scale_a, grad_qkv, qkv_b,
        after=(grad_qkv_w,),
    )
    down_sum = scatter_down.result(sums_a)
    grad_embed = grad_embed + embed_h1

    small = jnp.concatenate(
        [
            grad_embed.reshape(PD, count_dev, part).transpose(1, 0, 2).reshape(count_dev, -1),
            grad_head.reshape(count_dev, -1),
        ],
        axis=1,
    )
    small = to_low(small).reshape(count_dev, 1, -1)
    mod_first = mod_row(sums_a)
    wide = mod_first.shape[-1]
    lines = max(small.shape[-1] // wide, 1)
    small = jnp.pad(small, ((0, 0), (0, 0), (0, lines * wide - small.shape[-1])))
    last = jnp.concatenate(
        [
            jnp.broadcast_to(mod_first[None], (count_dev, FRAMES, wide)),
            small.reshape(count_dev, lines, wide),
        ],
        axis=1,
    )
    last = lax.all_to_all(tie(last, qkv_terms), BOTH, 0, 0, tiled=True)
    small = jnp.sum(last[:, FRAMES:].astype(f32), axis=0).reshape(-1)
    embed_sum = small[: PD * part].reshape(PD, part)
    head_sum = small[PD * part : 2 * PD * part].reshape(part, PD)
    qkv_sum = tie(qkv_terms, last).reshape(clips, rows, part, 3 * width).astype(f32)
    qkv_sum = to_low(jnp.sum(qkv_sum, axis=0)).reshape(rows, part, 3, width)
    turned = dot_low("rdgv,wv->dgrw", qkv_sum[:, :, :2], perm)
    straight = qkv_sum[:, :, 2:].transpose(1, 2, 0, 3).astype(f32)
    qkv_sum = jnp.concatenate([turned, straight], axis=1).reshape(part, 3 * D)

    grad_mod_b = jnp.concatenate([mod_all(last[:, :FRAMES]), mod_all(mod_rest)], axis=1)
    grad_adaln = dot_low("fd,fm->dm", cond_act, grad_mod_b)
    grad_cond_act = dot_low("fm,dm->fd", grad_mod_b, adaln_low)
    unused_silu, silu_pull = jax.vjp(jax.nn.silu, cond)
    grad_cond = silu_pull(grad_cond_act)[0]
    grad_table = jnp.einsum(
        "fl,fd->dl", one_hot, grad_cond, precision=precise, preferred_element_type=f32
    )

    fixes = (1.0 - beta_one**STEP, 1.0 - beta_two**STEP)
    reduced = [
        embed_sum, grad_table, grad_adaln, qkv_sum, None, None, down_sum, head_sum.T,
    ]
    turned = (1, 7)
    flip = lambda k, array: jnp.swapaxes(array, -1, -2) if k in turned else array
    weights = [flip(k, array) for k, array in enumerate(masters)]
    moms, updates, rows_of_sums = [None] * 8, [None] * 8, []
    for group in ((6,), (3,), (0, 1, 2, 7), (4, 5)):
        if group == (4, 5):
            tall_sum = scatter_up.result(rows_of_sums[-1])

            keep = lax.dynamic_slice_in_dim(tall_sum, core * part, part)
            got = exchange(to_low(lax.dynamic_slice_in_dim(tall_sum, (1 - core) * part, part)), 1)
            got = got.astype(f32)
            pair_sum = jnp.stack([jnp.where(is_zero, keep, got), jnp.where(is_zero, got, keep)], axis=1)
            up_sum = pair_sum[:, :, :hidden].reshape(part, 2, count_dev // 2, unit)
            up_sum = up_sum.transpose(0, 2, 1, 3).reshape(part, FF)
            proj_sum = pair_sum[:, :, hidden:].reshape(part, D)
            reduced[4], reduced[5] = proj_sum, up_sum
        entries = [
            (weights[k], reduced[k], flip(k, firsts[k]), flip(k, seconds[k])) for k in group
        ]
        got_moms, got_updates, sums = run_lamb(entries, group, fixes)
        rows_of_sums.append(sums)
        for k, mom, update in zip(group, got_moms, got_updates):
            moms[k], updates[k] = flip(k, mom), update
    lane = jnp.arange(128, dtype=jnp.int32)[None, :]
    sums = sum(rows_of_sums) + jnp.where(lane == 16, loss_local, 0.0)
    totals = spread(sums, BOTH).reshape(count_dev, 128)
    news = run_update(weights, updates, totals)
    news = [flip(k, array) for k, array in enumerate(news)]
    totals = jnp.sum(totals, axis=0)
    norms = jnp.sqrt(totals[:16].reshape(8, 2))
    return (*news, *moms, norms, totals[16:17] / (PD * count))


def solution(mesh):
    wide, tall = P(None, BOTH), P(BOTH, None)
    weights = (wide, wide, tall, tall, tall, tall, tall, tall)
    moments = (P(None, None, BOTH),) * 2 + (P(None, BOTH, None),) * 6
    return jax.shard_map(
        body,
        mesh=mesh,
        in_specs=(
            P("clip", None, "row", None),
            P("clip", None, "row", None),
            P("clip", None),
            P("clip", None),
            P("clip", None),
        )
        + weights * 3,
        out_specs=weights + moments + (P(), P()),
        check_vma=False,
    )
```

```python
import functools
import math

import jax
import jax.numpy as jnp
from jax import lax
from jax.experimental import pallas as pl
from jax.experimental.pallas import tpu as pltpu
from jax.sharding import PartitionSpec as P

D = 1024
HEADS = 16
HD = 64
FF = 4096
PD = 16
GRID = 16
LEVELS = 1000
STEP = 7
FRAMES = 8
CLIPS = 2
PER_FRAME = GRID * GRID
TOK = FRAMES * PER_FRAME
BOTH = ("clip", "row")
VMEM_BYTES = 56 * 1024 * 1024

precise = lax.Precision.HIGHEST
beta_one = 0.9
beta_two = 0.999
adam_eps = 1e-08
weight_decay = 0.01
learn_rate = 1.0
norm_eps = 1e-06
f32 = jnp.float32
bf16 = jnp.bfloat16


def to_low(values):
    return values.astype(bf16)


def dot_low(formula, left, right):
    return jnp.einsum(formula, left, right, preferred_element_type=f32)


def mm(left, right, left_dim, right_dim):
    return lax.dot_general(
        left, right, (((left_dim,), (right_dim,)), ((), ())), preferred_element_type=f32
    )


def layer_norm(values):
    center = values - jnp.mean(values, axis=-1, keepdims=True)
    spread = jnp.mean(center * center, axis=-1, keepdims=True)
    return center * lax.rsqrt(spread + norm_eps)


def norm_parts(values):
    center = values - jnp.mean(values, axis=-1, keepdims=True)
    spread = jnp.mean(center * center, axis=-1, keepdims=True)
    inverse = lax.rsqrt(spread + norm_eps)
    return center * inverse, inverse


def norm_back(normed, inverse, grad):
    mean_g = jnp.mean(grad, axis=-1, keepdims=True)
    mean_gn = jnp.mean(grad * normed, axis=-1, keepdims=True)
    return inverse * (grad - mean_g - normed * mean_gn)


def modulate(normed, shift, scale):
    return normed * (1.0 + scale[:, None, :]) + shift[:, None, :]


def gelu_tanh(values):
    return jax.nn.gelu(values, approximate=True)


def frame_layout(clip_row, length_row):
    frame_idx = jnp.arange(FRAMES, dtype=jnp.int32)
    same_clip = clip_row[:, None] == clip_row[None, :]
    starts = jnp.min(jnp.where(same_clip, frame_idx[None, :], FRAMES), axis=1)
    frame_pos = frame_idx - starts
    slot_idx = jnp.arange(CLIPS, dtype=jnp.int32)
    length = jnp.sum(
        jnp.where(clip_row[:, None] == slot_idx[None, :], length_row[None, :], 0), axis=1
    )
    is_true = frame_pos < length
    stops = jnp.minimum(frame_idx + 1, starts + length)
    return (frame_pos, is_true, starts, stops)


def noise_mix(level_row):
    angle = (level_row.astype(f32) + 0.5) * (math.pi / (2 * LEVELS))
    return (jnp.cos(angle), jnp.sin(angle))


def group_angles(frame_pos, lanes):
    place = jnp.arange(GRID, dtype=jnp.int32)
    j = jnp.arange(lanes, dtype=jnp.int32) % (HD // 2)
    edges = (0, HD // 8, HD // 8 + 3 * HD // 16, HD // 2)
    tables, masks = [], []
    for k, along in enumerate((frame_pos, place, place)):
        size = edges[k + 1] - edges[k]
        frequency = 10000.0 ** (-(j - edges[k]).astype(f32) / size)
        masks.append((j >= edges[k]) & (j < edges[k + 1]))
        frequency = jnp.where(masks[k], frequency, 0.0)
        tables.append(along.astype(f32)[:, None] * frequency[None, :])
    shape = (FRAMES, GRID, GRID, lanes)
    result = []
    for fn in (jnp.cos, jnp.sin):
        at_f = fn(tables[0])[:, None, None, :]
        at_r = fn(tables[1])[None, :, None, :]
        at_c = fn(tables[2])[None, None, :, :]
        value = jnp.where(masks[0], at_f, jnp.where(masks[1], at_r, at_c))
        result.append(jnp.broadcast_to(value, shape).reshape(TOK, lanes))
    return result


def rotary_order(width):
    order = []
    heads = width // HD
    for half in range(2):
        for head in range(heads):
            offset = 0
            for part in (HD // 4, 3 * HD // 8, 3 * HD // 8):
                start = head * HD + offset + half * (part // 2)
                order.extend(range(start, start + part // 2))
                offset += part
    return order


def rotary_permutation(width):
    order = jnp.array(rotary_order(width), dtype=jnp.int32)
    return (jnp.arange(width, dtype=jnp.int32)[:, None] == order[None, :]).astype(bf16)


def shape_of_mesh():
    clips, rows = lax.axis_size("clip"), lax.axis_size("row")
    ny, nz = rows // 2, 4
    nx = clips // nz
    bits = [count.bit_length() - 1 for count in (rows, rows * nx)]
    return (ny, nx, nz), (1, bits[0], bits[1])


def exchange(values, mask):
    count = lax.axis_size("clip") * lax.axis_size("row")
    return lax.ppermute(values, BOTH, [(i, i ^ mask) for i in range(count)])


def along(number):
    sizes, bits = shape_of_mesh()
    return {m: m << bits[number] for m in range(1, sizes[number])}


class Gather:
    def __init__(self, shard, use_y=True):
        self.shard = shard
        self.z_masks, self.x_masks = along(2), along(1)
        self.y_masks = along(0) if use_y else {}

    def go_z(self, *hold):
        came = [exchange(self.shard, mask) for mask in self.z_masks.values()]
        self.own = jnp.stack([self.shard] + came)
        if hold:
            self.own = tie(self.own, *hold)

    def go_direct(self):
        self.go_xy()
        self.slant = [
            (exchange(self.own, y_mask ^ x_mask), my, mx, 0)
            for my, y_mask in self.y_masks.items()
            for mx, x_mask in self.x_masks.items()
        ]

    def go_xy(self, hold_x=()):
        self.at_y = {m: exchange(self.own, mask) for m, mask in self.y_masks.items()}
        sent = tie(self.own, *hold_x) if hold_x else self.own
        self.at_x = {m: exchange(sent, mask) for m, mask in self.x_masks.items()}

    def came_xy(self):
        return tuple(self.at_y.values()) + tuple(self.at_x.values())

    def go_slant(self, *hold):
        at_y, at_x = self.at_y, self.at_x
        if hold:
            at_y = {m: tie(array, *hold) for m, array in at_y.items()}
            at_x = {m: tie(array, *hold) for m, array in at_x.items()}
        half = self.own.shape[0] // 2
        self.slant = []
        for my in at_y:
            for mx in at_x:
                self.slant.append((exchange(at_y[my][:half], self.x_masks[mx]), my, mx, 0))
                self.slant.append((exchange(at_x[mx][half:], self.y_masks[my]), my, mx, half))

    def pieces(self):
        pieces = [(self.own, 0, 0, 0)]
        pieces += [(array, m, 0, 0) for m, array in self.at_y.items()]
        pieces += [(array, 0, m, 0) for m, array in self.at_x.items()]
        return pieces + self.slant


class Scatter:
    def __init__(self, groups, *hold):
        self.groups = groups
        self.z_masks, self.x_masks, self.y_masks = along(2), along(1), along(0)
        half = groups[0, 0].shape[0] // 2
        at_y = {m: [[], []] for m in self.y_masks}
        at_x = {m: [[], []] for m in self.x_masks}
        for my in self.y_masks:
            for mx in self.x_masks:
                piece = groups[my, mx]
                one = exchange(piece[:half], self.x_masks[mx])
                two = exchange(piece[half:], self.y_masks[my])
                if hold:
                    one, two = tie(one, *hold), tie(two, *hold)
                at_y[my][0].append(one)
                at_x[mx][1].append(two)

        def joined(piece, terms):
            if not (terms[0] or terms[1]):
                return piece
            parts = total(piece[:half], terms[0]), total(piece[half:], terms[1])
            return jnp.concatenate(parts)

        self.sent = {(m, 0): joined(groups[m, 0], at_y[m]) for m in self.y_masks}
        self.sent.update({(0, m): joined(groups[0, m], at_x[m]) for m in self.x_masks})

    def go_xy(self, extra=None, *hold):
        masks = {(m, 0): mask for m, mask in self.y_masks.items()}
        masks.update({(0, m): mask for m, mask in self.x_masks.items()})
        sent, self.extra, slant = dict(self.sent), extra, []
        if extra is not None:
            sent = {g: jnp.concatenate([piece, extra[g]], axis=2) for g, piece in sent.items()}
            slant = [(extra[my, mx], self.y_masks[my] ^ self.x_masks[mx])
                     for my in self.y_masks for mx in self.x_masks]
        if hold:
            sent = {g: tie(piece, *hold) for g, piece in sent.items()}
        self.came = [exchange(piece, masks[g]) for g, piece in sent.items()]
        self.came_slant = [exchange(piece, mask) for piece, mask in slant]

    def take_xy(self, *hold):
        came = list(self.came)
        if hold:
            came = [tie(array, *hold) for array in came]
        width = self.groups[0, 0].shape[2]
        self.own = total(self.groups[0, 0], [array[:, :, :width] for array in came])
        if self.extra is not None:
            terms = [array[:, :, width:] for array in came] + self.came_slant
            self.own = jnp.concatenate([self.own, total(self.extra[0, 0], terms)], axis=2)

    def go_z(self, *hold):
        parts = {m: self.own[m] for m in self.z_masks}
        if hold:
            parts = {m: tie(part, *hold) for m, part in parts.items()}
        self.came_z = [exchange(parts[m], mask) for m, mask in self.z_masks.items()]

    def result(self, *hold):
        came = list(self.came_z)
        if hold:
            came = [tie(array, *hold) for array in came]
        value = self.own[0].astype(f32)
        for array in came:
            value = value + array.astype(f32)
        return value


def total(piece, terms):
    if not terms:
        return piece
    value = piece.astype(f32)
    for term in terms:
        value = value + term.astype(f32)
    return to_low(value)


def tie(values, *others):
    return lax.optimization_barrier((values,) + others)[0]


def row_masks():
    return [1 << bit for bit in range(lax.axis_size("row").bit_length() - 1)]


def row_sum(values, *hold):
    for mask in row_masks():
        values = values + exchange(to_low(values), mask).astype(f32)
    return tie(values, *hold) if hold else values


def row_gather(values):
    place = lax.axis_index("row")
    values = values[None]
    for mask in row_masks():
        other = exchange(values, mask)
        first = place & mask == 0
        values = jnp.concatenate(
            [jnp.where(first, values, other), jnp.where(first, other, values)], axis=0
        )
    return values


def row_swap(values):
    place = lax.axis_index("row")
    steps = len(row_masks())
    values = values.reshape((2,) * steps + values.shape[1:])
    for step, mask in enumerate(row_masks()):
        axis = steps - 1 - step
        mine = (place >> step) & 1
        keep = lax.dynamic_index_in_dim(values, mine, axis, keepdims=False)
        got = exchange(lax.dynamic_index_in_dim(values, 1 - mine, axis, keepdims=False), mask)
        low, high = jnp.where(mine == 0, keep, got), jnp.where(mine == 0, got, keep)
        values = jnp.stack([low, high], axis=axis)
    return values.reshape((-1,) + values.shape[steps:])


def spread(values, axes):
    names = axes if isinstance(axes, tuple) else (axes,)
    count = 1
    for name in names:
        count *= lax.axis_size(name)
    copies = jnp.broadcast_to(values[None], (count,) + values.shape)
    return lax.all_to_all(copies, axes, 0, 0, tiled=True)


def run_kernel(
    kernel, grid, inputs, outputs, scratch=(), scalars=None, after=(), flops=0, moved=2**22, exps=0
):
    count = 0 if scalars is None else 1

    def spec(block, index):
        if index is None:
            zeros = (0,) * len(block)
            return pl.BlockSpec(block, lambda *ids: zeros)
        return pl.BlockSpec(block, lambda *ids: index(*ids[: len(grid)]))

    arrays, in_specs = [], []
    for entry in inputs:
        arrays.append(entry[0])
        if len(entry) == 1:
            in_specs.append(spec(entry[0].shape, None))
        elif len(entry) == 2:
            in_specs.append(pl.BlockSpec(memory_space=entry[1]))
        else:
            in_specs.append(spec(entry[1], entry[2]))
    many, extra = len(arrays), len(after)
    arrays.extend(after)
    in_specs.extend([pl.BlockSpec(memory_space=pl.ANY)] * extra)
    out_specs, out_shape = [], []
    for shape, dtype, *rest in outputs:
        out_shape.append(jax.ShapeDtypeStruct(shape, dtype))
        if not rest:
            out_specs.append(spec(shape, None))
        elif len(rest) == 1:
            out_specs.append(pl.BlockSpec(memory_space=rest[0]))
        else:
            out_specs.append(spec(*rest))

    def wrapped(*refs):
        kernel(*refs[: count + many], *refs[count + many + extra :])

    call = pl.pallas_call(
        wrapped,
        grid_spec=pltpu.PrefetchScalarGridSpec(
            num_scalar_prefetch=count,
            grid=grid,
            in_specs=in_specs,
            out_specs=out_specs,
            scratch_shapes=list(scratch),
        ),
        out_shape=out_shape,
        compiler_params=pltpu.CompilerParams(vmem_limit_bytes=VMEM_BYTES),
        cost_estimate=pl.CostEstimate(flops=flops, bytes_accessed=moved, transcendentals=exps),
    )
    return call(*([] if scalars is None else [scalars]), *arrays)


def frame_rows(columns):
    return (PER_FRAME, columns), lambda f: (f, 0)


def frame_lines(ref, first, count, per_frame):
    lines = [
        jnp.broadcast_to(ref[pl.ds(first + k, 1), :], (per_frame, ref.shape[1]))
        for k in range(count)
    ]
    return jnp.concatenate(lines, axis=0)


def head_mask(width, head, rotary):
    lane = lax.broadcasted_iota(jnp.int32, (1, width), 1)
    if rotary:
        return (lane % (width // 2)) // (HD // 2) == head
    return lane // HD == head


def chip_number(coords, my, mx, mz):
    return ((coords[2] ^ mz) * coords[5] + (coords[1] ^ mx)) * coords[4] + (coords[0] ^ my)


def run_place(coords, pieces, columns, after=()):
    rows = pieces[0][0].shape[1]
    chips = sum(piece[0].shape[0] for piece in pieces)
    edges = [sum(columns[:k]) for k in range(len(columns) + 1)]

    def kernel(coords_ref, *refs):
        sources = refs[: len(pieces)]
        targets = refs[len(pieces) : len(pieces) + len(columns)]
        sems = refs[-1]
        copies = []
        for source, (array, my, mx, first) in zip(sources, pieces):
            for k in range(array.shape[0]):
                chip = chip_number(coords_ref, my, mx, first + k)
                spot = pl.ds(pl.multiple_of(chip * rows, rows), rows)
                for number, target in enumerate(targets):
                    lanes = pl.ds(edges[number], columns[number])
                    copies.append(
                        pltpu.make_async_copy(
                            source.at[k, :, lanes], target.at[spot, :], sems.at[len(copies)]
                        )
                    )
        for copy in copies:
            copy.start()
        for copy in copies:
            copy.wait()

    return run_kernel(
        kernel,
        (1,),
        [(piece[0], pl.ANY) for piece in pieces],
        [((chips * rows, wide), bf16) for wide in columns],
        [pltpu.SemaphoreType.DMA((chips * len(columns),))],
        coords,
        after,
        moved=4 * chips * rows * sum(columns),
    )


def run_qkv_attend(coords, span, noisy, embed, shift, scale, cosine, sine, pieces, ranks, after=()):
    rows, columns = pieces[0][0].shape[1:]
    width = columns // 3
    half, heads, per_frame = width // 2, width // HD, PER_FRAME // ranks
    count = 2
    block, steps = count * PER_FRAME, FRAMES // count
    stack = heads * PER_FRAME
    base = coords.shape[0]

    def kernel(number_ref, noisy_ref, embed_ref, shift_ref, scale_ref, cos_ref, sin_ref, *refs):
        sources = refs[: len(pieces)]
        q_ref, k_ref, v_ref, in_ref, w_ref, o_ref, lse_ref, sems, *scratch = refs[len(pieces) :]
        step = pl.program_id(0)

        def copies():
            made = []
            for source, (array, my, mx, first) in zip(sources, pieces):
                for k in range(array.shape[0]):
                    place = (number_ref[2] ^ (first + k)) * number_ref[5] + (number_ref[1] ^ mx)
                    spot = pl.ds(pl.multiple_of(place * rows, rows), rows)
                    made.append(
                        pltpu.make_async_copy(source.at[k], w_ref.at[spot, :], sems.at[len(made)])
                    )
            return made

        @pl.when(step == 0)
        def start():
            for copy in copies():
                copy.start()

        @pl.when(step < steps)
        def project():
            normed, unused = norm_parts(mm(noisy_ref[...], embed_ref[...], 1, 0))
            scale = frame_lines(scale_ref, step * count, count, PER_FRAME)
            shift = frame_lines(shift_ref, step * count, count, PER_FRAME)
            attn_in = to_low(normed * (1.0 + scale) + shift)
            in_ref[...] = attn_in

            @pl.when(step == 0)
            def finish():
                for copy in copies():
                    copy.wait()

            out = mm(attn_in, w_ref[...], 1, 0)
            cos, sin = cos_ref[...], sin_ref[...]
            spot = pl.ds(step * block, block)
            for ref, first, factor in ((q_ref, 0, HD**-0.5), (k_ref, width, 1.0)):
                lower = out[:, first : first + half]
                upper = out[:, first + half : first + width]
                ref[spot, :half] = to_low(lower * cos - upper * sin) * factor
                ref[spot, half:] = to_low(upper * cos + lower * sin) * factor
            v_ref[spot, :] = to_low(out[:, 2 * width :])

        @pl.when(step >= steps)
        def attend():
            frame = step - steps
            first, last = number_ref[base + frame], number_ref[base + FRAMES + frame]
            attend_frame(frame, first, last, q_ref, k_ref, v_ref, o_ref, lse_ref, *scratch)

    lines = lambda wide: ((block, wide), lambda i: (jnp.minimum(i, steps - 1), 0))
    at_frame = lambda i: jnp.maximum(i - steps, 0)
    chips = sum(piece[0].shape[0] for piece in pieces)
    return run_kernel(
        kernel,
        (steps + FRAMES,),
        [
            (noisy, *lines(PD)),
            (embed,),
            (shift,),
            (scale,),
            (cosine, *lines(half)),
            (sine, *lines(half)),
        ]
        + [(piece[0], pl.ANY) for piece in pieces],
        [((TOK, width), bf16)] * 3
        + [
            ((TOK, D), bf16, *lines(D)),
            ((D, columns), bf16),
            (
                (ranks, FRAMES, per_frame, width),
                bf16,
                (ranks, 1, per_frame, width),
                lambda i: (0, at_frame(i), 0, 0),
            ),
            ((FRAMES * stack, 128), f32, (stack, 128), lambda i: (at_frame(i), 0)),
        ],
        [
            pltpu.SemaphoreType.DMA((chips,)),
            pltpu.VMEM((stack, width), bf16),
            pltpu.VMEM((FRAMES, stack, PER_FRAME), f32),
            pltpu.VMEM((stack, 128), f32),
            pltpu.VMEM((stack, 128), f32),
            pltpu.VMEM((stack, width), f32),
        ],
        jnp.concatenate([coords, span.reshape(-1)]),
        after,
        flops=2 * TOK * D * columns + 4 * 36 * PER_FRAME * PER_FRAME * 256 * heads,
        moved=20 * 2**20,
        exps=36 * PER_FRAME * PER_FRAME * heads,
    )


def attend_frame(frame, start, stop, q_ref, k_ref, v_ref, o_ref, lse_ref, q_scr, s_scr, m_scr, l_scr, acc_scr):
    width = q_ref.shape[1]
    heads = width // HD
    block = PER_FRAME
    query = q_ref[pl.ds(frame * block, block), :]
    for head in range(heads):
        q_scr[head * block : (head + 1) * block, :] = jnp.where(
            head_mask(width, head, True), query, jnp.zeros_like(query)
        )
    m_scr[...] = jnp.full_like(m_scr, -1e30)
    l_scr[...] = jnp.zeros_like(l_scr)
    acc_scr[...] = jnp.zeros_like(acc_scr)

    def scores(e, carry):
        keys = k_ref[pl.ds(e * block, block), :]
        for head in range(heads):
            rows = slice(head * block, (head + 1) * block)
            score = mm(q_scr[rows, :], keys, 1, 1)
            s_scr[e, rows, :] = score
            top = jnp.maximum(score[:, :128], score[:, 128:])
            m_scr[rows, :] = jnp.maximum(m_scr[rows, :], top)
        return carry

    lax.fori_loop(start, stop, scores, 0)
    for head in range(heads):
        rows = slice(head * block, (head + 1) * block)
        m_scr[rows, :] = jnp.broadcast_to(
            jnp.max(m_scr[rows, :], axis=1, keepdims=True), (block, 128)
        )

    def combine(e, carry):
        values = v_ref[pl.ds(e * block, block), :]
        for head in range(heads):
            rows = slice(head * block, (head + 1) * block)
            top = m_scr[rows, :]
            left = jnp.exp(s_scr[e, rows, :128] - top)
            right = jnp.exp(s_scr[e, rows, 128:] - top)
            l_scr[rows, :] = l_scr[rows, :] + (left + right)
            weight = jnp.concatenate([to_low(left), to_low(right)], axis=1)
            acc_scr[rows, :] = acc_scr[rows, :] + mm(weight, values, 1, 0)
        return carry

    lax.fori_loop(start, stop, combine, 0)
    result = jnp.zeros((block, width), f32)
    for head in range(heads):
        rows = slice(head * block, (head + 1) * block)
        total = jnp.sum(l_scr[rows, :], axis=1, keepdims=True)
        lse_ref[rows, :] = m_scr[rows, :] + jnp.log(total)
        result = jnp.where(head_mask(width, head, False), acc_scr[rows, :] / total, result)
    o_ref[...] = to_low(result).reshape(o_ref.shape)


def attend_back_kernel(
    span_ref, q_ref, k_ref, v_ref, o_ref, g_ref, lse_ref, cos_ref, sin_ref, out_ref,
    q_scr, g_scr, d_scr, dq_scr, dk_scr, dv_scr, p_scr, s_scr,
):
    frame = pl.program_id(0)
    width = q_ref.shape[1]
    half = width // 2
    heads = width // HD
    block = PER_FRAME
    start, stop = span_ref[0, frame], span_ref[1, frame]

    @pl.when(frame == 0)
    def clear():
        dk_scr[...] = jnp.zeros_like(dk_scr)
        dv_scr[...] = jnp.zeros_like(dv_scr)

    query = q_ref[...]
    grad = g_ref[...].reshape(block, width)
    product = grad.astype(f32) * o_ref[...].reshape(block, width).astype(f32)
    for head in range(heads):
        rows = slice(head * block, (head + 1) * block)
        q_scr[rows, :] = jnp.where(head_mask(width, head, True), query, jnp.zeros_like(query))
        own = head_mask(width, head, False)
        g_scr[rows, :] = jnp.where(own, grad, jnp.zeros_like(grad))
        inner = jnp.sum(jnp.where(own, product, 0.0), axis=1, keepdims=True)
        d_scr[rows, :] = jnp.broadcast_to(inner, (block, 128))
    dq_scr[...] = jnp.zeros_like(dq_scr)

    def step(e, carry):
        spot = pl.ds(e * block, block)
        keys, values = k_ref[spot, :], v_ref[spot, :]
        for head in range(heads):
            rows = slice(head * block, (head + 1) * block)
            score = mm(q_scr[rows, :], keys, 1, 1)
            grad_w = mm(g_scr[rows, :], values, 1, 1)
            lse, inner = lse_ref[rows, :], d_scr[rows, :]
            for part in range(2):
                lanes = slice(part * 128, (part + 1) * 128)
                weight = jnp.exp(score[:, lanes] - lse)
                p_scr[rows, lanes] = to_low(weight)
                s_scr[rows, lanes] = to_low(weight * (grad_w[:, lanes] - inner))
        dq_scr[...] = dq_scr[...] + mm(s_scr[...], keys, 1, 0)
        dk_scr[spot, :] = dk_scr[spot, :] + mm(s_scr[...], q_scr[...], 0, 0)
        dv_scr[spot, :] = dv_scr[spot, :] + mm(p_scr[...], g_scr[...], 0, 0)
        return carry

    lax.fori_loop(start, stop, step, 0)

    def unrotate(grads, cosine, sine, where, base):
        lower, upper = grads[:, :half], grads[:, half:]
        out_ref[where, base : base + half] = to_low(lower * cosine + upper * sine)
        out_ref[where, base + half : base + width] = to_low(upper * cosine - lower * sine)

    total = jnp.zeros((block, width), f32)
    for head in range(heads):
        rows = slice(head * block, (head + 1) * block)
        total = jnp.where(head_mask(width, head, True), dq_scr[rows, :], total)
    spot = pl.ds(frame * block, block)
    unrotate(total * HD**-0.5, cos_ref[spot, :], sin_ref[spot, :], spot, 0)

    @pl.when(frame == FRAMES - 1)
    def finish():
        def one(e, carry):
            spot = pl.ds(e * block, block)
            unrotate(dk_scr[spot, :], cos_ref[spot, :], sin_ref[spot, :], spot, width)
            out_ref[spot, 2 * width :] = to_low(dv_scr[spot, :])
            return carry

        lax.fori_loop(0, FRAMES, one, 0)


def run_attend_back(span, query, keys, values, out, grad, lse, cosine, sine, after=()):
    block = PER_FRAME
    rows, unused, per_frame, width = out.shape
    heads = width // HD
    parts = (rows, 1, per_frame, width), lambda f: (0, f, 0, 0)
    return run_kernel(
        attend_back_kernel,
        (FRAMES,),
        [
            (query, *frame_rows(width)),
            (keys,),
            (values,),
            (out, *parts),
            (grad, *parts),
            (lse, (heads * block, 128), lambda f: (f, 0)),
            (cosine,),
            (sine,),
        ],
        [((TOK, 3 * width), bf16)],
        [
            pltpu.VMEM((heads * block, width), bf16),
            pltpu.VMEM((heads * block, width), bf16),
            pltpu.VMEM((heads * block, 128), f32),
            pltpu.VMEM((heads * block, width), f32),
            pltpu.VMEM((TOK, width), f32),
            pltpu.VMEM((TOK, width), f32),
            pltpu.VMEM((heads * block, block), bf16),
            pltpu.VMEM((heads * block, block), bf16),
        ],
        span,
        after,
        flops=5 * 2 * 36 * block * block * 256 * heads,
        moved=12 * 2**20,
        exps=36 * block * block * heads,
    )[0]


def run_qkv_dw(attn_in, grad, after=()):
    columns = grad.shape[1]
    count = 2
    block, steps = count * PER_FRAME, FRAMES // count

    def kernel(in_ref, g_ref, out_ref, acc):
        step = pl.program_id(0)
        accumulate(acc, step, lambda: mm(in_ref[...], g_ref[...], 0, 0))

        @pl.when(step == steps - 1)
        def finish():
            out_ref[...] = to_low(acc[...])

    return run_kernel(
        kernel,
        (steps,),
        [
            (attn_in, (block, D), lambda i: (i, 0)),
            (grad, (block, columns), lambda i: (i, 0)),
        ],
        [((D, columns), bf16)],
        [pltpu.VMEM((D, columns), f32)],
        after=after,
        flops=2 * TOK * D * columns,
        moved=10 * 2**20,
    )[0]


def run_qkv_back(noisy, embed, scale, grad, weight, after=()):
    columns = weight.shape[1]

    def kernel(noisy_ref, embed_ref, scale_ref, g_ref, w_ref, sum_ref, ge_ref):
        frame = pl.program_id(0)
        noisy = noisy_ref[...]
        normed, inverse = norm_parts(mm(noisy, embed_ref[...], 1, 0))
        grad_in = mm(g_ref[...], w_ref[...], 1, 1)
        spot = pl.ds(frame, 1)
        sum_ref[spot, :D] = jnp.sum(grad_in, axis=0, keepdims=True)
        sum_ref[spot, D:] = jnp.sum(grad_in * normed, axis=0, keepdims=True)
        grad_h = norm_back(normed, inverse, grad_in * (1.0 + scale_ref[spot, :]))
        accumulate(ge_ref, frame, lambda: mm(noisy, to_low(grad_h), 0, 0))

    return run_kernel(
        kernel,
        (FRAMES,),
        [
            (noisy, *frame_rows(PD)),
            (embed,),
            (scale,),
            (grad, *frame_rows(columns)),
            (weight,),
        ],
        [((FRAMES, 2 * D), f32), ((PD, D), f32)],
        after=after,
        flops=2 * TOK * D * columns,
        moved=8 * 2**20,
    )


REST = {
    name: slice(k * D, (k + 1) * D)
    for k, name in enumerate(("gate_a", "shift_m", "scale_m", "gate_m", "shift_f", "scale_f"))
}


def by_frame(ref, name, first, count, per_frame):
    rows = [
        jnp.broadcast_to(ref[pl.ds(first + k, 1), REST[name]], (per_frame, D))
        for k in range(count)
    ]
    return jnp.concatenate(rows, axis=0)


def store_sums(ref, first, number, values, per_frame):
    for k in range(values.shape[0] // per_frame):
        rows = values[k * per_frame : (k + 1) * per_frame]
        lanes = slice(number * D, (number + 1) * D)
        ref[pl.ds(first + k, 1), lanes] = jnp.sum(rows, axis=0, keepdims=True)


def run_proj(coords, attn, noisy, embed, rest, own, other, after=()):
    rows, tokens, width = attn.shape
    per_frame, steps = tokens // FRAMES, 2
    block, count = tokens // steps, FRAMES // steps

    def kernel(coords_ref, a_ref, n_ref, e_ref, rest_ref, own_ref, other_ref, h_ref, p_ref, in_ref):
        first = pl.program_id(0) * count
        mine = coords_ref[3] == 0
        attn_b = jnp.concatenate([a_ref[r] for r in range(rows)], axis=1)
        one, two = mm(attn_b, own_ref[...], 1, 0), mm(attn_b, other_ref[...], 1, 0)
        out = jnp.concatenate([jnp.where(mine, one, two), jnp.where(mine, two, one)], axis=1)
        p_ref[...] = out
        hidden = mm(n_ref[...], e_ref[...], 1, 0)
        hidden = hidden + by_frame(rest_ref, "gate_a", first, count, per_frame) * out
        h_ref[...] = hidden
        normed, unused = norm_parts(hidden)
        scale = by_frame(rest_ref, "scale_m", first, count, per_frame)
        shift = by_frame(rest_ref, "shift_m", first, count, per_frame)
        in_ref[...] = to_low(normed * (1.0 + scale) + shift)

    part = (block, D), lambda i: (i, 0)
    return run_kernel(
        kernel,
        (steps,),
        [
            (attn, (rows, block, width), lambda i: (0, i, 0)),
            (noisy, (block, PD), lambda i: (i, 0)),
            (embed,),
            (rest,),
            (own,),
            (other,),
        ],
        [((tokens, D), f32, *part), ((tokens, D), f32, *part), ((tokens, D), bf16, *part)],
        scalars=coords,
        after=after,
        flops=2 * tokens * D * D,
        moved=10 * 2**20,
    )


GELU_C = math.sqrt(2.0 / math.pi)
GELU_A = 0.044715


def gelu_value(x):
    return 0.5 * x * (1.0 + jnp.tanh(GELU_C * (x + GELU_A * (x * x * x))))


def gelu_slope(x):
    square = x * x
    t = jnp.tanh(GELU_C * x * (1.0 + GELU_A * square))
    return 0.5 * (1.0 + t) + (0.5 * GELU_C) * x * (1.0 - t * t) * (1.0 + 3.0 * GELU_A * square)


CHUNK = 512


def down_rows(weight):
    return weight, (CHUNK, D), lambda j: (j, 0)


def up_columns(weight):
    return weight, (D, CHUNK), lambda j: (0, j)


def run_up(mlp_in, up, after=()):
    tokens, hidden = mlp_in.shape[0], up.shape[1]

    def kernel(in_ref, up_ref, out_ref, act_ref):
        out = mm(in_ref[...], up_ref[...], 1, 0)
        out_ref[...] = out
        act_ref[...] = to_low(gelu_value(out))

    part = (tokens, CHUNK), lambda j: (0, j)
    return run_kernel(
        kernel,
        (hidden // CHUNK,),
        [(mlp_in,), up_columns(up)],
        [((tokens, hidden), f32, *part), ((tokens, hidden), bf16, *part)],
        after=after,
        flops=2 * tokens * D * hidden,
        moved=10 * 2**20,
    )


def parts_of(tokens):
    size = tokens // 2
    return [slice(k * size, (k + 1) * size) for k in range(2)]


def run_up_down(mlp_in, up, down, dtype, after=()):
    tokens, hidden = mlp_in.shape[0], up.shape[1]
    steps = hidden // CHUNK

    def kernel(in_ref, up_ref, down_ref, out_ref, act_ref, part_ref, acc):
        j = pl.program_id(0)

        @pl.when(j == 0)
        def clear():
            acc[...] = jnp.zeros_like(acc)

        spans = parts_of(tokens)
        ready = mm(in_ref[spans[0], :], up_ref[...], 1, 0)
        for k, span in enumerate(spans):
            out = ready
            if k + 1 < len(spans):
                ready = mm(in_ref[spans[k + 1], :], up_ref[...], 1, 0)
            out_ref[span, :] = out
            act_ref[span, :] = to_low(gelu_value(out))
        acc[...] = acc[...] + mm(act_ref[...], down_ref[...], 1, 0)

        @pl.when(j == steps - 1)
        def finish():
            part_ref[...] = acc[...].astype(part_ref.dtype)

    part = (tokens, CHUNK), lambda j: (0, j)
    return run_kernel(
        kernel,
        (steps,),
        [(mlp_in,), up_columns(up), down_rows(down)],
        [
            ((tokens, hidden), f32, *part),
            ((tokens, hidden), bf16, *part),
            ((tokens, D), dtype),
        ],
        [pltpu.VMEM((tokens, D), f32)],
        after=after,
        flops=4 * tokens * D * hidden,
        moved=16 * 2**20,
    )


def accumulate(acc, step, term):
    @pl.when(step == 0)
    def first():
        acc[...] = jnp.zeros_like(acc)

    acc[...] = acc[...] + term()


def run_down(act, down, after=()):
    tokens, hidden = act.shape

    def kernel(act_ref, down_ref, out_ref):
        accumulate(out_ref, pl.program_id(0), lambda: mm(act_ref[...], down_ref[...], 1, 0))

    return run_kernel(
        kernel,
        (hidden // CHUNK,),
        [(act, (tokens, CHUNK), lambda j: (0, j)), down_rows(down)],
        [((tokens, D), f32)],
        after=after,
        flops=2 * tokens * D * hidden,
        moved=8 * 2**20,
    )[0]


def run_head(flags, hidden1, part, got, rest, head, target, after=()):
    tokens = hidden1.shape[0]
    per_frame, count = tokens // FRAMES, 2
    block = count * per_frame

    def kernel(
        flag_ref, h_ref, p_ref, got_ref, rest_ref, head_ref, t_ref,
        gd_ref, gh_ref, sum_ref, ghead_ref, loss_ref,
    ):
        first = pl.program_id(0) * count

        @pl.when(first == 0)
        def clear():
            ghead_ref[...] = jnp.zeros_like(ghead_ref)

        mod = lambda name: by_frame(rest_ref, name, first, count, per_frame)
        frame_of = lax.broadcasted_iota(jnp.int32, (block, 1), 0) // per_frame
        true = jnp.where(frame_of == 0, flag_ref[first], flag_ref[first + 1])
        down_out = p_ref[...] + got_ref[...].astype(f32)
        hidden = h_ref[...] + mod("gate_m") * down_out
        normed, inverse = norm_parts(hidden)
        scale = 1.0 + mod("scale_f")
        final_in = to_low(normed * scale + mod("shift_f"))
        pred = mm(final_in, head_ref[...], 1, 0)
        error = (pred - t_ref[...]) * true
        loss_ref[pl.ds(pl.program_id(0), 1), :] = jnp.broadcast_to(
            jnp.sum(jnp.sum(error * error, axis=1, keepdims=True), axis=0, keepdims=True), (1, 128)
        )
        grad_pred = to_low(2.0 * error / flag_ref[FRAMES])
        ghead_ref[...] = ghead_ref[...] + mm(final_in, grad_pred, 0, 0)
        grad_fin = mm(grad_pred, head_ref[...], 1, 1)
        store_sums(sum_ref, first, 1, grad_fin, per_frame)
        store_sums(sum_ref, first, 2, grad_fin * normed, per_frame)
        grad = norm_back(normed, inverse, grad_fin * scale)
        gh_ref[...] = grad
        store_sums(sum_ref, first, 0, grad * down_out, per_frame)
        gd_ref[...] = to_low(grad * mod("gate_m"))

    part_spec = (block, D), lambda f: (f, 0)
    return run_kernel(
        kernel,
        (FRAMES // count,),
        [
            (flags, pltpu.SMEM),
            (hidden1, *part_spec),
            (part, *part_spec),
            (got, *part_spec),
            (rest,),
            (head,),
            (target, (block, PD), lambda f: (f, 0)),
        ],
        [
            ((tokens, D), bf16, *part_spec),
            ((tokens, D), f32, *part_spec),
            ((FRAMES, 3 * D), f32),
            ((D, PD), f32),
            ((FRAMES // count, 128), f32),
        ],
        after=after,
        flops=8 * tokens * D * PD,
        moved=10 * 2**20,
    )


def run_act_back(grad, down, up_out, after=()):
    tokens, hidden = up_out.shape

    def kernel(g_ref, down_ref, up_ref, out_ref):
        grad_act = mm(g_ref[...], down_ref[...], 1, 1)
        out_ref[...] = to_low(grad_act * gelu_slope(up_ref[...]))

    part = (tokens, CHUNK), lambda j: (0, j)
    return run_kernel(
        kernel,
        (hidden // CHUNK,),
        [(grad,), down_rows(down), (up_out, *part)],
        [((tokens, hidden), bf16, *part)],
        after=after,
        flops=2 * tokens * D * hidden,
        moved=10 * 2**20,
    )[0]


def run_act_up_back(grad, down, up_out, up, dtype, after=()):
    tokens, hidden = up_out.shape
    steps = hidden // CHUNK

    def kernel(g_ref, down_ref, o_ref, up_ref, out_ref, part_ref, acc):
        j = pl.program_id(0)

        @pl.when(j == 0)
        def clear():
            acc[...] = jnp.zeros_like(acc)

        spans = parts_of(tokens)
        ready = mm(g_ref[spans[0], :], down_ref[...], 1, 1)
        for k, span in enumerate(spans):
            grad_act = ready
            if k + 1 < len(spans):
                ready = mm(g_ref[spans[k + 1], :], down_ref[...], 1, 1)
            out_ref[span, :] = to_low(grad_act * gelu_slope(o_ref[span, :]))
        acc[...] = acc[...] + mm(out_ref[...], up_ref[...], 1, 1)

        @pl.when(j == steps - 1)
        def finish():
            part_ref[...] = acc[...].astype(part_ref.dtype)

    part = (tokens, CHUNK), lambda j: (0, j)
    return run_kernel(
        kernel,
        (steps,),
        [(grad,), down_rows(down), (up_out, *part), up_columns(up)],
        [((tokens, hidden), bf16, *part), ((tokens, D), dtype)],
        [pltpu.VMEM((tokens, D), f32)],
        after=after,
        flops=4 * tokens * D * hidden,
        moved=16 * 2**20,
    )


def run_up_back(grad, up, after=()):
    tokens, hidden = grad.shape

    def kernel(g_ref, up_ref, out_ref):
        accumulate(out_ref, pl.program_id(0), lambda: mm(g_ref[...], up_ref[...], 1, 1))

    return run_kernel(
        kernel,
        (hidden // CHUNK,),
        [(grad, (tokens, CHUNK), lambda j: (0, j)), up_columns(up)],
        [((tokens, D), f32)],
        after=after,
        flops=2 * tokens * D * hidden,
        moved=8 * 2**20,
    )[0]


def group_list(sizes):
    ny, nx, nz = sizes
    return [(my, mx) for my in range(ny) for mx in range(nx)]


def run_down_dw(coords, sizes, acts, grads, after=()):
    groups, nz = group_list(sizes), sizes[2]
    hidden = acts[0].shape[1]
    rows = hidden // (len(groups) * nz)
    steps = hidden // CHUNK

    def kernel(coords_ref, a_ref, b_ref, ga_ref, gb_ref, *refs):
        outs, acc = refs[: len(groups)], refs[len(groups)]
        j = pl.program_id(0)
        acc[j] = mm(a_ref[...], ga_ref[...], 0, 0) + mm(b_ref[...], gb_ref[...], 0, 0)

        @pl.when(j == steps - 1)
        def finish():
            for out, (my, mx) in zip(outs, groups):
                for mz in range(nz):
                    first = chip_number(coords_ref, my, mx, mz) * rows
                    spot = pl.ds(pl.multiple_of(first % CHUNK, rows), rows)
                    out[mz] = to_low(acc[first // CHUNK, spot, :])

    part = (acts[0].shape[0], CHUNK), lambda j: (0, j)
    outs = run_kernel(
        kernel,
        (steps,),
        [(acts[0], *part), (acts[1], *part), (grads[0],), (grads[1],)],
        [((nz, rows, D), bf16)] * len(groups),
        [pltpu.VMEM((steps, CHUNK, D), f32)],
        coords,
        after,
        flops=4 * acts[0].shape[0] * D * hidden,
        moved=10 * 2**20,
    )
    return dict(zip(groups, outs))


def run_act_up_dw(coords, sizes, ins, grad_up, grad, down, up_out, up, after=()):
    groups, nz = group_list(sizes), sizes[2]
    rows = D // (len(groups) * nz)
    tokens, hidden = up_out.shape
    steps = hidden // CHUNK

    def kernel(coords_ref, a_ref, b_ref, ga_ref, g_ref, down_ref, o_ref, up_ref, part_ref, *refs):
        outs, (acc, part_acc, gb_scr) = refs[: len(groups)], refs[len(groups) :]
        j = pl.program_id(0)

        @pl.when(j == 0)
        def clear():
            part_acc[...] = jnp.zeros_like(part_acc)

        spans = parts_of(tokens)
        ready = mm(g_ref[spans[0], :], down_ref[...], 1, 1)
        for k, span in enumerate(spans):
            grad_act = ready
            if k + 1 < len(spans):
                ready = mm(g_ref[spans[k + 1], :], down_ref[...], 1, 1)
            gb_scr[span, :] = to_low(grad_act * gelu_slope(o_ref[span, :]))
        acc[...] = mm(a_ref[...], ga_ref[...], 0, 0) + mm(b_ref[...], gb_scr[...], 0, 0)
        part_acc[...] = part_acc[...] + mm(gb_scr[...], up_ref[...], 1, 1)
        for out, (my, mx) in zip(outs, groups):
            for mz in range(nz):
                first = chip_number(coords_ref, my, mx, mz) * rows
                out[mz] = to_low(acc[pl.ds(pl.multiple_of(first, rows), rows), :])

        @pl.when(j == steps - 1)
        def finish():
            part_ref[...] = to_low(part_acc[...])

    part = (tokens, CHUNK), lambda j: (0, j)
    outs = run_kernel(
        kernel,
        (steps,),
        [
            (ins[0],),
            (ins[1],),
            (grad_up, *part),
            (grad,),
            down_rows(down),
            (up_out, *part),
            up_columns(up),
        ],
        [((tokens, D), bf16)]
        + [((nz, rows, hidden), bf16, (nz, rows, CHUNK), lambda j: (0, 0, j))] * len(groups),
        [
            pltpu.VMEM((D, CHUNK), f32),
            pltpu.VMEM((tokens, D), f32),
            pltpu.VMEM((tokens, CHUNK), bf16),
        ],
        coords,
        after,
        flops=8 * tokens * D * hidden,
        moved=26 * 2**20,
    )
    return outs[0], dict(zip(groups, outs[1:]))


def run_add_pieces(coords, sizes, terms, after=()):
    groups, nz = group_list(sizes), sizes[2]
    rows, columns = terms[0].shape[0] // (len(groups) * nz), terms[0].shape[1]

    def kernel(coords_ref, a_ref, b_ref, *refs):
        outs, acc = refs[: len(groups)], refs[len(groups)]
        acc[...] = a_ref[...].astype(f32) + b_ref[...].astype(f32)
        for out, (my, mx) in zip(outs, groups):
            for mz in range(nz):
                first = chip_number(coords_ref, my, mx, mz) * rows
                out[mz] = to_low(acc[pl.ds(pl.multiple_of(first, rows), rows), :])

    outs = run_kernel(
        kernel,
        (1,),
        [(terms[0],), (terms[1],)],
        [((nz, rows, columns), bf16)] * len(groups),
        [pltpu.VMEM(terms[0].shape, f32)],
        coords,
        after,
        moved=6 * terms[0].size,
    )
    return dict(zip(groups, outs))


def run_proj_back(coords, grad_h2, part, got, hidden1, proj_out, rest, own, other, attn, noisy, after=()):
    rows, tokens, width = attn.shape
    per_frame, steps = tokens // FRAMES, 2
    block, count = tokens // steps, FRAMES // steps

    def kernel(
        coords_ref, g_ref, p_ref, got_ref, h_ref, po_ref, rest_ref, own_ref, other_ref, a_ref, n_ref,
        ga_ref, mine_ref, theirs_ref, sum_ref, ge_ref, acc,
    ):
        step = pl.program_id(0)
        first = step * count
        mine = coords_ref[3] == 0
        grad_mlp = p_ref[...] + got_ref[...].astype(f32)
        normed, inverse = norm_parts(h_ref[...])
        store_sums(sum_ref, first, 1, grad_mlp, per_frame)
        store_sums(sum_ref, first, 2, grad_mlp * normed, per_frame)
        scale = by_frame(rest_ref, "scale_m", first, count, per_frame)
        grad = g_ref[...] + norm_back(normed, inverse, grad_mlp * (1.0 + scale))
        store_sums(sum_ref, first, 0, grad * po_ref[...], per_frame)
        low = to_low(grad * by_frame(rest_ref, "gate_a", first, count, per_frame))
        lower, upper = low[:, : D // 2], low[:, D // 2 :]
        grad_attn = mm(jnp.where(mine, lower, upper), own_ref[...], 1, 1)
        grad_attn = grad_attn + mm(jnp.where(mine, upper, lower), other_ref[...], 1, 1)
        grad_attn = to_low(grad_attn)
        attn_b = jnp.concatenate([a_ref[r] for r in range(rows)], axis=1)
        for r in range(rows):
            ga_ref[r] = grad_attn[:, r * width : (r + 1) * width]
        accumulate(acc, step, lambda: mm(attn_b, low, 0, 0))
        accumulate(ge_ref, step, lambda: mm(n_ref[...], to_low(grad), 0, 0))

        @pl.when(step == steps - 1)
        def finish():
            lower, upper = to_low(acc[:, : D // 2]), to_low(acc[:, D // 2 :])
            mine_ref[...] = jnp.where(mine, lower, upper)
            theirs_ref[...] = jnp.where(mine, upper, lower)

    piece = (block, D), lambda i: (i, 0)
    wide = (rows, block, width), lambda i: (0, i, 0)
    return run_kernel(
        kernel,
        (steps,),
        [
            (grad_h2, *piece),
            (part, *piece),
            (got, *piece),
            (hidden1, *piece),
            (proj_out, *piece),
            (rest,),
            (own,),
            (other,),
            (attn, *wide),
            (noisy, (block, PD), lambda i: (i, 0)),
        ],
        [
            ((rows, tokens, width), bf16, *wide),
            ((D, D // 2), bf16),
            ((D, D // 2), bf16),
            ((FRAMES, 3 * D), f32),
            ((PD, D), f32),
        ],
        [pltpu.VMEM((D, D), f32)],
        coords,
        after,
        flops=4 * tokens * D * D,
        moved=18 * 2**20,
    )


def run_lamb(entries, slots, fixes, after=()):
    def kernel(*refs):
        many = len(entries)
        ins, outs = refs[: 4 * many], refs[4 * many : 6 * many]
        sums = refs[6 * many]
        lane = lax.broadcasted_iota(jnp.int32, (1, 128), 1)
        row = jnp.zeros((1, 128), f32)
        for k, slot in enumerate(slots):
            weight, grad, first, second = (ref[...] for ref in ins[4 * k : 4 * k + 4])
            mom_ref, update_ref = outs[2 * k : 2 * k + 2]
            first_n, second_n, update = lamb_direction(weight, grad, first, second, *fixes)
            mom_ref[0] = first_n
            mom_ref[1] = second_n
            update_ref[...] = update
            for value, place in ((weight, 2 * slot), (update, 2 * slot + 1)):
                total = jnp.sum(value * value, axis=0, keepdims=True)
                total = jnp.sum(total, axis=1, keepdims=True)
                row = row + jnp.where(lane == place, total, 0.0)
        sums[...] = row

    outputs = []
    for weight, *unused in entries:
        outputs += [((2,) + weight.shape, f32), (weight.shape, f32)]
    moved = 28 * sum(entry[0].size for entry in entries)
    flat = [(array,) for entry in entries for array in entry]
    outs = run_kernel(kernel, (1,), flat, outputs + [((1, 128), f32)], after=after, moved=moved)
    return outs[0:-1:2], outs[1:-1:2], outs[-1]


def run_update(weights, updates, totals):
    def kernel(totals_ref, *refs):
        many = len(weights)
        lane = lax.broadcasted_iota(jnp.int32, (1, 128), 1)
        norms = jnp.sqrt(jnp.sum(totals_ref[...], axis=0, keepdims=True))
        for k in range(many):
            weight_ref, update_ref, out_ref = refs[k], refs[many + k], refs[2 * many + k]
            pick = lambda at: jnp.sum(jnp.where(lane == at, norms, 0.0), axis=1, keepdims=True)
            trust = learn_rate * (pick(2 * k) / pick(2 * k + 1))
            out_ref[...] = weight_ref[...] - trust * update_ref[...]

    return run_kernel(
        kernel,
        (1,),
        [(totals,)] + [(array,) for array in list(weights) + list(updates)],
        [(weight.shape, f32) for weight in weights],
        moved=12 * sum(weight.size for weight in weights),
    )


def lamb_direction(weight, gradient, first_m, second_m, fix_one, fix_two):
    first_n = beta_one * first_m + (1.0 - beta_one) * gradient
    second_n = jnp.sqrt(beta_two * second_m * second_m + (1.0 - beta_two) * gradient * gradient)
    update = first_n / fix_one / (second_n / math.sqrt(fix_two) + adam_eps) + weight_decay * weight
    return (first_n, second_n, update)


def body(
    latents, noise, levels, clip_ids, clip_lens,
    embed_w, table_w, adaln_w, qkv_w, proj_w, up_w, down_w, head_w,
    embed_avg, table_avg, adaln_avg, qkv_avg, proj_avg, up_avg, down_avg, head_avg,
    embed_sq, table_sq, adaln_sq, qkv_sq, proj_sq, up_sq, down_sq, head_sq,
):
    masters = (embed_w, table_w, adaln_w, qkv_w, proj_w, up_w, down_w, head_w)
    firsts = (embed_avg, table_avg, adaln_avg, qkv_avg, proj_avg, up_avg, down_avg, head_avg)
    seconds = (embed_sq, table_sq, adaln_sq, qkv_sq, proj_sq, up_sq, down_sq, head_sq)
    clips, rows = lax.axis_size("clip"), lax.axis_size("row")
    count_dev = clips * rows
    sizes, unused_bits = shape_of_mesh()
    ny, nx, nz = sizes
    clip_index, row_index = lax.axis_index("clip"), lax.axis_index("row")
    core = row_index % 2
    coords = jnp.stack(
        [
            row_index // 2,
            clip_index % nx,
            clip_index // nx,
            core,
            jnp.full_like(core, ny),
            jnp.full_like(core, nx),
        ]
    ).astype(jnp.int32)
    part = D // count_dev
    width = D // rows
    row_local = GRID // rows
    per_frame = row_local * GRID
    count_tok = FRAMES * per_frame
    hidden = FF // 2
    unit = FF // count_dev
    level_row = levels[0]
    frame_pos, is_true, starts, stops = frame_layout(clip_ids[0], clip_lens[0])
    span = jnp.stack([starts, stops]).astype(jnp.int32)

    own_count = jnp.sum(is_true.astype(f32))
    packed = jnp.concatenate(
        [
            level_row.astype(f32),
            jnp.broadcast_to(own_count, (8,)),
            embed_w.reshape(-1),
            head_w.reshape(-1),
        ]
    )
    everyone = spread(packed.reshape(1, -1), BOTH).reshape(count_dev, -1)
    all_levels = everyone[::rows, :FRAMES].astype(jnp.int32).reshape(-1)
    count = jnp.sum(everyone[::rows, FRAMES]) * PER_FRAME
    embed_b = to_low(everyone[:, 16 : 16 + PD * part].reshape(count_dev, PD, part))
    embed_b = embed_b.transpose(1, 0, 2).reshape(PD, D)
    head_b = to_low(everyone[:, 16 + PD * part :]).reshape(D, PD)

    one_hot = (all_levels[:, None] == jnp.arange(LEVELS, dtype=jnp.int32)[None, :]).astype(f32)
    cond = dot_low("fl,ld->fd", to_low(one_hot), to_low(table_w))
    cond_act = to_low(jax.nn.silu(cond))
    adaln_low = to_low(adaln_w)

    def mod_terms(lower, upper):
        wide = (upper - lower) * D // rows
        terms = to_low(dot_low("fd,dm->fm", cond_act, adaln_low[:, lower * D : upper * D]))
        terms = terms.reshape(clips, FRAMES, rows, wide).transpose(0, 2, 1, 3)
        return terms.reshape(count_dev, FRAMES, wide)

    def modulation(terms):
        total = row_gather(jnp.sum(terms.astype(f32), axis=0))
        return total.transpose(1, 0, 2).reshape(FRAMES, -1)

    first_terms = lax.all_to_all(mod_terms(0, 2), BOTH, 0, 0, tiled=True)
    first = modulation(first_terms)
    shift_a, scale_a = first[:, :D], first[:, D:]

    alpha, sigma = noise_mix(level_row)
    clean = latents[0].reshape(FRAMES, per_frame, PD)
    fresh = noise[0].reshape(FRAMES, per_frame, PD)
    noisy = alpha[:, None, None] * clean + sigma[:, None, None] * fresh
    target = (alpha[:, None, None] * fresh - sigma[:, None, None] * clean).reshape(count_tok, PD)
    noisy_own = to_low(noisy).reshape(count_tok, PD)
    perm = rotary_permutation(width)
    qkv_low = to_low(qkv_w).reshape(part, 3, rows, width)
    turned = to_low(dot_low("dgrw,wv->rdgv", qkv_low[:, :2], perm))
    mine = jnp.concatenate([turned, qkv_low[:, 2:].transpose(2, 0, 1, 3)], axis=2)
    mine = mine.reshape(rows, part, 3 * width)
    token_cols = count_tok * PD // part
    tokens = jnp.broadcast_to(noisy_own.reshape(1, part, token_cols), (rows, part, token_cols))
    mine = row_swap(jnp.concatenate([mine, tokens], axis=2))
    noisy_all = mine[:, :, 3 * width :].reshape(rows, FRAMES, per_frame, PD)
    noisy_all = noisy_all.transpose(1, 0, 2, 3).reshape(TOK, PD)
    def halves(weight, blocks):
        parts = weight.reshape(weight.shape[0], -1, 2, weight.shape[1] // (2 * blocks))
        mine = lax.dynamic_index_in_dim(parts, core, 2, keepdims=False)
        theirs = lax.dynamic_index_in_dim(parts, 1 - core, 2, keepdims=False)
        return mine.reshape(weight.shape[0], -1), theirs.reshape(weight.shape[0], -1)

    up_mine, up_theirs = halves(to_low(up_w), count_dev // 2)
    proj_mine, proj_theirs = halves(to_low(proj_w), 1)
    tall_mine = jnp.concatenate([up_mine, proj_mine], axis=1)
    tall_got = exchange(jnp.concatenate([up_theirs, proj_theirs], axis=1), 1)
    is_zero = core == 0
    tall = jnp.concatenate(
        [jnp.where(is_zero, tall_mine, tall_got), jnp.where(is_zero, tall_got, tall_mine)]
    )
    gather_down = Gather(to_low(down_w))
    gather_down.go_z()
    gather_down.go_xy()
    gather_down.go_slant()
    mine = tie(mine[:, :, : 3 * width], gather_down.own)
    gather_qkv = Gather(mine.reshape(rows * part, 3 * width), False)
    gather_qkv.go_z(first_terms)
    gather_qkv.go_xy()
    gather_qkv.go_slant()
    gather_tall = Gather(tie(tall, gather_qkv.own, *gather_down.came_xy()))
    gather_tall.go_z()
    gather_tall.go_direct()
    rest_sent = mod_terms(2, 8)

    cosine, sine = group_angles(frame_pos, width // 2)
    flags = jnp.concatenate([is_true.astype(f32), (PD * count).reshape(1)])
    rest_terms = lax.all_to_all(rest_sent, BOTH, 0, 0, tiled=True)
    query, keys, values, attn_in, qkv_b, attn_heads, lse = run_qkv_attend(
        coords, span, noisy_all, embed_b, shift_a, scale_a, cosine, sine, gather_qkv.pieces(),
        rows, after=(gather_tall.own, rest_sent, flags, head_b) + tuple(piece[0] for piece in gather_down.slant),
    )
    rest_terms = tie(rest_terms, query)
    rest = modulation(rest_terms)

    def swap_row(wide):
        return lax.all_to_all(wide, "row", 0, 0, tiled=True)

    attn = tie(attn_heads, rest_terms).reshape(rows, count_tok, width)
    attn = swap_row(attn)
    down_b = run_place(coords, gather_down.pieces(), (D,), after=(attn_heads,))[0]
    up_b, proj_own = run_place(
        coords, gather_tall.pieces(), (hidden, D // 2), after=(down_b,)
    )
    proj_other = exchange(proj_own, 1)
    hidden1, proj_out, mlp_in = run_proj(
        coords, attn, noisy_own, embed_b, rest, proj_own, proj_other
    )
    mlp_in_other = exchange(mlp_in, 1)
    up_out_other, act_other, part_other = run_up_down(mlp_in_other, up_b, down_b, bf16)
    part_got = exchange(part_other, 1)
    up_out, act, part_own = run_up_down(mlp_in, up_b, down_b, f32, after=(part_other,))
    grad_down_out, grad_h2, sums_f, grad_head, losses = run_head(
        flags, hidden1, part_own, part_got, rest, head_b, target
    )
    loss_local = jnp.sum(losses[:, 0])

    grad_down_other = exchange(grad_down_out, 1)
    down_groups = run_down_dw(
        coords, sizes, (act, act_other), (grad_down_out, grad_down_other)
    )
    scatter_down = Scatter(down_groups)
    grad_up, mlp_own = run_act_up_back(
        grad_down_out, down_b, up_out, up_b, f32, after=(down_groups[0, 0],)
    )
    mlp_other, up_groups = run_act_up_dw(
        coords, sizes, (mlp_in, mlp_in_other), grad_up, grad_down_other, down_b,
        up_out_other, up_b, after=tuple(scatter_down.sent.values()),
    )
    mlp_got = exchange(mlp_other, 1)
    scatter_down.go_xy()
    scatter_down.take_xy(up_groups[0, 0])
    scatter_down.go_z()
    grad_attn, proj_mine, proj_theirs, sums_m, embed_h1 = run_proj_back(
        coords, grad_h2, mlp_own, mlp_got, hidden1, proj_out, rest,
        proj_own, proj_other, attn, noisy_own, after=(scatter_down.own,),
    )
    grad_attn = swap_row(grad_attn).reshape(rows, FRAMES, per_frame, width)
    scatter_up = Scatter(up_groups, proj_mine)
    proj_groups = run_add_pieces(coords, sizes, (proj_mine, exchange(proj_theirs, 1)))
    scatter_up.go_xy(proj_groups, grad_attn)

    def mod_row(values_mod, *hold):
        wide = values_mod.shape[1] // rows
        total = to_low(row_sum(values_mod, *hold))
        return lax.dynamic_slice_in_dim(total, row_index * wide, wide, axis=1)

    def mod_all(total):
        wide = total.shape[-1]
        total = total.reshape(clips, rows, FRAMES, wide)
        return total.transpose(0, 2, 1, 3).reshape(clips * FRAMES, rows * wide)

    mod_rest = spread(mod_row(jnp.concatenate([sums_m, sums_f], axis=1)), BOTH)
    grad_qkv = run_attend_back(
        span, query, keys, values, attn_heads, grad_attn, lse, cosine, sine,
        after=(proj_groups[0, 0],) + tuple(scatter_up.sent.values()),
    )
    scatter_up.take_xy(grad_qkv)
    grad_qkv_w = run_qkv_dw(
        attn_in, grad_qkv, after=(scatter_up.own, mod_rest, *scatter_down.came_z)
    )
    qkv_terms = grad_qkv_w.reshape(count_dev, part, 3 * width)
    qkv_terms = lax.all_to_all(qkv_terms, BOTH, 0, 0, tiled=True)
    scatter_up.go_z(qkv_terms)
    sums_a, grad_embed = run_qkv_back(
        noisy_all, embed_b, scale_a, grad_qkv, qkv_b,
        after=(grad_qkv_w,),
    )
    down_sum = scatter_down.result(sums_a)
    grad_embed = grad_embed + embed_h1

    small = jnp.concatenate(
        [
            grad_embed.reshape(PD, count_dev, part).transpose(1, 0, 2).reshape(count_dev, -1),
            grad_head.reshape(count_dev, -1),
        ],
        axis=1,
    )
    small = to_low(small).reshape(count_dev, 1, -1)
    mod_first = mod_row(sums_a)
    wide = mod_first.shape[-1]
    lines = max(small.shape[-1] // wide, 1)
    small = jnp.pad(small, ((0, 0), (0, 0), (0, lines * wide - small.shape[-1])))
    last = jnp.concatenate(
        [
            jnp.broadcast_to(mod_first[None], (count_dev, FRAMES, wide)),
            small.reshape(count_dev, lines, wide),
        ],
        axis=1,
    )
    fixes = (1.0 - beta_one**STEP, 1.0 - beta_two**STEP)
    early = run_lamb([(down_w, down_sum, down_avg, down_sq)], (6,), fixes)
    last = lax.all_to_all(tie(last, qkv_terms, early[2]), BOTH, 0, 0, tiled=True)
    small = jnp.sum(last[:, FRAMES:].astype(f32), axis=0).reshape(-1)
    embed_sum = small[: PD * part].reshape(PD, part)
    head_sum = small[PD * part : 2 * PD * part].reshape(part, PD)
    qkv_sum = tie(qkv_terms, last).reshape(clips, rows, part, 3 * width).astype(f32)
    qkv_sum = to_low(jnp.sum(qkv_sum, axis=0)).reshape(rows, part, 3, width)
    turned = dot_low("rdgv,wv->dgrw", qkv_sum[:, :, :2], perm)
    straight = qkv_sum[:, :, 2:].transpose(1, 2, 0, 3).astype(f32)
    qkv_sum = jnp.concatenate([turned, straight], axis=1).reshape(part, 3 * D)

    grad_mod_b = jnp.concatenate([mod_all(last[:, :FRAMES]), mod_all(mod_rest)], axis=1)
    grad_adaln = dot_low("fd,fm->dm", cond_act, grad_mod_b)
    grad_cond_act = dot_low("fm,dm->fd", grad_mod_b, adaln_low)
    unused_silu, silu_pull = jax.vjp(jax.nn.silu, cond)
    grad_cond = silu_pull(grad_cond_act)[0]
    grad_table = jnp.einsum(
        "fl,fd->dl", one_hot, grad_cond, precision=precise, preferred_element_type=f32
    )

    reduced = [
        embed_sum, grad_table, grad_adaln, qkv_sum, None, None, down_sum, head_sum.T,
    ]
    turned = (1, 7)
    flip = lambda k, array: jnp.swapaxes(array, -1, -2) if k in turned else array
    weights = [flip(k, array) for k, array in enumerate(masters)]
    moms, updates, rows_of_sums = [None] * 8, [None] * 8, []
    for group in ((6,), (3,), (0, 1, 2, 7), (4, 5)):
        if group == (4, 5):
            tall_sum = scatter_up.result(*rows_of_sums)

            keep = lax.dynamic_slice_in_dim(tall_sum, core * part, part)
            got = exchange(to_low(lax.dynamic_slice_in_dim(tall_sum, (1 - core) * part, part)), 1)
            got = got.astype(f32)
            pair_sum = jnp.stack([jnp.where(is_zero, keep, got), jnp.where(is_zero, got, keep)], axis=1)
            up_sum = pair_sum[:, :, :hidden].reshape(part, 2, count_dev // 2, unit)
            up_sum = up_sum.transpose(0, 2, 1, 3).reshape(part, FF)
            proj_sum = pair_sum[:, :, hidden:].reshape(part, D)
            reduced[4], reduced[5] = proj_sum, up_sum
        entries = [
            (weights[k], reduced[k], flip(k, firsts[k]), flip(k, seconds[k])) for k in group
        ]
        got_moms, got_updates, sums = early if group == (6,) else run_lamb(entries, group, fixes)
        rows_of_sums.append(sums)
        for k, mom, update in zip(group, got_moms, got_updates):
            moms[k], updates[k] = flip(k, mom), update
    lane = jnp.arange(128, dtype=jnp.int32)[None, :]
    sums = sum(rows_of_sums) + jnp.where(lane == 16, loss_local, 0.0)
    totals = spread(sums, BOTH).reshape(count_dev, 128)
    news = run_update(weights, updates, totals)
    news = [flip(k, array) for k, array in enumerate(news)]
    totals = jnp.sum(totals, axis=0)
    norms = jnp.sqrt(totals[:16].reshape(8, 2))
    return (*news, *moms, norms, totals[16:17] / (PD * count))


def solution(mesh):
    wide, tall = P(None, BOTH), P(BOTH, None)
    weights = (wide, wide, tall, tall, tall, tall, tall, tall)
    moments = (P(None, None, BOTH),) * 2 + (P(None, BOTH, None),) * 6
    return jax.shard_map(
        body,
        mesh=mesh,
        in_specs=(
            P("clip", None, "row", None),
            P("clip", None, "row", None),
            P("clip", None),
            P("clip", None),
            P("clip", None),
        )
        + weights * 3,
        out_specs=weights + moments + (P(), P()),
        check_vma=False,
    )
```
